128 devices in a mesh: cmp: 32 (over y, x, core), off: 4 (over z).
Axes of the slice: x: 4, y: 4, z: 4, core: 2. Of those that a mesh axis runs over, the one named last changes fastest.
Arguments:
- traces: bfloat16 [32768, 2048], P(('cmp', 'off')), may hold values from -6 to 6
- shot_id: int32 [32768], P(('cmp', 'off')), may hold values from 0 to 255, as said below
- receiver_id: int32 [32768], P(('cmp', 'off')), may hold values from 0 to 1023
- cmp_bin: int32 [32768], P(('cmp', 'off')), may hold values from 0 to 511, as said below
- offset_class: int32 [32768], P(('cmp', 'off')), may hold values from 0 to 3, as said below
- shift_int: int32 [32768], P(('cmp', 'off')), may hold values from -8 to 8
- frac_index: int32 [32768], P(('cmp', 'off')), may hold values from 0 to 31
- damping_table: float32 [8], replicated, may hold values from 0.1 to 3
- damping_index: int32 [2], replicated, may hold values from 0 to 7
Outputs:
- shot_static: float32 [256], replicated
- receiver_static: float32 [1024], replicated
- pilot: bfloat16 [512, 2048], P('cmp')
The draws below stay inside these ranges and needn't reach their ends.
Inputs may be any that keep to these rules, and one draw needn't show every extreme that they name: Each device holds the traces of its own shots: shot_id // 2 equals the trace's row // 256. Call the owner of a trace the pair (cmp_bin // 16, offset_class). Among the 256 traces of one device, at most 4 have the same owner; on every device some owners have exactly 4, and some owners receive exactly 4 traces from every device. See the promise above on owners, which ties cmp_bin and offset_class together.
All inputs are finite; a program needn't handle non-finite values.
Results may differ from the reference program's by a relative error of at most 0.0054.
Values may be sent and summed in bfloat16 or wider, within the bound.
No kernel may reach another device: no remote copies, remote signals or barrier semaphores. Data moves between devices by JAX's collectives and lax.ppermute only.
A program may use at most 64 MiB of HBM per device.

```python
import math
import jax
import jax.numpy as jnp
from jax import lax

NS = 2048
LAGS = 101
TAPS = 16
NPHASE = 32
SHIFT_MAX = 8
ITERS = 2
NTAB = 8
TR_DEV = 256
SHOT_DEV = 2
CLASSES = 4
TRACE_LIMIT = 4
BIN_DEV = 16
BINS = 512
TRACES = 32768
NSHOT = 256
NREC = 1024
DEVICES = 128


def route_owner(key):
    total_slot_count = DEVICES * TRACE_LIMIT
    hot_order = jax.random.permutation(jax.random.fold_in(key, 11), DEVICES)
    busiest_owner = hot_order < DEVICES // 8
    slot_index_list = jnp.arange(total_slot_count, dtype=jnp.int32)
    extra_credit = jnp.where(busiest_owner[slot_index_list // TRACE_LIMIT], 1 << 17, 0).astype(jnp.int32)

    def one_block(block_key):
        random_jitter = jax.random.randint(jax.random.fold_in(block_key, 1), (total_slot_count,), 0, 1 << 16, dtype=jnp.int32)
        ranking_scores = (random_jitter + extra_credit) * total_slot_count + slot_index_list
        _, chosen = lax.top_k(ranking_scores, TR_DEV)
        shuffle = jax.random.permutation(jax.random.fold_in(block_key, 2), TR_DEV)
        return (chosen[shuffle] // TRACE_LIMIT).astype(jnp.int32)
    block_keys = jax.random.split(jax.random.fold_in(key, 13), DEVICES)
    return jax.vmap(one_block)(block_keys).reshape(-1)


def draw_cmp_bin(key, part):
    owner_rank = route_owner(key)
    local_bin = jax.random.randint(jax.random.fold_in(key, 17), (TRACES,), 0, BIN_DEV, dtype=jnp.int32)
    return (owner_rank // CLASSES * BIN_DEV + local_bin).astype(jnp.int32)


def draw_offset_class(key, part):
    return (route_owner(key) % CLASSES).astype(jnp.int32)


def draw_shot_id(key, part):
    rows = jnp.arange(TRACES, dtype=jnp.int32)
    local_shot = jax.random.randint(jax.random.fold_in(key, 19), (TRACES,), 0, SHOT_DEV, dtype=jnp.int32)
    return (rows // TR_DEV * SHOT_DEV + local_shot).astype(jnp.int32)


def with_ends(entries, rng, low, largest):
    place = [jax.random.randint(jax.random.fold_in(rng, axis), (), 0, length) for axis, length in enumerate(entries.shape)]
    widest = entries.shape.index(max(entries.shape))
    beside = place[:widest] + [(place[widest] + 1) % entries.shape[widest]] + place[widest + 1:]
    return entries.at[tuple(place)].set(low).at[tuple(beside)].set(largest)


def level_of(rng, shape, cuts, least, high):
    def one(position, parts):
        heights = jax.random.uniform(jax.random.fold_in(jax.random.fold_in(rng, 6), position), (parts,), jnp.float32, least / len(cuts), high / len(cuts))
        return jnp.repeat(jnp.exp(heights), shape[position] // parts).reshape((-1,) + (1,) * (len(shape) - position - 1))

    loudness = one(*cuts[0])
    for cut in cuts[1:]:
        loudness = loudness * one(*cut)
    return loudness


def centred(stream_key, extent, width, reach, cuts=(), held_as=jnp.bfloat16):
    gain = level_of(stream_key, extent, cuts, -0.22, 0.18) if cuts else 1.0
    result = jax.random.normal(stream_key, extent, jnp.float32) * width * gain
    return jnp.minimum(jnp.maximum(result, -reach), reach).astype(held_as)


def setup_inputs(seed: int = 0) -> dict:
    keys = jax.random.split(jax.random.key(seed), 10)
    return {
        "traces": centred(keys[0], (TRACES, NS), 1.0, 6.0, ((0, 128),)),
        "shot_id": draw_shot_id(jax.random.fold_in(keys[9], 71), 0),
        "receiver_id": with_ends(jax.random.randint(keys[2], (TRACES,), 0, NREC), jax.random.fold_in(keys[2], 1), 0, NREC - 1).astype(jnp.int32),
        "cmp_bin": draw_cmp_bin(jax.random.fold_in(keys[9], 71), 0),
        "offset_class": draw_offset_class(jax.random.fold_in(keys[9], 71), 0),
        "shift_int": with_ends(jax.random.randint(keys[5], (TRACES,), -SHIFT_MAX, SHIFT_MAX + 1), jax.random.fold_in(keys[5], 1), -SHIFT_MAX, SHIFT_MAX).astype(jnp.int32),
        "frac_index": with_ends(jax.random.randint(keys[6], (TRACES,), 0, NPHASE), jax.random.fold_in(keys[6], 1), 0, NPHASE - 1).astype(jnp.int32),
        "damping_table": jnp.clip(jnp.exp(jax.random.uniform(keys[7], (NTAB,), jnp.float32, math.log(0.1), math.log(3.0))), 0.1, 3.0),
        "damping_index": jax.random.randint(keys[8], (ITERS,), 0, NTAB).astype(jnp.int32),
    }


BETA = 24.0
EPS = 1e-06

def fir_taps(frac_total):
    tap_pos = jnp.arange(TAPS, dtype=jnp.float32) - (TAPS // 2 - 1)
    offset = tap_pos - frac_total[..., None]
    return jnp.sinc(offset) * (0.5 + 0.5 * jnp.cos(jnp.pi * offset / (TAPS // 2)))

def spread_taps(taps_now, shifts):
    reach_all = TAPS + 2 * SHIFT_MAX
    targets = jnp.arange(reach_all, dtype=jnp.int32) - (TAPS // 2 - 1) - SHIFT_MAX
    landing = shifts[..., None] + jnp.arange(TAPS, dtype=jnp.int32) - (TAPS // 2 - 1)
    matches = landing[..., None, :] == targets[:, None]
    return lax.optimization_barrier(jnp.sum(jnp.where(matches, taps_now[..., None, :], 0.0), axis=-1))

def shift_traces(raw_rows, shifts, frac_total):
    kernel = spread_taps(fir_taps(frac_total), shifts)
    samples = raw_rows.shape[-1]
    widths = [(0, 0)] * (raw_rows.ndim - 1) + [(TAPS // 2 - 1 + SHIFT_MAX, TAPS // 2 + SHIFT_MAX)]
    padded = jnp.pad(raw_rows, widths)
    accumulated = jnp.zeros(raw_rows.shape, jnp.float32)
    for offset in range(TAPS + 2 * SHIFT_MAX):
        accumulated = accumulated + kernel[..., offset, None] * padded[..., offset:offset + samples].astype(jnp.float32)
    return accumulated.astype(jnp.bfloat16)

def blocked(values):
    return values.reshape((TRACES // TR_DEV, TR_DEV) + values.shape[1:])

def reference(traces, shot_id, receiver_id, cmp_bin, offset_class, shift_int, frac_index, damping_table, damping_index):
    weight = 1.0 / (1.0 + offset_class.astype(jnp.float32))
    unit_rows = jnp.ones((TRACES,), jnp.float32)
    shot_count = jax.ops.segment_sum(unit_rows, shot_id, NSHOT)
    receiver_count = jax.ops.segment_sum(unit_rows, receiver_id, NREC)
    shot_static = jnp.zeros((NSHOT,), jnp.float32)
    receiver_static = jnp.zeros((NREC,), jnp.float32)
    lag_values = jnp.arange(LAGS, dtype=jnp.float32) - LAGS // 2
    half_lag = LAGS // 2
    length = 2 * NS
    pilot = None
    for iteration in range(ITERS):
        damping = damping_table[damping_index[iteration]]
        frac_total = frac_index.astype(jnp.float32) / NPHASE + shot_static[shot_id] + receiver_static[receiver_id]

        def stack_block(state_pair, pieces):
            stacked, weight_sum = state_pair
            raw_rows, shifts, frac_now, bin_rows, weight_rows = pieces
            shifted = shift_traces(raw_rows, shifts, frac_now)
            stacked = stacked + jax.ops.segment_sum(shifted.astype(jnp.float32) * weight_rows[:, None], bin_rows, BINS)
            weight_sum = weight_sum + jax.ops.segment_sum(weight_rows, bin_rows, BINS)
            return ((stacked, weight_sum), shifted)
        start_pair = (jnp.zeros((BINS, NS), jnp.float32), jnp.zeros((BINS,), jnp.float32))
        (stacked, weight_sum), shifted_all = lax.scan(stack_block, start_pair, (blocked(traces), blocked(shift_int), blocked(frac_total), blocked(cmp_bin), blocked(weight)))
        pilot = (stacked * lax.rsqrt(weight_sum + 1.0)[:, None]).astype(jnp.bfloat16)
        pilot_wide = pilot.astype(jnp.float32)
        pilot_scale = lax.rsqrt(lax.optimization_barrier(jnp.sum(pilot_wide * pilot_wide, axis=1)) + EPS)
        pilot_spec = jnp.fft.rfft(pilot_wide, n=length, axis=1)

        def corr_block(state_pair, pieces):
            shot_grad, receiver_grad = state_pair
            shifted, bin_rows, shot_rows, receivers = pieces
            wide_rows = shifted.astype(jnp.float32)
            spectrum = jnp.fft.rfft(wide_rows, n=length, axis=1)
            cross_corr = jnp.fft.irfft(jnp.conj(spectrum) * pilot_spec[bin_rows], n=length, axis=1)
            lagged = jnp.concatenate([cross_corr[:, length - half_lag:], cross_corr[:, :half_lag + 1]], axis=1)
            scales = lax.rsqrt(lax.optimization_barrier(jnp.sum(wide_rows * wide_rows, axis=1)) + EPS) * pilot_scale[bin_rows]
            ncorr = lagged * scales[:, None]
            exponent = jnp.exp(BETA * ncorr)
            delay_est = lax.optimization_barrier(jnp.sum(exponent * lag_values, axis=1)) / lax.optimization_barrier(jnp.sum(exponent, axis=1))
            shot_grad = shot_grad - jax.ops.segment_sum(delay_est, shot_rows, NSHOT)
            receiver_grad = receiver_grad - jax.ops.segment_sum(delay_est, receivers, NREC)
            return ((shot_grad, receiver_grad), None)
        grad_start = (jnp.zeros((NSHOT,), jnp.float32), jnp.zeros((NREC,), jnp.float32))
        (shot_grad, receiver_grad), _ = lax.scan(corr_block, grad_start, (shifted_all, blocked(cmp_bin), blocked(shot_id), blocked(receiver_id)))
        shot_static = shot_static + shot_grad / ((1.0 + damping) * shot_count + damping)
        receiver_static = receiver_static + receiver_grad / ((1.0 + damping) * receiver_count + damping)
    return (shot_static, receiver_static, pilot)
```

```python
import functools

import jax
import jax.numpy as jnp
from jax import lax
from jax.experimental import pallas as pl
from jax.experimental.pallas import tpu as pltpu
from jax.sharding import PartitionSpec as P

NS = 2048
LAGS = 101
HALF = LAGS // 2
TAPS = 16
NPHASE = 32
SHIFT_MAX = 8
CLASSES = 4
TRACE_LIMIT = 4
BIN_DEV = 16
TR_DEV = 256
DEVICES = 128
SLOTS = DEVICES * TRACE_LIMIT
LANES = 128
WIDE = NS + LANES
LROWS = 112
LAG_TOP = 106
BINS_STEP = 4
BETA = 24.0
EPS = 1e-06
F32 = jnp.float32
BF16 = jnp.bfloat16
HEAD = 16

NN = (((1,), (0,)), ((), ()))
NT = (((1,), (1,)), ((), ()))
TN = (((0,), (0,)), ((), ()))


def dot(a, b, dims, precision=None):
    return lax.dot_general(a, b, dims, precision=precision, preferred_element_type=F32)


def iota(shape, axis):
    return lax.broadcasted_iota(jnp.int32, shape, axis)


def pack_kernel(meta_ref, x_ref, out_ref, y_ref):
    meta = meta_ref[...]
    shot, rec, bin_, cls, shift, frac = [meta[i : i + 1, :] for i in range(6)]
    dest = (bin_ // BIN_DEV) * CLASSES + cls
    rows = [
        shot // 128,
        shot % 128,
        rec // 128,
        rec % 128,
        bin_ % BIN_DEV,
        frac,
        jnp.ones_like(shot),
        shift + SHIFT_MAX,
        dest,
    ]
    sub = iota((16, TR_DEV), 0)
    info = jnp.zeros((16, TR_DEV), F32)
    for i, row in enumerate(rows):
        info = jnp.where(sub == i, row.astype(F32), info)
    place = (iota((16, LANES), 1) == iota((16, LANES), 0) + HEAD).astype(F32).astype(BF16)
    cols = dot(info.astype(BF16), place, TN)
    shift_col = cols[:, HEAD + 7 : HEAD + 8].astype(jnp.int32)
    dest_col = cols[:, HEAD + 8 : HEAD + 9]
    same = (dest_col == dest.astype(F32)) & (iota((TR_DEV, TR_DEV), 0) < iota((TR_DEV, TR_DEV), 1))
    rank = jnp.sum(jnp.where(same, 1.0, 0.0), axis=0, keepdims=True).astype(jnp.int32)
    slot = dest * TRACE_LIMIT + rank
    onehot = (iota((SLOTS, TR_DEV), 0) == slot).astype(F32).astype(BF16)
    step = 32
    for r in range(0, TR_DEV, step):
        y = jnp.concatenate([x_ref[r : r + step, :].astype(F32), jnp.zeros((step, LANES), F32)], axis=1)
        y = pltpu.roll(y, SHIFT_MAX, 1)
        amount = shift_col[r : r + step, :]
        for bit in range(5):
            on = ((amount >> bit) & 1) == 1
            y = jnp.where(on, pltpu.roll(y, WIDE - (1 << bit), 1), y)
        y_ref[r : r + step, :NS] = y[:, :NS].astype(BF16)
        y_ref[r : r + step, NS:] = (y[:, NS:] + cols[r : r + step, :]).astype(BF16)
    out_ref[...] = dot(onehot, y_ref[...], NN).astype(BF16)


def spread_slots(y_ref, xt_ref):
    eye = (iota((LANES, LANES), 0) == iota((LANES, LANES), 1)).astype(F32).astype(BF16)
    for c in range(NS // LANES):
        block = dot(eye, y_ref[:, c * LANES : (c + 1) * LANES], NT)
        for q in range(SLOTS // LANES):
            xt_ref[q, 8 + c * LANES : 8 + (c + 1) * LANES, :] = block[:, q * LANES : (q + 1) * LANES]
    block = dot(eye, y_ref[:, NS:], NT)
    for q in range(SLOTS // LANES):
        part = block[:, q * LANES : (q + 1) * LANES]
        xt_ref[q, 0:8, :] = part[120:128, :]
        xt_ref[q, 8 + NS : 16 + NS, :] = part[0:8, :]
    return block[HEAD : HEAD + 16, :]


def one_hot_rows(row, count):
    return (iota((count, SLOTS), 0) == row.astype(jnp.int32)).astype(F32)


def damped(grad_count, damp):
    return grad_count[0:8, :] / ((1.0 + damp) * grad_count[8:16, :] + damp)


def stack_kernel(first, *refs):
    if first:
        weight_ref, y_ref, part_ref, st_ref, side_ref, xt_ref = refs
    else:
        weight_ref, y_ref, rec_ref, shot_ref, part_ref, st_ref, side_ref, xt_ref = refs
    head = spread_slots(y_ref, xt_ref)
    frac = head[5:6, :] * (1.0 / NPHASE)
    live = head[6:7, :]
    if not first:
        for table_ref, at in ((shot_ref, 0), (rec_ref, 2)):
            low = one_hot_rows(head[at + 1 : at + 2, :], 128)
            high = one_hot_rows(head[at : at + 1, :], 8)
            found = dot(table_ref[...], low, NN, lax.Precision.HIGHEST)
            frac = frac + jnp.sum(found * high, axis=0, keepdims=True)
    u = (iota((TAPS, SLOTS), 0) - (TAPS // 2 - 1)).astype(F32) - frac
    angle = jnp.pi * u
    safe = jnp.where(u == 0.0, 1.0, angle)
    sinc = jnp.where(u == 0.0, 1.0, jnp.sin(safe) / safe)
    taps = sinc * (0.5 + 0.5 * jnp.cos(angle * (1.0 / (TAPS // 2))))
    chunk = 16
    energies = []
    for q in range(SLOTS // LANES):
        tap = [jnp.broadcast_to(taps[k : k + 1, q * LANES : (q + 1) * LANES], (8, LANES)) for k in range(TAPS)]

        def body(i, energy):
            base = i * chunk
            halves = []
            for h in range(chunk // 8):
                total = tap[0] * xt_ref[q, pl.ds(base + 8 * h + 1, 8), :]
                for k in range(1, TAPS):
                    total = total + tap[k] * xt_ref[q, pl.ds(base + 8 * h + 1 + k, 8), :]
                halves.append(total)
            rounded = jnp.concatenate(halves, axis=0).astype(BF16)
            st_ref[pl.ds(pl.multiple_of(base, chunk), chunk), q * LANES : (q + 1) * LANES] = rounded
            wide = rounded.astype(F32)
            return energy + wide[0:8, :] * wide[0:8, :] + wide[8:16, :] * wide[8:16, :]

        energy = lax.fori_loop(0, NS // chunk, body, jnp.zeros((8, LANES), F32), unroll=4)
        energies.append(jnp.sum(energy, axis=0, keepdims=True))
    side_ref[0:16, :] = head
    side_ref[16:24, :] = jnp.broadcast_to(jnp.concatenate(energies, axis=1), (8, SLOTS))
    weight = weight_ref[0, 0]
    member = one_hot_rows(head[4:5, :], BIN_DEV) * live
    part_ref[:, :NS] = (weight * dot(member.astype(BF16), st_ref[...], NT)).astype(BF16)
    mass = weight * jnp.sum(member, axis=1, keepdims=True)
    m0 = mass.astype(BF16).astype(F32)
    m1 = (mass - m0).astype(BF16).astype(F32)
    m2 = mass - m0 - m1
    lane = iota((BIN_DEV, LANES), 1)
    tail = jnp.where(lane == 0, m0, jnp.where(lane == 1, m1, jnp.where(lane == 2, m2, 0.0)))
    part_ref[:, NS:] = tail.astype(BF16)


def corr_kernel(first, p0_ref, p1_ref, p2_ref, p3_ref, st_ref, side_ref, pilot_ref, grad_ref, lag_ref, wide_ref):
    total = (p0_ref[...].astype(F32) + p2_ref[...].astype(F32)) + (
        p1_ref[...].astype(F32) + p3_ref[...].astype(F32)
    )
    mass = (total[:, NS : NS + 1] + total[:, NS + 1 : NS + 2]) + total[:, NS + 2 : NS + 3]
    pilot = (total[:, :NS] * lax.rsqrt(mass + 1.0)).astype(BF16)
    pilot_ref[...] = pilot
    wide = pilot.astype(F32)
    wide_ref[:, :NS] = wide
    wide_ref[:, NS:] = jnp.zeros((BIN_DEV, LANES), F32)
    pilot_scale = lax.rsqrt(jnp.sum(wide * wide, axis=1, keepdims=True) + EPS)
    head = side_ref[0:16, :]
    live = head[6:7, :]
    member = one_hot_rows(head[4:5, :], BIN_DEV) * live
    corr = jnp.zeros((LROWS, SLOTS), F32)
    for b0 in range(0, BIN_DEV, BINS_STEP):
        for bb in range(BINS_STEP):
            row = jnp.broadcast_to(wide_ref[b0 + bb : b0 + bb + 1, :], (8, WIDE))
            for g in range(0, LROWS, 16):
                two = [
                    pltpu.roll(row, (WIDE - (LAG_TOP - HALF) + g + h) % WIDE, 1, stride=1, stride_axis=0)[:, :NS]
                    for h in (0, 8)
                ]
                at = (b0 + bb) * LROWS + g
                lag_ref[at : at + 16, :] = jnp.concatenate(two, axis=0).astype(BF16)
        every = dot(lag_ref[b0 * LROWS : (b0 + BINS_STEP) * LROWS, :], st_ref[...], NN)
        for bb in range(BINS_STEP):
            corr = corr + member[b0 + bb : b0 + bb + 1, :] * every[bb * LROWS : (bb + 1) * LROWS, :]
    scale = lax.rsqrt(side_ref[16:17, :] + EPS) * jnp.sum(member * pilot_scale, axis=0, keepdims=True)
    lag = LAG_TOP - iota((LROWS, SLOTS), 0)
    exponent = jnp.where((lag >= 0) & (lag < LAGS), jnp.exp(BETA * (corr * scale)), 0.0)
    delay = jnp.sum(exponent * (lag - HALF).astype(F32), axis=0, keepdims=True) / jnp.sum(
        exponent, axis=0, keepdims=True
    )
    misfit = -delay * live
    for at, out in ((2, 0), (0, 16 if first else 8)):
        low = one_hot_rows(head[at + 1 : at + 2, :], 128)
        high = one_hot_rows(head[at : at + 1, :], 8)
        values = high * misfit
        if first:
            values = jnp.concatenate([values, high * live], axis=0)
        sums = dot(values, low, NT, lax.Precision.HIGHEST)
        grad_ref[out : out + sums.shape[0], :] = sums


VMEM = pl.BlockSpec(memory_space=pltpu.VMEM)
SMEM = pl.BlockSpec(memory_space=pltpu.SMEM)
PARAMS = pltpu.CompilerParams(vmem_limit_bytes=40 * 1024 * 1024)


def shape(dims, dtype):
    return jax.ShapeDtypeStruct(dims, dtype)


def pack(meta, traces):
    return pl.pallas_call(
        pack_kernel,
        out_shape=shape((SLOTS, WIDE), BF16),
        in_specs=[VMEM, VMEM],
        out_specs=VMEM,
        scratch_shapes=[pltpu.VMEM((TR_DEV, WIDE), BF16)],
        compiler_params=PARAMS,
        name="pack",
    )(meta, traces)


def stack(weight, slots, tables):
    first = tables is None
    args = (weight, slots) + (() if first else tables)
    return pl.pallas_call(
        functools.partial(stack_kernel, first),
        out_shape=(shape((BIN_DEV, WIDE), BF16), shape((NS, SLOTS), BF16), shape((24, SLOTS), F32)),
        in_specs=[SMEM] + [VMEM] * (len(args) - 1),
        out_specs=(VMEM, VMEM, VMEM),
        scratch_shapes=[pltpu.VMEM((SLOTS // LANES, NS + 16, LANES), F32)],
        compiler_params=PARAMS,
        name="stack",
    )(*args)


def correlate(first, parts, shifted, side):
    return pl.pallas_call(
        functools.partial(corr_kernel, first),
        out_shape=(shape((BIN_DEV, NS), BF16), shape((32 if first else 16, LANES), F32)),
        in_specs=[VMEM] * 6,
        out_specs=(VMEM, VMEM),
        scratch_shapes=[pltpu.VMEM((BIN_DEV * LROWS, NS), BF16), pltpu.VMEM((BIN_DEV, WIDE), F32)],
        compiler_params=PARAMS,
        name="correlate",
    )(*parts, shifted, side)


def cmp_pairs(move):
    pairs = []
    for y in range(4):
        for x in range(4):
            for c in range(2):
                y2, x2, c2 = move(y, x, c)
                pairs.append(((y * 4 + x) * 2 + c, (y2 * 4 + x2) * 2 + c2))
    return pairs


def ring_sum(value, axis, perms):
    got = [lax.ppermute(value, axis, perm) for perm in perms]
    if len(got) == 1:
        return value + got[0]
    return (value + got[1]) + (got[0] + got[2])


def off_perm(d):
    return [(i, (i + d) % 4) for i in range(4)]


def sum_all(value):
    value = ring_sum(value, "cmp", [cmp_pairs(lambda y, x, c: (y, x, 1 - c))])
    value = ring_sum(value, "cmp", [cmp_pairs(lambda y, x, c, d=d: (y, (x + d) % 4, c)) for d in (1, 2, 3)])
    value = ring_sum(value, "cmp", [cmp_pairs(lambda y, x, c, d=d: ((y + d) % 4, x, c)) for d in (1, 2, 3)])
    return ring_sum(value, "off", [off_perm(d) for d in (1, 2, 3)])


def on_device(
    traces,
    shot_id,
    receiver_id,
    cmp_bin,
    offset_class,
    shift_int,
    frac_index,
    damping_table,
    damping_index,
):
    meta = jnp.stack([shot_id, receiver_id, cmp_bin, offset_class, shift_int, frac_index, frac_index, frac_index])
    outgoing = pack(meta, traces).reshape(DEVICES, TRACE_LIMIT, WIDE)
    arrived = lax.all_to_all(outgoing, ("cmp", "off"), split_axis=0, concat_axis=0, tiled=True)
    slots = arrived.reshape(SLOTS, WIDE)
    weight = (1.0 / (1.0 + lax.axis_index("off").astype(F32))).reshape(1, 1)
    entries = jnp.arange(damping_table.shape[0], dtype=jnp.int32)
    damps = [jnp.sum(jnp.where(entries == damping_index[i], damping_table, 0.0)) for i in range(2)]
    tables = None
    for iteration in range(2):
        first = iteration == 0
        part, shifted, side = stack(weight, slots, tables)
        others = [lax.ppermute(part, "off", off_perm(d)) for d in (1, 2, 3)]
        pilot, sums = correlate(first, (part, *others), shifted, side)
        sums = sum_all(sums)
        damp = damps[iteration]
        if first:
            rec_count, shot_count = sums[8:16], sums[24:32]
            rec = sums[0:8] / ((1.0 + damp) * rec_count + damp)
            shot = sums[16:24] / ((1.0 + damp) * shot_count + damp)
            tables = (rec, shot)
        else:
            rec = rec + sums[0:8] / ((1.0 + damp) * rec_count + damp)
            shot = shot + sums[8:16] / ((1.0 + damp) * shot_count + damp)
    return (shot[0:2].reshape(256), rec.reshape(1024), pilot)


def solution(mesh):
    placed = (
        P(("cmp", "off"), None),
        P(("cmp", "off")),
        P(("cmp", "off")),
        P(("cmp", "off")),
        P(("cmp", "off")),
        P(("cmp", "off")),
        P(("cmp", "off")),
        P(),
        P(),
    )
    return jax.shard_map(
        on_device, mesh=mesh, in_specs=placed, out_specs=(P(), P(), P("cmp", None)), check_vma=False
    )
```

```python
import functools

import jax
import jax.numpy as jnp
from jax import lax
from jax.experimental import pallas as pl
from jax.experimental.pallas import tpu as pltpu
from jax.sharding import PartitionSpec as P

NS = 2048
LAGS = 101
HALF = LAGS // 2
TAPS = 16
NPHASE = 32
SHIFT_MAX = 8
CLASSES = 4
TRACE_LIMIT = 4
BIN_DEV = 16
TR_DEV = 256
DEVICES = 128
SLOTS = DEVICES * TRACE_LIMIT
LANES = 128
WIDE = NS + LANES
LROWS = 112
LAG_TOP = 106
BINS_STEP = 4
BETA = 24.0
EPS = 1e-06
F32 = jnp.float32
BF16 = jnp.bfloat16
HEAD = 16

NN = (((1,), (0,)), ((), ()))
NT = (((1,), (1,)), ((), ()))
TN = (((0,), (0,)), ((), ()))


def dot(a, b, dims, precision=None):
    return lax.dot_general(a, b, dims, precision=precision, preferred_element_type=F32)


def iota(shape, axis):
    return lax.broadcasted_iota(jnp.int32, shape, axis)


def pack_kernel(shot_ref, rec_ref, bin_ref, cls_ref, shift_ref, frac_ref, x_ref, out_ref, y_ref):
    shot, rec, bin_, cls = shot_ref[...], rec_ref[...], bin_ref[...], cls_ref[...]
    dest = (bin_ // BIN_DEV) * CLASSES + cls
    rows = [
        shot // 128,
        shot % 128,
        rec // 128,
        rec % 128,
        bin_ % BIN_DEV,
        frac_ref[...],
        jnp.ones_like(shot),
        shift_ref[...] + SHIFT_MAX,
        dest,
    ]
    sub = iota((16, TR_DEV), 0)
    info = jnp.zeros((16, TR_DEV), F32)
    for i, row in enumerate(rows):
        info = jnp.where(sub == i, row.astype(F32), info)
    place = (iota((16, LANES), 1) == iota((16, LANES), 0) + HEAD).astype(F32).astype(BF16)
    cols = dot(info.astype(BF16), place, TN)
    amount = cols[:, HEAD + 7 : HEAD + 8].astype(jnp.int32)
    dest_col = cols[:, HEAD + 8 : HEAD + 9]
    same = (dest_col == dest.astype(F32)) & (iota((TR_DEV, TR_DEV), 0) < iota((TR_DEV, TR_DEV), 1))
    rank = jnp.sum(jnp.where(same, 1.0, 0.0), axis=0, keepdims=True).astype(jnp.int32)
    slot = dest * TRACE_LIMIT + rank
    onehot = (iota((SLOTS, TR_DEV), 0) == slot).astype(F32).astype(BF16)
    on = [((amount >> bit) & 1).astype(F32).astype(BF16) > 0 for bit in range(5)]
    cols = cols.astype(BF16)
    step = 32
    for r in range(0, TR_DEV, step):
        y = jnp.concatenate([x_ref[r : r + step, :], jnp.zeros((step, LANES), BF16)], axis=1)
        y = pltpu.roll(y, SHIFT_MAX, 1)
        for bit in range(5):
            y = jnp.where(on[bit][r : r + step, :], pltpu.roll(y, WIDE - (1 << bit), 1), y)
        y_ref[r : r + step, :NS] = y[:, :NS]
        y_ref[r : r + step, NS:] = y[:, NS:] + cols[r : r + step, :]
    out_ref[...] = dot(onehot, y_ref[...], NN).reshape(DEVICES, TRACE_LIMIT, WIDE).astype(BF16)


def one_hot_rows(row, count):
    return (iota((count, SLOTS), 0) == row.astype(jnp.int32)).astype(F32)


def unit(size):
    return (iota((size, size), 0) == iota((size, size), 1)).astype(F32).astype(BF16)


def stack_rows(weight, y_ref, head, frac, side_ref, part_ref, sum_ref):
    live = head[6:7, :]
    u = (iota((TAPS, SLOTS), 0) - (TAPS // 2 - 1)).astype(F32) - frac
    angle = jnp.pi * u
    safe = jnp.where(u == 0.0, 1.0, angle)
    sinc = jnp.where(u == 0.0, 1.0, jnp.sin(safe) / safe)
    taps = sinc * (0.5 + 0.5 * jnp.cos(angle * (1.0 / (TAPS // 2))))
    side_ref[0:16, :] = head
    side_ref[16:32, :] = taps
    member = one_hot_rows(head[4:5, :], BIN_DEV) * live
    rows = [member * taps[k : k + 1, :] for k in range(TAPS)]
    high = [row.astype(BF16) for row in rows]
    low = [(row - top.astype(F32)).astype(BF16) for row, top in zip(rows, high)]
    slots = y_ref[...]
    sum_ref[...] = dot(jnp.concatenate(high, axis=0), slots, NN) + dot(jnp.concatenate(low, axis=0), slots, NN)
    total = jnp.zeros((BIN_DEV, WIDE), F32)
    for k in range(TAPS):
        total = total + pltpu.roll(sum_ref[k * BIN_DEV : (k + 1) * BIN_DEV, :], (TAPS // 2 - 1 - k) % WIDE, 1)
    part_ref[:, :NS] = (weight * total[:, :NS]).astype(BF16)
    mass = weight * jnp.sum(member, axis=1, keepdims=True)
    m0 = mass.astype(BF16).astype(F32)
    m1 = (mass - m0).astype(BF16).astype(F32)
    m2 = mass - m0 - m1
    lane = iota((BIN_DEV, LANES), 1)
    tail = jnp.where(lane == 0, m0, jnp.where(lane == 1, m1, jnp.where(lane == 2, m2, 0.0)))
    part_ref[:, NS:] = tail.astype(BF16)


def first_kernel(weight_ref, slots_ref, part_ref, side_ref, y_ref, sum_ref):
    y_ref[...] = slots_ref[...].reshape(SLOTS, WIDE)
    head = dot(unit(LANES), y_ref[:, NS:], NT)[HEAD : HEAD + 16, :]
    stack_rows(weight_ref[0, 0], y_ref, head, head[5:6, :] * (1.0 / NPHASE), side_ref, part_ref, sum_ref)


def next_kernel(weight_ref, y_ref, head_ref, rec_ref, shot_ref, part_ref, side_ref, sum_ref):
    head = head_ref[0:16, :]
    frac = head[5:6, :] * (1.0 / NPHASE)
    for table_ref, at in ((shot_ref, 0), (rec_ref, 2)):
        low = one_hot_rows(head[at + 1 : at + 2, :], 128)
        high = one_hot_rows(head[at : at + 1, :], 8)
        found = dot(table_ref[...], low, NN, lax.Precision.HIGHEST)
        frac = frac + jnp.sum(found * high, axis=0, keepdims=True)
    stack_rows(weight_ref[0, 0], y_ref, head, frac, side_ref, part_ref, sum_ref)


def shift_kernel(y_ref, side_ref, st_ref, energy_ref, xt_ref):
    eye = unit(LANES)
    groups = SLOTS // LANES
    for c in range(NS // LANES):
        block = dot(eye, y_ref[:, c * LANES : (c + 1) * LANES], NT)
        for q in range(groups):
            xt_ref[q, 8 + c * LANES : 8 + (c + 1) * LANES, :] = block[:, q * LANES : (q + 1) * LANES]
    block = dot(eye, y_ref[:, NS:], NT)
    for q in range(groups):
        part = block[:, q * LANES : (q + 1) * LANES]
        xt_ref[q, 0:8, :] = part[120:128, :]
        xt_ref[q, 8 + NS : 16 + NS, :] = part[0:8, :]
    chunk = 32
    energies = []
    for q in range(groups):
        tap = [
            jnp.broadcast_to(side_ref[16 + k : 17 + k, q * LANES : (q + 1) * LANES], (8, LANES)) for k in range(TAPS)
        ]

        def body(i, energy):
            base = pl.multiple_of(i * chunk, chunk)
            totals = [None] * (chunk // 8)
            for p in range(chunk + TAPS - 8):
                window = xt_ref[q, pl.ds(base + 1 + p, 8), :]
                for h in range(chunk // 8):
                    k = p - 8 * h
                    if 0 <= k < TAPS:
                        term = tap[k] * window
                        totals[h] = term if totals[h] is None else totals[h] + term
            for h in range(0, chunk // 8, 2):
                rounded = jnp.concatenate(totals[h : h + 2], axis=0).astype(BF16)
                st_ref[pl.ds(base + 8 * h, 16), q * LANES : (q + 1) * LANES] = rounded
                wide = rounded.astype(F32)
                energy = energy + wide[0:8, :] * wide[0:8, :] + wide[8:16, :] * wide[8:16, :]
            return energy

        energy = lax.fori_loop(0, NS // chunk, body, jnp.zeros((8, LANES), F32), unroll=2)
        energies.append(jnp.sum(energy, axis=0, keepdims=True))
    energy_ref[...] = jnp.broadcast_to(jnp.concatenate(energies, axis=1), (8, SLOTS))


def corr_kernel(first, p0_ref, p1_ref, p2_ref, p3_ref, st_ref, energy_ref, side_ref, pilot_ref, grad_ref, lag_ref, wide_ref):
    total = (p0_ref[...].astype(F32) + p2_ref[...].astype(F32)) + (
        p1_ref[...].astype(F32) + p3_ref[...].astype(F32)
    )
    mass = (total[:, NS : NS + 1] + total[:, NS + 1 : NS + 2]) + total[:, NS + 2 : NS + 3]
    pilot = (total[:, :NS] * lax.rsqrt(mass + 1.0)).astype(BF16)
    pilot_ref[...] = pilot
    wide = pilot.astype(F32)
    wide_ref[:, :NS] = wide
    wide_ref[:, NS:] = jnp.zeros((BIN_DEV, LANES), F32)
    pilot_scale = lax.rsqrt(jnp.sum(wide * wide, axis=1, keepdims=True) + EPS)
    head = side_ref[0:16, :]
    live = head[6:7, :]
    member = one_hot_rows(head[4:5, :], BIN_DEV) * live
    corr = jnp.zeros((LROWS, SLOTS), F32)
    for b0 in range(0, BIN_DEV, BINS_STEP):
        for bb in range(BINS_STEP):
            row = jnp.broadcast_to(wide_ref[b0 + bb : b0 + bb + 1, :], (16, WIDE)).astype(BF16)
            row = pltpu.roll(row, 0, 1, stride=1, stride_axis=0)
            for g in range(0, LROWS, 16):
                at = (b0 + bb) * LROWS + g
                lag_ref[at : at + 16, :] = pltpu.roll(row, (WIDE - (LAG_TOP - HALF) + g) % WIDE, 1)[:, :NS]
        every = dot(lag_ref[b0 * LROWS : (b0 + BINS_STEP) * LROWS, :], st_ref[...], NN)
        for bb in range(BINS_STEP):
            corr = corr + member[b0 + bb : b0 + bb + 1, :] * every[bb * LROWS : (bb + 1) * LROWS, :]
    scale = lax.rsqrt(energy_ref[0:1, :] + EPS) * jnp.sum(member * pilot_scale, axis=0, keepdims=True)
    lag = LAG_TOP - iota((LROWS, SLOTS), 0)
    exponent = jnp.where((lag >= 0) & (lag < LAGS), jnp.exp(BETA * (corr * scale)), 0.0)
    delay = jnp.sum(exponent * (lag - HALF).astype(F32), axis=0, keepdims=True) / jnp.sum(
        exponent, axis=0, keepdims=True
    )
    misfit = -delay * live
    for at, out in ((2, 0), (0, 16 if first else 8)):
        low = one_hot_rows(head[at + 1 : at + 2, :], 128)
        high = one_hot_rows(head[at : at + 1, :], 8)
        values = high * misfit
        if first:
            values = jnp.concatenate([values, high * live], axis=0)
        sums = dot(values, low, NT, lax.Precision.HIGHEST)
        grad_ref[out : out + sums.shape[0], :] = sums


VMEM = pl.BlockSpec(memory_space=pltpu.VMEM)
SMEM = pl.BlockSpec(memory_space=pltpu.SMEM)
PARAMS = pltpu.CompilerParams(vmem_limit_bytes=40 * 1024 * 1024)


def shape(dims, dtype):
    return jax.ShapeDtypeStruct(dims, dtype)


def call(kernel, out, memory, scratch, name, flops, moved, *args):
    return pl.pallas_call(
        kernel,
        out_shape=out,
        in_specs=[SMEM if space else VMEM for space in memory],
        out_specs=jax.tree.map(lambda _: VMEM, out),
        scratch_shapes=scratch,
        compiler_params=PARAMS,
        cost_estimate=pl.CostEstimate(flops=flops, bytes_accessed=moved, transcendentals=0),
        name=name,
    )(*args)


def pack(traces, *meta):
    return call(
        pack_kernel,
        shape((DEVICES, TRACE_LIMIT, WIDE), BF16),
        (0,) * 7,
        [pltpu.VMEM((TR_DEV, WIDE), BF16)],
        "pack",
        10**9,
        3 * 2**20,
        *[row.reshape(1, TR_DEV) for row in meta],
        traces,
    )


PART = shape((BIN_DEV, WIDE), BF16)
SIDE = shape((32, SLOTS), F32)
ROWS = pltpu.VMEM((TAPS * BIN_DEV, WIDE), F32)


def stack_first(weight, slots):
    out = (PART, SIDE, shape((SLOTS, WIDE), BF16))
    return call(first_kernel, out, (1, 0), [ROWS], "stack_first", 3 * 10**9, 10**7, weight, slots)


def stack_next(weight, rows, side, rec, shot):
    return call(
        next_kernel, (PART, SIDE), (1, 0, 0, 0, 0), [ROWS], "stack_next", 3 * 10**9, 10**7, weight, rows, side, rec, shot
    )


def shift(rows, side):
    out = (shape((NS, SLOTS), BF16), shape((8, SLOTS), F32))
    scratch = [pltpu.VMEM((SLOTS // LANES, NS + 16, LANES), F32)]
    return call(shift_kernel, out, (0, 0), scratch, "shift", 6 * 10**9, 2 * 10**7, rows, side)


def correlate(first, parts, shifted, energy, side):
    out = (shape((BIN_DEV, NS), BF16), shape((32 if first else 16, LANES), F32))
    scratch = [pltpu.VMEM((BIN_DEV * LROWS, NS), BF16), pltpu.VMEM((BIN_DEV, WIDE), F32)]
    kernel = functools.partial(corr_kernel, first)
    return call(kernel, out, (0,) * 7, scratch, "correlate", 4 * 10**9, 10**7, *parts, shifted, energy, side)


def cmp_pairs(move):
    pairs = []
    for y in range(4):
        for x in range(4):
            for c in range(2):
                y2, x2, c2 = move(y, x, c)
                pairs.append(((y * 4 + x) * 2 + c, (y2 * 4 + x2) * 2 + c2))
    return pairs


def ring_sum(value, axis, perms):
    got = [lax.ppermute(value, axis, perm) for perm in perms]
    if len(got) == 1:
        return value + got[0]
    return (value + got[1]) + (got[0] + got[2])


def off_perm(d):
    return [(i, (i + d) % 4) for i in range(4)]


def sum_all(value):
    value = ring_sum(value, "cmp", [cmp_pairs(lambda y, x, c: (y, x, 1 - c))])
    value = ring_sum(value, "cmp", [cmp_pairs(lambda y, x, c, d=d: (y, (x + d) % 4, c)) for d in (1, 2, 3)])
    value = ring_sum(value, "cmp", [cmp_pairs(lambda y, x, c, d=d: ((y + d) % 4, x, c)) for d in (1, 2, 3)])
    return ring_sum(value, "off", [off_perm(d) for d in (1, 2, 3)])


def on_device(
    traces,
    shot_id,
    receiver_id,
    cmp_bin,
    offset_class,
    shift_int,
    frac_index,
    damping_table,
    damping_index,
):
    outgoing = pack(traces, shot_id, receiver_id, cmp_bin, offset_class, shift_int, frac_index)
    slots = lax.all_to_all(outgoing, ("cmp", "off"), split_axis=0, concat_axis=0, tiled=True)
    weight = (1.0 / (1.0 + lax.axis_index("off").astype(F32))).reshape(1, 1)
    entries = jnp.arange(damping_table.shape[0], dtype=jnp.int32)
    damps = [jnp.sum(jnp.where(entries == damping_index[i], damping_table, 0.0)) for i in range(2)]
    for iteration in range(2):
        first = iteration == 0
        if first:
            part, side, rows = stack_first(weight, slots)
        else:
            part, side = stack_next(weight, rows, side, rec, shot)
        others = [lax.ppermute(part, "off", off_perm(d)) for d in (1, 2, 3)]
        shifted, energy = shift(rows, side)
        pilot, sums = correlate(first, (part, *others), shifted, energy, side)
        sums = sum_all(sums)
        damp = damps[iteration]
        if first:
            rec_count, shot_count = sums[8:16], sums[24:32]
            rec = sums[0:8] / ((1.0 + damp) * rec_count + damp)
            shot = sums[16:24] / ((1.0 + damp) * shot_count + damp)
        else:
            rec = rec + sums[0:8] / ((1.0 + damp) * rec_count + damp)
            shot = shot + sums[8:16] / ((1.0 + damp) * shot_count + damp)
    return (shot[0:2].reshape(256), rec.reshape(1024), pilot)


def solution(mesh):
    placed = (
        P(("cmp", "off"), None),
        P(("cmp", "off")),
        P(("cmp", "off")),
        P(("cmp", "off")),
        P(("cmp", "off")),
        P(("cmp", "off")),
        P(("cmp", "off")),
        P(),
        P(),
    )
    return jax.shard_map(
        on_device, mesh=mesh, in_specs=placed, out_specs=(P(), P(), P("cmp", None)), check_vma=False
    )
```

```python
import functools

import jax
import jax.numpy as jnp
from jax import lax
from jax.experimental import pallas as pl
from jax.experimental.pallas import tpu as pltpu
from jax.sharding import PartitionSpec as P

NS = 2048
LAGS = 101
HALF = LAGS // 2
TAPS = 16
NPHASE = 32
SHIFT_MAX = 8
CLASSES = 4
TRACE_LIMIT = 4
BIN_DEV = 16
TR_DEV = 256
DEVICES = 128
SLOTS = DEVICES * TRACE_LIMIT
LANES = 128
WIDE = NS + LANES
LROWS = 112
LAG_TOP = 106
BINS_STEP = 4
PACK_ROWS = 64
PACK_OUT = 4
PACK_VMEM = 63 * 1024 * 1024
BETA = 24.0
EPS = 1e-06
F32 = jnp.float32
BF16 = jnp.bfloat16
HEAD = 16

NN = (((1,), (0,)), ((), ()))
NT = (((1,), (1,)), ((), ()))
TN = (((0,), (0,)), ((), ()))


def dot(a, b, dims, precision=None):
    return lax.dot_general(a, b, dims, precision=precision, preferred_element_type=F32)


def iota(shape, axis):
    return lax.broadcasted_iota(jnp.int32, shape, axis)


def pack_kernel(*refs):
    meta_in, x_in, out_ref = refs[:6], refs[6], refs[7]
    meta_refs, (x_ref, y_ref, o_ref, meta_sem, x_sem, o_sem) = refs[8:14], refs[14:]
    parts = TR_DEV // PACK_ROWS
    x_copies = [
        pltpu.make_async_copy(
            x_in.at[pl.ds(i * PACK_ROWS, PACK_ROWS), :], x_ref.at[pl.ds(i * PACK_ROWS, PACK_ROWS), :], x_sem.at[i]
        )
        for i in range(parts)
    ]
    meta_copies = [pltpu.make_async_copy(meta_in[i], meta_refs[i], meta_sem.at[i]) for i in range(6)]
    for copy in meta_copies + x_copies:
        copy.start()
    for copy in meta_copies:
        copy.wait()
    shot, rec, bin_, cls, whole, frac = [ref[...] for ref in meta_refs]
    dest = (bin_ // BIN_DEV) * CLASSES + cls
    rows = [
        shot // 128,
        shot % 128,
        rec // 128,
        rec % 128,
        bin_ % BIN_DEV,
        frac,
        jnp.ones_like(shot),
        whole + SHIFT_MAX,
        dest,
    ]
    sub = iota((16, TR_DEV), 0)
    info = jnp.zeros((16, TR_DEV), F32)
    for i, row in enumerate(rows):
        info = jnp.where(sub == i, row.astype(F32), info)
    place = (iota((16, LANES), 1) == iota((16, LANES), 0) + HEAD).astype(F32).astype(BF16)
    cols = dot(info.astype(BF16), place, TN)
    amount = cols[:, HEAD + 7 : HEAD + 8].astype(jnp.int32)
    dest_col = cols[:, HEAD + 8 : HEAD + 9]
    same = (dest_col == dest.astype(F32)) & (iota((TR_DEV, TR_DEV), 0) < iota((TR_DEV, TR_DEV), 1))
    rank = jnp.sum(jnp.where(same, 1.0, 0.0), axis=0, keepdims=True).astype(jnp.int32)
    slot = dest * TRACE_LIMIT + rank
    onehot = (iota((SLOTS, TR_DEV), 0) == slot).astype(F32).astype(BF16)
    on = [((amount >> bit) & 1).astype(F32).astype(BF16) > 0 for bit in range(5)]
    cols = cols.astype(BF16)
    step = 32
    for r in range(0, TR_DEV, step):
        if r % PACK_ROWS == 0:
            x_copies[r // PACK_ROWS].wait()
        y = jnp.concatenate([x_ref[r : r + step, :], jnp.zeros((step, LANES), BF16)], axis=1)
        y = pltpu.roll(y, SHIFT_MAX, 1)
        for bit in range(5):
            y = jnp.where(on[bit][r : r + step, :], pltpu.roll(y, WIDE - (1 << bit), 1), y)
        y_ref[r : r + step, :NS] = y[:, :NS]
        y_ref[r : r + step, NS:] = y[:, NS:] + cols[r : r + step, :]
    out_copies = []
    group = DEVICES // PACK_OUT
    for i in range(PACK_OUT):
        rows = onehot[i * group * TRACE_LIMIT : (i + 1) * group * TRACE_LIMIT, :]
        placed = dot(rows, y_ref[...], NN).reshape(group, TRACE_LIMIT, WIDE).astype(BF16)
        o_ref[i * group : (i + 1) * group] = placed
        copy = pltpu.make_async_copy(
            o_ref.at[pl.ds(i * group, group)], out_ref.at[pl.ds(i * group, group)], o_sem.at[i]
        )
        copy.start()
        out_copies.append(copy)
    for copy in out_copies:
        copy.wait()


def one_hot_rows(row, count):
    return (iota((count, SLOTS), 0) == row.astype(jnp.int32)).astype(F32)


def unit(size):
    return (iota((size, size), 0) == iota((size, size), 1)).astype(F32).astype(BF16)


def stack_rows(weight, y_ref, head, frac, side_ref, part_ref, sum_ref):
    live = head[6:7, :]
    u = (iota((TAPS, SLOTS), 0) - (TAPS // 2 - 1)).astype(F32) - frac
    angle = jnp.pi * u
    safe = jnp.where(u == 0.0, 1.0, angle)
    sinc = jnp.where(u == 0.0, 1.0, jnp.sin(safe) / safe)
    taps = sinc * (0.5 + 0.5 * jnp.cos(angle * (1.0 / (TAPS // 2))))
    side_ref[0:16, :] = head
    side_ref[16:32, :] = taps
    member = one_hot_rows(head[4:5, :], BIN_DEV) * live
    rows = [member * taps[k : k + 1, :] for k in range(TAPS)]
    high = [row.astype(BF16) for row in rows]
    low = [(row - top.astype(F32)).astype(BF16) for row, top in zip(rows, high)]
    slots = y_ref[...]
    sum_ref[...] = dot(jnp.concatenate(high, axis=0), slots, NN) + dot(jnp.concatenate(low, axis=0), slots, NN)
    total = jnp.zeros((BIN_DEV, WIDE), F32)
    for k in range(TAPS):
        total = total + pltpu.roll(sum_ref[k * BIN_DEV : (k + 1) * BIN_DEV, :], (TAPS // 2 - 1 - k) % WIDE, 1)
    part_ref[:, :NS] = (weight * total[:, :NS]).astype(BF16)
    mass = weight * jnp.sum(member, axis=1, keepdims=True)
    m0 = mass.astype(BF16).astype(F32)
    m1 = (mass - m0).astype(BF16).astype(F32)
    m2 = mass - m0 - m1
    lane = iota((BIN_DEV, LANES), 1)
    tail = jnp.where(lane == 0, m0, jnp.where(lane == 1, m1, jnp.where(lane == 2, m2, 0.0)))
    part_ref[:, NS:] = tail.astype(BF16)


def first_kernel(weight_ref, slots_ref, part_ref, side_ref, y_ref, sum_ref):
    y_ref[...] = slots_ref[...].reshape(SLOTS, WIDE)
    head = dot(unit(LANES), y_ref[:, NS:], NT)[HEAD : HEAD + 16, :]
    stack_rows(weight_ref[0, 0], y_ref, head, head[5:6, :] * (1.0 / NPHASE), side_ref, part_ref, sum_ref)


def paired(refs):
    return (refs[0][...] + refs[2][...]) + (refs[1][...] + refs[3][...])


def next_kernel(
    weight_ref, index_ref, table_ref, y_ref, head_ref, g0, g1, g2, g3, part_ref, side_ref, known_ref, sum_ref
):
    damp = table_ref[index_ref[0]]
    sums = paired((g0, g1, g2, g3))
    known_ref[0:8, :] = sums[0:8, :] / ((1.0 + damp) * sums[8:16, :] + damp)
    known_ref[8:16, :] = sums[16:24, :] / ((1.0 + damp) * sums[24:32, :] + damp)
    known_ref[16:24, :] = sums[8:16, :]
    known_ref[24:32, :] = sums[24:32, :]
    head = head_ref[0:16, :]
    frac = head[5:6, :] * (1.0 / NPHASE)
    for base, at in ((8, 0), (0, 2)):
        low = one_hot_rows(head[at + 1 : at + 2, :], 128)
        high = one_hot_rows(head[at : at + 1, :], 8)
        found = dot(known_ref[base : base + 8, :], low, NN, lax.Precision.HIGHEST)
        frac = frac + jnp.sum(found * high, axis=0, keepdims=True)
    stack_rows(weight_ref[0, 0], y_ref, head, frac, side_ref, part_ref, sum_ref)


def last_kernel(index_ref, table_ref, known_ref, g0, g1, g2, g3, rec_ref, shot_ref):
    damp = table_ref[index_ref[1]]
    sums = paired((g0, g1, g2, g3))
    rec_ref[...] = known_ref[0:8, :] + sums[0:8, :] / ((1.0 + damp) * known_ref[16:24, :] + damp)
    shot_ref[...] = known_ref[8:10, :] + sums[8:10, :] / ((1.0 + damp) * known_ref[24:26, :] + damp)


def shift_kernel(y_ref, side_ref, st_ref, energy_ref, xt_ref):
    eye = unit(LANES)
    groups = SLOTS // LANES
    for c in range(NS // LANES):
        block = dot(eye, y_ref[:, c * LANES : (c + 1) * LANES], NT)
        for q in range(groups):
            xt_ref[q, 8 + c * LANES : 8 + (c + 1) * LANES, :] = block[:, q * LANES : (q + 1) * LANES]
    block = dot(eye, y_ref[:, NS:], NT)
    for q in range(groups):
        part = block[:, q * LANES : (q + 1) * LANES]
        xt_ref[q, 0:8, :] = part[120:128, :]
        xt_ref[q, 8 + NS : 16 + NS, :] = part[0:8, :]
    chunk = 32
    energies = []
    for q in range(groups):
        tap = [
            jnp.broadcast_to(side_ref[16 + k : 17 + k, q * LANES : (q + 1) * LANES], (8, LANES)) for k in range(TAPS)
        ]

        def body(i, energy):
            base = pl.multiple_of(i * chunk, chunk)
            totals = [None] * (chunk // 8)
            for p in range(chunk + TAPS - 8):
                window = xt_ref[q, pl.ds(base + 1 + p, 8), :]
                for h in range(chunk // 8):
                    k = p - 8 * h
                    if 0 <= k < TAPS:
                        term = tap[k] * window
                        totals[h] = term if totals[h] is None else totals[h] + term
            for h in range(0, chunk // 8, 2):
                rounded = jnp.concatenate(totals[h : h + 2], axis=0).astype(BF16)
                st_ref[pl.ds(base + 8 * h, 16), q * LANES : (q + 1) * LANES] = rounded
                wide = rounded.astype(F32)
                energy = energy + wide[0:8, :] * wide[0:8, :] + wide[8:16, :] * wide[8:16, :]
            return energy

        energy = lax.fori_loop(0, NS // chunk, body, jnp.zeros((8, LANES), F32), unroll=2)
        energies.append(jnp.sum(energy, axis=0, keepdims=True))
    energy_ref[...] = jnp.broadcast_to(jnp.concatenate(energies, axis=1), (8, SLOTS))


def corr_kernel(first, p0_ref, p1_ref, p2_ref, p3_ref, st_ref, energy_ref, side_ref, pilot_ref, grad_ref, lag_ref, wide_ref):
    total = (p0_ref[...].astype(F32) + p2_ref[...].astype(F32)) + (
        p1_ref[...].astype(F32) + p3_ref[...].astype(F32)
    )
    mass = (total[:, NS : NS + 1] + total[:, NS + 1 : NS + 2]) + total[:, NS + 2 : NS + 3]
    pilot = (total[:, :NS] * lax.rsqrt(mass + 1.0)).astype(BF16)
    pilot_ref[...] = pilot
    wide = pilot.astype(F32)
    wide_ref[:, :NS] = wide
    wide_ref[:, NS:] = jnp.zeros((BIN_DEV, LANES), F32)
    pilot_scale = lax.rsqrt(jnp.sum(wide * wide, axis=1, keepdims=True) + EPS)
    head = side_ref[0:16, :]
    live = head[6:7, :]
    member = one_hot_rows(head[4:5, :], BIN_DEV) * live
    corr = jnp.zeros((LROWS, SLOTS), F32)
    for b0 in range(0, BIN_DEV, BINS_STEP):
        for bb in range(BINS_STEP):
            row = jnp.broadcast_to(wide_ref[b0 + bb : b0 + bb + 1, :], (8, WIDE))
            for g in range(0, LROWS, 16):
                two = [
                    pltpu.roll(row, (WIDE - (LAG_TOP - HALF) + g + h) % WIDE, 1, stride=1, stride_axis=0)[:, :NS]
                    for h in (0, 8)
                ]
                at = (b0 + bb) * LROWS + g
                lag_ref[at : at + 16, :] = jnp.concatenate(two, axis=0).astype(BF16)
        every = dot(lag_ref[b0 * LROWS : (b0 + BINS_STEP) * LROWS, :], st_ref[...], NN)
        for bb in range(BINS_STEP):
            corr = corr + member[b0 + bb : b0 + bb + 1, :] * every[bb * LROWS : (bb + 1) * LROWS, :]
    scale = lax.rsqrt(energy_ref[0:1, :] + EPS) * jnp.sum(member * pilot_scale, axis=0, keepdims=True)
    lag = LAG_TOP - iota((LROWS, SLOTS), 0)
    exponent = jnp.where((lag >= 0) & (lag < LAGS), jnp.exp(BETA * (corr * scale)), 0.0)
    delay = jnp.sum(exponent * (lag - HALF).astype(F32), axis=0, keepdims=True) / jnp.sum(
        exponent, axis=0, keepdims=True
    )
    misfit = -delay * live
    for at, out in ((2, 0), (0, 16 if first else 8)):
        low = one_hot_rows(head[at + 1 : at + 2, :], 128)
        high = one_hot_rows(head[at : at + 1, :], 8)
        values = high * misfit
        if first:
            values = jnp.concatenate([values, high * live], axis=0)
        sums = dot(values, low, NT, lax.Precision.HIGHEST)
        grad_ref[out : out + sums.shape[0], :] = sums


VMEM = pl.BlockSpec(memory_space=pltpu.VMEM)
HBM = pl.BlockSpec(memory_space=pl.ANY)
SMEM = pl.BlockSpec(memory_space=pltpu.SMEM)
PARAMS = pltpu.CompilerParams(vmem_limit_bytes=40 * 1024 * 1024)


def shape(dims, dtype):
    return jax.ShapeDtypeStruct(dims, dtype)


def call(kernel, out, memory, scratch, name, flops, moved, *args):
    return pl.pallas_call(
        kernel,
        out_shape=out,
        in_specs=[SMEM if space else VMEM for space in memory],
        out_specs=jax.tree.map(lambda _: VMEM, out),
        scratch_shapes=scratch,
        compiler_params=PARAMS,
        cost_estimate=pl.CostEstimate(flops=flops, bytes_accessed=moved, transcendentals=0),
        name=name,
    )(*args)


def pack(traces, *meta):
    scratch = [pltpu.VMEM((1, TR_DEV), jnp.int32)] * 6 + [
        pltpu.VMEM((TR_DEV, NS), BF16),
        pltpu.VMEM((TR_DEV, WIDE), BF16),
        pltpu.VMEM((DEVICES, TRACE_LIMIT, WIDE), BF16),
        pltpu.SemaphoreType.DMA((6,)),
        pltpu.SemaphoreType.DMA((TR_DEV // PACK_ROWS,)),
        pltpu.SemaphoreType.DMA((PACK_OUT,)),
    ]
    return pl.pallas_call(
        pack_kernel,
        out_shape=shape((DEVICES, TRACE_LIMIT, WIDE), BF16),
        in_specs=[HBM] * 7,
        out_specs=HBM,
        scratch_shapes=scratch,
        compiler_params=pltpu.CompilerParams(vmem_limit_bytes=PACK_VMEM),
        name="pack",
    )(*[row.reshape(1, TR_DEV) for row in meta], traces)


PART = shape((BIN_DEV, WIDE), BF16)
SIDE = shape((32, SLOTS), F32)
ROWS = pltpu.VMEM((TAPS * BIN_DEV, WIDE), F32)


def stack_first(weight, slots):
    out = (PART, SIDE, shape((SLOTS, WIDE), BF16))
    return call(first_kernel, out, (1, 0), [ROWS], "stack_first", 3 * 10**9, 10**7, weight, slots)


KNOWN = shape((32, LANES), F32)


def stack_next(weight, index, table, rows, side, sums):
    memory = (1, 1, 1) + (0,) * 6
    out = (PART, SIDE, KNOWN)
    return call(
        next_kernel, out, memory, [ROWS], "stack_next", 3 * 10**9, 10**7, weight, index, table, rows, side, *sums
    )


def finish(index, table, known, sums):
    out = (shape((8, LANES), F32), shape((2, LANES), F32))
    return call(last_kernel, out, (1, 1) + (0,) * 5, [], "finish", 10**4, 10**5, index, table, known, *sums)


def shift(rows, side):
    out = (shape((NS, SLOTS), BF16), shape((8, SLOTS), F32))
    scratch = [pltpu.VMEM((SLOTS // LANES, NS + 16, LANES), F32)]
    return call(shift_kernel, out, (0, 0), scratch, "shift", 6 * 10**9, 2 * 10**7, rows, side)


def correlate(first, parts, shifted, energy, side):
    out = (shape((BIN_DEV, NS), BF16), shape((32 if first else 16, LANES), F32))
    scratch = [pltpu.VMEM((BIN_DEV * LROWS, NS), BF16), pltpu.VMEM((BIN_DEV, WIDE), F32)]
    kernel = functools.partial(corr_kernel, first)
    return call(kernel, out, (0,) * 7, scratch, "correlate", 4 * 10**9, 10**7, *parts, shifted, energy, side)


def cmp_pairs(move):
    pairs = []
    for y in range(4):
        for x in range(4):
            for c in range(2):
                y2, x2, c2 = move(y, x, c)
                pairs.append(((y * 4 + x) * 2 + c, (y2 * 4 + x2) * 2 + c2))
    return pairs


def ring_sum(value, axis, perms):
    got = [lax.ppermute(value, axis, perm) for perm in perms]
    if len(got) == 1:
        return value + got[0]
    return (value + got[1]) + (got[0] + got[2])


def off_perm(d):
    return [(i, (i + d) % 4) for i in range(4)]


def sum_most(value):
    value = ring_sum(value, "cmp", [cmp_pairs(lambda y, x, c: (y, x, 1 - c))])
    value = ring_sum(value, "cmp", [cmp_pairs(lambda y, x, c, d=d: (y, (x + d) % 4, c)) for d in (1, 2, 3)])
    value = ring_sum(value, "cmp", [cmp_pairs(lambda y, x, c, d=d: ((y + d) % 4, x, c)) for d in (1, 2, 3)])
    return (value, *[lax.ppermute(value, "off", off_perm(d)) for d in (1, 2, 3)])


def from_stack(first, part, rows, side):
    others = [lax.ppermute(part, "off", off_perm(d)) for d in (1, 2, 3)]
    shifted, energy = shift(rows, side)
    pilot, sums = correlate(first, (part, *others), shifted, energy, side)
    return pilot, sum_most(sums)


def on_device(
    traces,
    shot_id,
    receiver_id,
    cmp_bin,
    offset_class,
    shift_int,
    frac_index,
    damping_table,
    damping_index,
):
    outgoing = pack(traces, shot_id, receiver_id, cmp_bin, offset_class, shift_int, frac_index)
    slots = lax.all_to_all(outgoing, ("cmp", "off"), split_axis=0, concat_axis=0, tiled=True)
    weight = (1.0 / (1.0 + lax.axis_index("off").astype(F32))).reshape(1, 1)
    part, side, rows = stack_first(weight, slots)
    pilot, sums = from_stack(True, part, rows, side)
    part, side, known = stack_next(weight, damping_index, damping_table, rows, side, sums)
    pilot, sums = from_stack(False, part, rows, side)
    rec, shot = finish(damping_index, damping_table, known, sums)
    return (shot.reshape(-1), rec.reshape(-1), pilot)


def solution(mesh):
    placed = (
        P(("cmp", "off"), None),
        P(("cmp", "off")),
        P(("cmp", "off")),
        P(("cmp", "off")),
        P(("cmp", "off")),
        P(("cmp", "off")),
        P(("cmp", "off")),
        P(),
        P(),
    )
    return jax.shard_map(
        on_device, mesh=mesh, in_specs=placed, out_specs=(P(), P(), P("cmp", None)), check_vma=False
    )
```

```python
import functools

import jax
import jax.numpy as jnp
from jax import lax
from jax.experimental import pallas as pl
from jax.experimental.pallas import tpu as pltpu
from jax.sharding import Mesh
from jax.sharding import PartitionSpec as P

NS = 2048
LAGS = 101
HALF = LAGS // 2
TAPS = 16
NPHASE = 32
SHIFT_MAX = 8
CLASSES = 4
TRACE_LIMIT = 4
BIN_DEV = 16
TR_DEV = 256
DEVICES = 128
SLOTS = DEVICES * TRACE_LIMIT
LANES = 128
WIDE = NS + LANES
LROWS = 112
LAG_TOP = 106
BINS_STEP = 4
PACK_ROWS = 64
PACK_OUT = 4
PACK_VMEM = 63 * 1024 * 1024
BETA = 24.0
EPS = 1e-06
F32 = jnp.float32
BF16 = jnp.bfloat16
HEAD = 16
AXES = ("y", "x", "core", "off")

NN = (((1,), (0,)), ((), ()))
NT = (((1,), (1,)), ((), ()))
TN = (((0,), (0,)), ((), ()))


def dot(a, b, dims, precision=None):
    return lax.dot_general(a, b, dims, precision=precision, preferred_element_type=F32)


def iota(shape, axis):
    return lax.broadcasted_iota(jnp.int32, shape, axis)


def pack_kernel(*refs):
    meta_in, x_in, out_ref = refs[:6], refs[6], refs[7]
    meta_refs, (x_ref, y_ref, o_ref, meta_sem, x_sem, o_sem) = refs[8:14], refs[14:]
    parts = TR_DEV // PACK_ROWS
    x_copies = [
        pltpu.make_async_copy(
            x_in.at[pl.ds(i * PACK_ROWS, PACK_ROWS), :], x_ref.at[pl.ds(i * PACK_ROWS, PACK_ROWS), :], x_sem.at[i]
        )
        for i in range(parts)
    ]
    meta_copies = [pltpu.make_async_copy(meta_in[i], meta_refs[i], meta_sem.at[i]) for i in range(6)]
    for copy in meta_copies + x_copies:
        copy.start()
    for copy in meta_copies:
        copy.wait()
    shot, rec, bin_, cls, whole, frac = [ref[...] for ref in meta_refs]
    dest = (bin_ // BIN_DEV) * CLASSES + cls
    rows = [
        shot // 128,
        shot % 128,
        rec // 128,
        rec % 128,
        bin_ % BIN_DEV,
        frac,
        jnp.ones_like(shot),
        whole + SHIFT_MAX,
        dest,
    ]
    sub = iota((16, TR_DEV), 0)
    info = jnp.zeros((16, TR_DEV), F32)
    for i, row in enumerate(rows):
        info = jnp.where(sub == i, row.astype(F32), info)
    place = (iota((16, LANES), 1) == iota((16, LANES), 0) + HEAD).astype(F32).astype(BF16)
    cols = dot(info.astype(BF16), place, TN)
    amount = cols[:, HEAD + 7 : HEAD + 8].astype(jnp.int32)
    dest_col = cols[:, HEAD + 8 : HEAD + 9]
    same = (dest_col == dest.astype(F32)) & (iota((TR_DEV, TR_DEV), 0) < iota((TR_DEV, TR_DEV), 1))
    rank = jnp.sum(jnp.where(same, 1.0, 0.0), axis=0, keepdims=True).astype(jnp.int32)
    slot = dest * TRACE_LIMIT + rank
    onehot = (iota((SLOTS, TR_DEV), 0) == slot).astype(F32).astype(BF16)
    on = [((amount >> bit) & 1).astype(F32).astype(BF16) > 0 for bit in range(5)]
    cols = cols.astype(BF16)
    step = 32
    for r in range(0, TR_DEV, step):
        if r % PACK_ROWS == 0:
            x_copies[r // PACK_ROWS].wait()
        y = jnp.concatenate([x_ref[r : r + step, :], jnp.zeros((step, LANES), BF16)], axis=1)
        y = pltpu.roll(y, SHIFT_MAX, 1)
        for bit in range(5):
            y = jnp.where(on[bit][r : r + step, :], pltpu.roll(y, WIDE - (1 << bit), 1), y)
        y_ref[r : r + step, :NS] = y[:, :NS]
        y_ref[r : r + step, NS:] = y[:, NS:] + cols[r : r + step, :]
    out_copies = []
    group = DEVICES // PACK_OUT
    for i in range(PACK_OUT):
        rows = onehot[i * group * TRACE_LIMIT : (i + 1) * group * TRACE_LIMIT, :]
        placed = dot(rows, y_ref[...], NN).reshape(group, TRACE_LIMIT, WIDE).astype(BF16)
        o_ref[i * group : (i + 1) * group] = placed
        copy = pltpu.make_async_copy(
            o_ref.at[pl.ds(i * group, group)], out_ref.at[pl.ds(i * group, group)], o_sem.at[i]
        )
        copy.start()
        out_copies.append(copy)
    for copy in out_copies:
        copy.wait()


def one_hot_rows(row, count):
    return (iota((count, SLOTS), 0) == row.astype(jnp.int32)).astype(F32)


def unit(size):
    return (iota((size, size), 0) == iota((size, size), 1)).astype(F32).astype(BF16)


def stack_rows(weight, y_ref, head, frac, side_ref, part_ref, sum_ref):
    live = head[6:7, :]
    u = (iota((TAPS, SLOTS), 0) - (TAPS // 2 - 1)).astype(F32) - frac
    angle = jnp.pi * u
    safe = jnp.where(u == 0.0, 1.0, angle)
    sinc = jnp.where(u == 0.0, 1.0, jnp.sin(safe) / safe)
    taps = sinc * (0.5 + 0.5 * jnp.cos(angle * (1.0 / (TAPS // 2))))
    side_ref[0:16, :] = head
    side_ref[16:32, :] = taps
    member = one_hot_rows(head[4:5, :], BIN_DEV) * live
    rows = [member * taps[k : k + 1, :] for k in range(TAPS)]
    high = [row.astype(BF16) for row in rows]
    low = [(row - top.astype(F32)).astype(BF16) for row, top in zip(rows, high)]
    slots = y_ref[...]
    sum_ref[...] = dot(jnp.concatenate(high, axis=0), slots, NN) + dot(jnp.concatenate(low, axis=0), slots, NN)
    total = jnp.zeros((BIN_DEV, WIDE), F32)
    for k in range(TAPS):
        total = total + pltpu.roll(sum_ref[k * BIN_DEV : (k + 1) * BIN_DEV, :], (TAPS // 2 - 1 - k) % WIDE, 1)
    part_ref[:, :NS] = (weight * total[:, :NS]).astype(BF16)
    mass = weight * jnp.sum(member, axis=1, keepdims=True)
    m0 = mass.astype(BF16).astype(F32)
    m1 = (mass - m0).astype(BF16).astype(F32)
    m2 = mass - m0 - m1
    lane = iota((BIN_DEV, LANES), 1)
    tail = jnp.where(lane == 0, m0, jnp.where(lane == 1, m1, jnp.where(lane == 2, m2, 0.0)))
    part_ref[:, NS:] = tail.astype(BF16)


def first_kernel(weight_ref, slots_ref, part_ref, side_ref, y_ref, sum_ref):
    y_ref[...] = slots_ref[...].reshape(SLOTS, WIDE)
    head = dot(unit(LANES), y_ref[:, NS:], NT)[HEAD : HEAD + 16, :]
    stack_rows(weight_ref[0, 0], y_ref, head, head[5:6, :] * (1.0 / NPHASE), side_ref, part_ref, sum_ref)


def next_kernel(
    weight_ref, index_ref, table_ref, y_ref, head_ref, sums_ref, part_ref, side_ref, known_ref, sum_ref
):
    damp = table_ref[index_ref[0]]
    sums = gathered(sums_ref)
    count = 256.0 * sums[10:20, :] + sums[20:30, :]
    known_ref[...] = jnp.zeros_like(known_ref)
    known_ref[0:10, :] = sums[0:10, :] / ((1.0 + damp) * count + damp)
    known_ref[16:26, :] = count
    head = head_ref[0:16, :]
    frac = head[5:6, :] * (1.0 / NPHASE)
    for base, at in ((8, 0), (0, 2)):
        low = one_hot_rows(head[at + 1 : at + 2, :], 128)
        high = one_hot_rows(head[at : at + 1, :], 8)
        found = dot(known_ref[base : base + 8, :], low, NN, lax.Precision.HIGHEST)
        frac = frac + jnp.sum(found * high, axis=0, keepdims=True)
    stack_rows(weight_ref[0, 0], y_ref, head, frac, side_ref, part_ref, sum_ref)


def last_kernel(index_ref, table_ref, known_ref, sums_ref, rec_ref, shot_ref):
    damp = table_ref[index_ref[1]]
    step = gathered(sums_ref) / ((1.0 + damp) * known_ref[16:32, :] + damp)
    total = known_ref[0:16, :] + step
    rec_ref[...] = total[0:8, :]
    shot_ref[...] = total[8:10, :]


def shift_kernel(y_ref, side_ref, st_ref, energy_ref, xt_ref):
    eye = unit(LANES)
    groups = SLOTS // LANES
    for c in range(NS // LANES):
        block = dot(eye, y_ref[:, c * LANES : (c + 1) * LANES], NT)
        for q in range(groups):
            xt_ref[q, 8 + c * LANES : 8 + (c + 1) * LANES, :] = block[:, q * LANES : (q + 1) * LANES]
    block = dot(eye, y_ref[:, NS:], NT)
    for q in range(groups):
        part = block[:, q * LANES : (q + 1) * LANES]
        xt_ref[q, 0:8, :] = part[120:128, :]
        xt_ref[q, 8 + NS : 16 + NS, :] = part[0:8, :]
    chunk = 32
    energies = []
    for q in range(groups):
        tap = [
            jnp.broadcast_to(side_ref[16 + k : 17 + k, q * LANES : (q + 1) * LANES], (8, LANES)) for k in range(TAPS)
        ]

        def body(i, energy):
            base = pl.multiple_of(i * chunk, chunk)
            totals = [None] * (chunk // 8)
            for p in range(chunk + TAPS - 8):
                window = xt_ref[q, pl.ds(base + 1 + p, 8), :]
                for h in range(chunk // 8):
                    k = p - 8 * h
                    if 0 <= k < TAPS:
                        term = tap[k] * window
                        totals[h] = term if totals[h] is None else totals[h] + term
            for h in range(0, chunk // 8, 2):
                rounded = jnp.concatenate(totals[h : h + 2], axis=0).astype(BF16)
                st_ref[pl.ds(base + 8 * h, 16), q * LANES : (q + 1) * LANES] = rounded
                wide = rounded.astype(F32)
                energy = energy + wide[0:8, :] * wide[0:8, :] + wide[8:16, :] * wide[8:16, :]
            return energy

        energy = lax.fori_loop(0, NS // chunk, body, jnp.zeros((8, LANES), F32), unroll=2)
        energies.append(jnp.sum(energy, axis=0, keepdims=True))
    energy_ref[...] = jnp.broadcast_to(jnp.concatenate(energies, axis=1), (8, SLOTS))


def corr_kernel(first, p0_ref, p1_ref, p2_ref, p3_ref, st_ref, energy_ref, side_ref, pilot_ref, grad_ref, lag_ref, wide_ref):
    total = (p0_ref[...].astype(F32) + p2_ref[...].astype(F32)) + (
        p1_ref[...].astype(F32) + p3_ref[...].astype(F32)
    )
    mass = (total[:, NS : NS + 1] + total[:, NS + 1 : NS + 2]) + total[:, NS + 2 : NS + 3]
    pilot = (total[:, :NS] * lax.rsqrt(mass + 1.0)).astype(BF16)
    pilot_ref[...] = pilot
    wide = pilot.astype(F32)
    wide_ref[:, :NS] = wide
    wide_ref[:, NS:] = jnp.zeros((BIN_DEV, LANES), F32)
    pilot_scale = lax.rsqrt(jnp.sum(wide * wide, axis=1, keepdims=True) + EPS)
    head = side_ref[0:16, :]
    live = head[6:7, :]
    member = one_hot_rows(head[4:5, :], BIN_DEV) * live
    corr = jnp.zeros((LROWS, SLOTS), F32)
    for b0 in range(0, BIN_DEV, BINS_STEP):
        for bb in range(BINS_STEP):
            row = jnp.broadcast_to(wide_ref[b0 + bb : b0 + bb + 1, :], (8, WIDE))
            for g in range(0, LROWS, 16):
                two = [
                    pltpu.roll(row, (WIDE - (LAG_TOP - HALF) + g + h) % WIDE, 1, stride=1, stride_axis=0)[:, :NS]
                    for h in (0, 8)
                ]
                at = (b0 + bb) * LROWS + g
                lag_ref[at : at + 16, :] = jnp.concatenate(two, axis=0).astype(BF16)
        every = dot(lag_ref[b0 * LROWS : (b0 + BINS_STEP) * LROWS, :], st_ref[...], NN)
        for bb in range(BINS_STEP):
            corr = corr + member[b0 + bb : b0 + bb + 1, :] * every[bb * LROWS : (bb + 1) * LROWS, :]
    scale = lax.rsqrt(energy_ref[0:1, :] + EPS) * jnp.sum(member * pilot_scale, axis=0, keepdims=True)
    lag = LAG_TOP - iota((LROWS, SLOTS), 0)
    exponent = jnp.where((lag >= 0) & (lag < LAGS), jnp.exp(BETA * (corr * scale)), 0.0)
    delay = jnp.sum(exponent * (lag - HALF).astype(F32), axis=0, keepdims=True) / jnp.sum(
        exponent, axis=0, keepdims=True
    )
    misfit = -delay * live
    grad_ref[...] = jnp.zeros_like(grad_ref)
    for at, out, rows in ((2, 0, 8), (0, 8, 2)):
        low = one_hot_rows(head[at + 1 : at + 2, :], 128)
        high = one_hot_rows(head[at : at + 1, :], 8)
        values = high * misfit
        if first:
            values = jnp.concatenate([values, high * live], axis=0)
        sums = dot(values, low, NT, lax.Precision.HIGHEST)
        grad_ref[out : out + rows, :] = sums[0:rows, :]
        if first:
            grad_ref[16 + out : 16 + out + rows, :] = sums[8 : 8 + rows, :]


def spread_kernel(own_ref, other_ref, out_ref, rows_ref):
    total = own_ref[...] + other_ref[...]
    rows_ref[...] = jnp.zeros_like(rows_ref)
    rows_ref[0:10, :] = total[0:10, :]
    if total.shape[0] > 16:
        count = total[16:26, :]
        large = jnp.floor(count * (1.0 / 256.0))
        rows_ref[10:20, :] = large
        rows_ref[20:30, :] = count - 256.0 * large
    out_ref[...] = jnp.broadcast_to(rows_ref[...].astype(BF16)[None], out_ref.shape)


def gathered(ref):
    return jnp.sum(ref[...].astype(F32), axis=0)


VMEM = pl.BlockSpec(memory_space=pltpu.VMEM)
HBM = pl.BlockSpec(memory_space=pl.ANY)
SMEM = pl.BlockSpec(memory_space=pltpu.SMEM)
PARAMS = pltpu.CompilerParams(vmem_limit_bytes=40 * 1024 * 1024)


def shape(dims, dtype):
    return jax.ShapeDtypeStruct(dims, dtype)


def call(kernel, out, memory, scratch, name, flops, moved, *args):
    return pl.pallas_call(
        kernel,
        out_shape=out,
        in_specs=[SMEM if space else VMEM for space in memory],
        out_specs=jax.tree.map(lambda _: VMEM, out),
        scratch_shapes=scratch,
        compiler_params=PARAMS,
        cost_estimate=pl.CostEstimate(flops=flops, bytes_accessed=moved, transcendentals=0),
        name=name,
    )(*args)


def pack(traces, *meta):
    scratch = [pltpu.VMEM((1, TR_DEV), jnp.int32)] * 6 + [
        pltpu.VMEM((TR_DEV, NS), BF16),
        pltpu.VMEM((TR_DEV, WIDE), BF16),
        pltpu.VMEM((DEVICES, TRACE_LIMIT, WIDE), BF16),
        pltpu.SemaphoreType.DMA((6,)),
        pltpu.SemaphoreType.DMA((TR_DEV // PACK_ROWS,)),
        pltpu.SemaphoreType.DMA((PACK_OUT,)),
    ]
    return pl.pallas_call(
        pack_kernel,
        out_shape=shape((DEVICES, TRACE_LIMIT, WIDE), BF16),
        in_specs=[HBM] * 7,
        out_specs=HBM,
        scratch_shapes=scratch,
        compiler_params=pltpu.CompilerParams(vmem_limit_bytes=PACK_VMEM),
        name="pack",
    )(*[row.reshape(1, TR_DEV) for row in meta], traces)


PART = shape((BIN_DEV, WIDE), BF16)
SIDE = shape((32, SLOTS), F32)
ROWS = pltpu.VMEM((TAPS * BIN_DEV, WIDE), F32)


def stack_first(weight, slots):
    out = (PART, SIDE, shape((SLOTS, WIDE), BF16))
    return call(first_kernel, out, (1, 0), [ROWS], "stack_first", 3 * 10**9, 10**7, weight, slots)


KNOWN = shape((32, LANES), F32)


def stack_next(weight, index, table, rows, side, sums):
    memory = (1, 1, 1, 0, 0, 0)
    out = (PART, SIDE, KNOWN)
    return call(
        next_kernel, out, memory, [ROWS], "stack_next", 3 * 10**9, 10**7, weight, index, table, rows, side, sums
    )


def finish(index, table, known, sums):
    out = (shape((8, LANES), F32), shape((2, LANES), F32))
    return call(last_kernel, out, (1, 1, 0, 0), [], "finish", 10**4, 10**5, index, table, known, sums)


def shift(rows, side):
    out = (shape((NS, SLOTS), BF16), shape((8, SLOTS), F32))
    scratch = [pltpu.VMEM((SLOTS // LANES, NS + 16, LANES), F32)]
    return call(shift_kernel, out, (0, 0), scratch, "shift", 6 * 10**9, 2 * 10**7, rows, side)


def correlate(first, parts, shifted, energy, side):
    out = (shape((BIN_DEV, NS), BF16), shape((32 if first else 16, LANES), F32))
    scratch = [pltpu.VMEM((BIN_DEV * LROWS, NS), BF16), pltpu.VMEM((BIN_DEV, WIDE), F32)]
    kernel = functools.partial(corr_kernel, first)
    return call(kernel, out, (0,) * 7, scratch, "correlate", 4 * 10**9, 10**7, *parts, shifted, energy, side)


def off_perm(d):
    return [(i, (i + d) % 4) for i in range(4)]


def sum_copies(value):
    other = lax.ppermute(value, "core", [(0, 1), (1, 0)])
    out = shape((DEVICES // 2, value.shape[0], LANES), BF16)
    scratch = [pltpu.VMEM(value.shape, F32)]
    copies = call(spread_kernel, out, (0, 0), scratch, "spread", 10**5, 10**6, value, other)
    return lax.all_to_all(copies, ("y", "x", "off"), split_axis=0, concat_axis=0, tiled=True)


def from_stack(first, part, rows, side):
    others = [lax.ppermute(part, "off", off_perm(d)) for d in (1, 2, 3)]
    shifted, energy = shift(rows, side)
    pilot, sums = correlate(first, (part, *others), shifted, energy, side)
    return pilot, sum_copies(sums)


def on_device(
    traces,
    shot_id,
    receiver_id,
    cmp_bin,
    offset_class,
    shift_int,
    frac_index,
    damping_table,
    damping_index,
):
    outgoing = pack(traces, shot_id, receiver_id, cmp_bin, offset_class, shift_int, frac_index)
    slots = lax.all_to_all(outgoing, AXES, split_axis=0, concat_axis=0, tiled=True)
    weight = (1.0 / (1.0 + lax.axis_index("off").astype(F32))).reshape(1, 1)
    part, side, rows = stack_first(weight, slots)
    pilot, sums = from_stack(True, part, rows, side)
    part, side, known = stack_next(weight, damping_index, damping_table, rows, side, sums)
    pilot, sums = from_stack(False, part, rows, side)
    rec, shot = finish(damping_index, damping_table, known, sums)
    return (shot.reshape(-1), rec.reshape(-1), pilot)


def solution(mesh):
    mesh = Mesh(mesh.devices.reshape(4, 4, 2, 4), AXES)
    placed = (P(AXES, None),) + (P(AXES),) * 6 + (P(), P())
    return jax.shard_map(
        on_device, mesh=mesh, in_specs=placed, out_specs=(P(), P(), P(AXES[:3], None)), check_vma=False
    )
```

```python
import functools

import jax
import jax.numpy as jnp
from jax import lax
from jax.experimental import pallas as pl
from jax.experimental.pallas import tpu as pltpu
from jax.sharding import Mesh
from jax.sharding import PartitionSpec as P

NS = 2048
LAGS = 101
HALF = LAGS // 2
TAPS = 16
NPHASE = 32
SHIFT_MAX = 8
CLASSES = 4
TRACE_LIMIT = 4
BIN_DEV = 16
TR_DEV = 256
DEVICES = 128
SLOTS = DEVICES * TRACE_LIMIT
LANES = 128
WIDE = NS + LANES
LROWS = 112
LAG_TOP = 106
BINS_STEP = 4
PACK_ROWS = 64
PACK_OUT = 4
PACK_VMEM = 63 * 1024 * 1024
BETA = 24.0
EPS = 1e-06
F32 = jnp.float32
BF16 = jnp.bfloat16
HEAD = 16
AXES = ("y", "x", "core", "off")

NN = (((1,), (0,)), ((), ()))
NT = (((1,), (1,)), ((), ()))
TN = (((0,), (0,)), ((), ()))


def dot(a, b, dims, precision=None):
    return lax.dot_general(a, b, dims, precision=precision, preferred_element_type=F32)


def iota(shape, axis):
    return lax.broadcasted_iota(jnp.int32, shape, axis)


def pack_kernel(*refs):
    meta_in, x_in, out_ref = refs[:6], refs[6], refs[7]
    meta_refs, (x_ref, y_ref, o_ref, meta_sem, x_sem, o_sem) = refs[8:14], refs[14:]
    parts = TR_DEV // PACK_ROWS
    x_copies = [
        pltpu.make_async_copy(
            x_in.at[pl.ds(i * PACK_ROWS, PACK_ROWS), :], x_ref.at[pl.ds(i * PACK_ROWS, PACK_ROWS), :], x_sem.at[i]
        )
        for i in range(parts)
    ]
    meta_copies = [pltpu.make_async_copy(meta_in[i], meta_refs[i], meta_sem.at[i]) for i in range(6)]
    for copy in meta_copies + x_copies:
        copy.start()
    for copy in meta_copies:
        copy.wait()
    shot, rec, bin_, cls, whole, frac = [ref[...] for ref in meta_refs]
    dest = (bin_ // BIN_DEV) * CLASSES + cls
    rows = [
        shot // 128,
        shot % 128,
        rec // 128,
        rec % 128,
        bin_ % BIN_DEV,
        frac,
        jnp.ones_like(shot),
        whole + SHIFT_MAX,
        dest,
    ]
    sub = iota((16, TR_DEV), 0)
    info = jnp.zeros((16, TR_DEV), F32)
    for i, row in enumerate(rows):
        info = jnp.where(sub == i, row.astype(F32), info)
    place = (iota((16, LANES), 1) == iota((16, LANES), 0) + HEAD).astype(F32).astype(BF16)
    cols = dot(info.astype(BF16), place, TN)
    amount = cols[:, HEAD + 7 : HEAD + 8].astype(jnp.int32)
    dest_col = cols[:, HEAD + 8 : HEAD + 9]
    same = (dest_col == dest.astype(F32)) & (iota((TR_DEV, TR_DEV), 0) < iota((TR_DEV, TR_DEV), 1))
    rank = jnp.sum(jnp.where(same, 1.0, 0.0), axis=0, keepdims=True).astype(jnp.int32)
    slot = dest * TRACE_LIMIT + rank
    onehot = (iota((SLOTS, TR_DEV), 0) == slot).astype(F32).astype(BF16)
    amount = amount - SHIFT_MAX
    tail = cols.astype(BF16)
    step = 32
    lane = iota((step, LANES), 1)
    blocks = WIDE // LANES
    for r in range(0, TR_DEV, step):
        if r % PACK_ROWS == 0:
            x_copies[r // PACK_ROWS].wait()
        source = lane + amount[r : r + step, :]
        index = source & (LANES - 1)
        turned = [
            jnp.take_along_axis(
                x_ref[r : r + step, c * LANES : (c + 1) * LANES].astype(F32), index, axis=1, mode="promise_in_bounds"
            )
            for c in range(blocks - 1)
        ] + [jnp.zeros((step, LANES), F32)]
        for c in range(blocks):
            before, after = turned[c - 1], turned[(c + 1) % blocks]
            y = jnp.where(source < 0, before, jnp.where(source >= LANES, after, turned[c])).astype(BF16)
            if c == blocks - 1:
                y = y + tail[r : r + step, :]
            y_ref[r : r + step, c * LANES : (c + 1) * LANES] = y
    out_copies = []
    group = DEVICES // PACK_OUT
    for i in range(PACK_OUT):
        rows = onehot[i * group * TRACE_LIMIT : (i + 1) * group * TRACE_LIMIT, :]
        placed = dot(rows, y_ref[...], NN).reshape(group, TRACE_LIMIT, WIDE).astype(BF16)
        o_ref[i * group : (i + 1) * group] = placed
        copy = pltpu.make_async_copy(
            o_ref.at[pl.ds(i * group, group)], out_ref.at[pl.ds(i * group, group)], o_sem.at[i]
        )
        copy.start()
        out_copies.append(copy)
    for copy in out_copies:
        copy.wait()


def one_hot_rows(row, count):
    return (iota((count, SLOTS), 0) == row.astype(jnp.int32)).astype(F32)


def one_hot_half(row, count):
    return one_hot_rows(row, count).astype(BF16)


def parts_of(value):
    top = value.astype(BF16)
    rest = value - top.astype(F32)
    middle = rest.astype(BF16)
    return jnp.concatenate([top, middle, (rest - middle.astype(F32)).astype(BF16)], axis=0)


def joined(sums):
    rows = sums.shape[0] // 3
    return (sums[0:rows, :] + sums[rows : 2 * rows, :]) + sums[2 * rows :, :]


def unit(size):
    return (iota((size, size), 0) == iota((size, size), 1)).astype(F32).astype(BF16)


def stack_rows(weight, y_ref, head, frac, side_ref, part_ref, sum_ref):
    live = head[6:7, :]
    u = (iota((TAPS, SLOTS), 0) - (TAPS // 2 - 1)).astype(F32) - frac
    angle = jnp.pi * u
    safe = jnp.where(u == 0.0, 1.0, angle)
    sinc = jnp.where(u == 0.0, 1.0, jnp.sin(safe) / safe)
    taps = sinc * (0.5 + 0.5 * jnp.cos(angle * (1.0 / (TAPS // 2))))
    side_ref[0:16, :] = head
    side_ref[16:32, :] = taps
    member = one_hot_rows(head[4:5, :], BIN_DEV) * live
    rows = [member * taps[k : k + 1, :] for k in range(TAPS)]
    high = [row.astype(BF16) for row in rows]
    low = [(row - top.astype(F32)).astype(BF16) for row, top in zip(rows, high)]
    slots = y_ref[...]
    sum_ref[...] = dot(jnp.concatenate(high, axis=0), slots, NN) + dot(jnp.concatenate(low, axis=0), slots, NN)
    total = jnp.zeros((BIN_DEV, WIDE), F32)
    for k in range(TAPS):
        total = total + pltpu.roll(sum_ref[k * BIN_DEV : (k + 1) * BIN_DEV, :], (TAPS // 2 - 1 - k) % WIDE, 1)
    part_ref[:, :NS] = (weight * total[:, :NS]).astype(BF16)
    mass = weight * jnp.sum(member, axis=1, keepdims=True)
    m0 = mass.astype(BF16).astype(F32)
    m1 = (mass - m0).astype(BF16).astype(F32)
    m2 = mass - m0 - m1
    lane = iota((BIN_DEV, LANES), 1)
    tail = jnp.where(lane == 0, m0, jnp.where(lane == 1, m1, jnp.where(lane == 2, m2, 0.0)))
    part_ref[:, NS:] = tail.astype(BF16)


def first_kernel(weight_ref, slots_ref, part_ref, side_ref, y_ref, sum_ref):
    y_ref[...] = slots_ref[...].reshape(SLOTS, WIDE)
    head = dot(unit(LANES), y_ref[:, NS:], NT)[HEAD : HEAD + 16, :]
    stack_rows(weight_ref[0, 0], y_ref, head, head[5:6, :] * (1.0 / NPHASE), side_ref, part_ref, sum_ref)


def next_kernel(
    weight_ref, index_ref, table_ref, y_ref, head_ref, sums_ref, part_ref, side_ref, known_ref, sum_ref
):
    damp = table_ref[index_ref[0]]
    sums = gathered(sums_ref)
    count = 256.0 * sums[10:20, :] + sums[20:30, :]
    known_ref[...] = jnp.zeros_like(known_ref)
    known_ref[0:10, :] = sums[0:10, :] / ((1.0 + damp) * count + damp)
    known_ref[16:26, :] = count
    head = head_ref[0:16, :]
    frac = head[5:6, :] * (1.0 / NPHASE)
    for base, at in ((8, 0), (0, 2)):
        low = one_hot_half(head[at + 1 : at + 2, :], 128)
        high = one_hot_rows(head[at : at + 1, :], 8)
        found = joined(dot(parts_of(known_ref[base : base + 8, :]), low, NN))
        frac = frac + jnp.sum(found * high, axis=0, keepdims=True)
    stack_rows(weight_ref[0, 0], y_ref, head, frac, side_ref, part_ref, sum_ref)


def last_kernel(index_ref, table_ref, known_ref, sums_ref, rec_ref, shot_ref):
    damp = table_ref[index_ref[1]]
    step = gathered(sums_ref) / ((1.0 + damp) * known_ref[16:32, :] + damp)
    total = known_ref[0:16, :] + step
    rec_ref[...] = total[0:8, :]
    shot_ref[...] = total[8:10, :]


def turn_kernel(y_ref, side_ref, st_ref, energy_ref, xt_ref):
    eye = unit(LANES)
    groups = SLOTS // LANES
    for c in range(NS // LANES):
        block = dot(eye, y_ref[:, c * LANES : (c + 1) * LANES], NT)
        for q in range(groups):
            xt_ref[q, 8 + c * LANES : 8 + (c + 1) * LANES, :] = block[:, q * LANES : (q + 1) * LANES]
    block = dot(eye, y_ref[:, NS:], NT)
    for q in range(groups):
        part = block[:, q * LANES : (q + 1) * LANES]
        xt_ref[q, 0:8, :] = part[120:128, :]
        xt_ref[q, 8 + NS : 16 + NS, :] = part[0:8, :]
    shift_kernel(xt_ref, side_ref, st_ref, energy_ref)


def shift_kernel(xt_ref, side_ref, st_ref, energy_ref):
    groups = SLOTS // LANES
    chunk = 32
    energies = []
    for q in range(groups):
        tap = [
            jnp.broadcast_to(side_ref[16 + k : 17 + k, q * LANES : (q + 1) * LANES], (8, LANES)) for k in range(TAPS)
        ]

        def body(i, energy):
            base = pl.multiple_of(i * chunk, chunk)
            totals = [None] * (chunk // 8)
            for p in range(chunk + TAPS - 8):
                window = xt_ref[q, pl.ds(base + 1 + p, 8), :]
                for h in range(chunk // 8):
                    k = p - 8 * h
                    if 0 <= k < TAPS:
                        term = tap[k] * window
                        totals[h] = term if totals[h] is None else totals[h] + term
            for h in range(0, chunk // 8, 2):
                rounded = jnp.concatenate(totals[h : h + 2], axis=0).astype(BF16)
                st_ref[pl.ds(base + 8 * h, 16), q * LANES : (q + 1) * LANES] = rounded
                energy = energy + (totals[h] * totals[h] + totals[h + 1] * totals[h + 1])
            return energy

        energy = lax.fori_loop(0, NS // chunk, body, jnp.zeros((8, LANES), F32), unroll=4)
        energies.append(jnp.sum(energy, axis=0, keepdims=True))
    energy_ref[...] = jnp.broadcast_to(jnp.concatenate(energies, axis=1), (8, SLOTS))


def corr_kernel(first, p0_ref, p1_ref, p2_ref, p3_ref, st_ref, energy_ref, side_ref, pilot_ref, grad_ref, lag_ref, wide_ref):
    total = (p0_ref[...].astype(F32) + p2_ref[...].astype(F32)) + (
        p1_ref[...].astype(F32) + p3_ref[...].astype(F32)
    )
    mass = (total[:, NS : NS + 1] + total[:, NS + 1 : NS + 2]) + total[:, NS + 2 : NS + 3]
    pilot = (total[:, :NS] * lax.rsqrt(mass + 1.0)).astype(BF16)
    pilot_ref[...] = pilot
    wide = pilot.astype(F32)
    wide_ref[:, :NS] = wide
    wide_ref[:, NS:] = jnp.zeros((BIN_DEV, LANES), F32)
    pilot_scale = lax.rsqrt(jnp.sum(wide * wide, axis=1, keepdims=True) + EPS)
    head = side_ref[0:16, :]
    live = head[6:7, :]
    member = one_hot_rows(head[4:5, :], BIN_DEV) * live
    corr = jnp.zeros((LROWS, SLOTS), F32)
    for b0 in range(0, BIN_DEV, BINS_STEP):
        for bb in range(BINS_STEP):
            row = jnp.broadcast_to(wide_ref[b0 + bb : b0 + bb + 1, :], (8, WIDE))
            for g in range(0, LROWS, 16):
                two = [
                    pltpu.roll(row, (WIDE - (LAG_TOP - HALF) + g + h) % WIDE, 1, stride=1, stride_axis=0)[:, :NS]
                    for h in (0, 8)
                ]
                at = (b0 + bb) * LROWS + g
                lag_ref[at : at + 16, :] = jnp.concatenate(two, axis=0).astype(BF16)
        every = dot(lag_ref[b0 * LROWS : (b0 + BINS_STEP) * LROWS, :], st_ref[...], NN)
        for bb in range(BINS_STEP):
            corr = corr + member[b0 + bb : b0 + bb + 1, :] * every[bb * LROWS : (bb + 1) * LROWS, :]
    scale = lax.rsqrt(energy_ref[0:1, :] + EPS) * jnp.sum(member * pilot_scale, axis=0, keepdims=True)
    lag = LAG_TOP - iota((LROWS, SLOTS), 0)
    exponent = jnp.where((lag >= 0) & (lag < LAGS), jnp.exp(BETA * (corr * scale)), 0.0)
    delay = jnp.sum(exponent * (lag - HALF).astype(F32), axis=0, keepdims=True) / jnp.sum(
        exponent, axis=0, keepdims=True
    )
    misfit = -delay * live
    grad_ref[...] = jnp.zeros_like(grad_ref)
    for at, out, rows in ((2, 0, 8), (0, 8, 2)):
        low = one_hot_half(head[at + 1 : at + 2, :], 128)
        high = one_hot_rows(head[at : at + 1, :], 8)
        values = high * misfit
        if first:
            values = jnp.concatenate([values, high * live], axis=0)
        sums = joined(dot(parts_of(values), low, NT))
        grad_ref[out : out + rows, :] = sums[0:rows, :]
        if first:
            grad_ref[16 + out : 16 + out + rows, :] = sums[8 : 8 + rows, :]


def spread_kernel(own_ref, other_ref, out_ref, rows_ref):
    total = own_ref[...] + other_ref[...]
    rows_ref[...] = jnp.zeros_like(rows_ref)
    rows_ref[0:10, :] = total[0:10, :]
    if total.shape[0] > 16:
        count = total[16:26, :]
        large = jnp.floor(count * (1.0 / 256.0))
        rows_ref[10:20, :] = large
        rows_ref[20:30, :] = count - 256.0 * large
    out_ref[...] = jnp.broadcast_to(rows_ref[...].astype(BF16)[None], out_ref.shape)


def gathered(ref):
    return jnp.sum(ref[...].astype(F32), axis=0)


VMEM = pl.BlockSpec(memory_space=pltpu.VMEM)
HBM = pl.BlockSpec(memory_space=pl.ANY)
SMEM = pl.BlockSpec(memory_space=pltpu.SMEM)
PARAMS = pltpu.CompilerParams(vmem_limit_bytes=40 * 1024 * 1024)


def shape(dims, dtype):
    return jax.ShapeDtypeStruct(dims, dtype)


def call(kernel, out, memory, scratch, name, flops, moved, *args):
    return pl.pallas_call(
        kernel,
        out_shape=out,
        in_specs=[SMEM if space else VMEM for space in memory],
        out_specs=jax.tree.map(lambda _: VMEM, out),
        scratch_shapes=scratch,
        compiler_params=PARAMS,
        cost_estimate=pl.CostEstimate(flops=flops, bytes_accessed=moved, transcendentals=0),
        name=name,
    )(*args)


def pack(traces, *meta):
    scratch = [pltpu.VMEM((1, TR_DEV), jnp.int32)] * 6 + [
        pltpu.VMEM((TR_DEV, NS), BF16),
        pltpu.VMEM((TR_DEV, WIDE), BF16),
        pltpu.VMEM((DEVICES, TRACE_LIMIT, WIDE), BF16),
        pltpu.SemaphoreType.DMA((6,)),
        pltpu.SemaphoreType.DMA((TR_DEV // PACK_ROWS,)),
        pltpu.SemaphoreType.DMA((PACK_OUT,)),
    ]
    return pl.pallas_call(
        pack_kernel,
        out_shape=shape((DEVICES, TRACE_LIMIT, WIDE), BF16),
        in_specs=[HBM] * 7,
        out_specs=HBM,
        scratch_shapes=scratch,
        compiler_params=pltpu.CompilerParams(vmem_limit_bytes=PACK_VMEM),
        name="pack",
    )(*[row.reshape(1, TR_DEV) for row in meta], traces)


PART = shape((BIN_DEV, WIDE), BF16)
SIDE = shape((32, SLOTS), F32)
ROWS = pltpu.VMEM((TAPS * BIN_DEV, WIDE), F32)


def stack_first(weight, slots):
    out = (PART, SIDE, shape((SLOTS, WIDE), BF16))
    return call(first_kernel, out, (1, 0), [ROWS], "stack_first", 3 * 10**9, 10**7, weight, slots)


KNOWN = shape((32, LANES), F32)


def stack_next(weight, index, table, rows, side, sums):
    memory = (1, 1, 1, 0, 0, 0)
    out = (PART, SIDE, KNOWN)
    return call(
        next_kernel, out, memory, [ROWS], "stack_next", 3 * 10**9, 10**7, weight, index, table, rows, side, sums
    )


def finish(index, table, known, sums):
    out = (shape((8, LANES), F32), shape((2, LANES), F32))
    return call(last_kernel, out, (1, 1, 0, 0), [], "finish", 10**4, 10**5, index, table, known, sums)


SHIFTED = (shape((NS, SLOTS), BF16), shape((8, SLOTS), F32))
TURNED = shape((SLOTS // LANES, NS + 16, LANES), F32)


def shift_first(rows, side):
    return call(turn_kernel, (*SHIFTED, TURNED), (0, 0), [], "shift_first", 6 * 10**9, 2 * 10**7, rows, side)


def shift_next(turned, side):
    return call(shift_kernel, SHIFTED, (0, 0), [], "shift_next", 6 * 10**9, 2 * 10**7, turned, side)


def correlate(first, parts, shifted, energy, side):
    out = (shape((BIN_DEV, NS), BF16), shape((32 if first else 16, LANES), F32))
    scratch = [pltpu.VMEM((BIN_DEV * LROWS, NS), BF16), pltpu.VMEM((BIN_DEV, WIDE), F32)]
    kernel = functools.partial(corr_kernel, first)
    return call(kernel, out, (0,) * 7, scratch, "correlate", 4 * 10**9, 10**7, *parts, shifted, energy, side)


def off_perm(d):
    return [(i, (i + d) % 4) for i in range(4)]


def sum_copies(value):
    other = lax.ppermute(value, "core", [(0, 1), (1, 0)])
    out = shape((DEVICES // 2, value.shape[0], LANES), BF16)
    scratch = [pltpu.VMEM(value.shape, F32)]
    copies = call(spread_kernel, out, (0, 0), scratch, "spread", 10**5, 10**6, value, other)
    return lax.all_to_all(copies, ("y", "x", "off"), split_axis=0, concat_axis=0, tiled=True)


def exchange(part):
    return part, *[lax.ppermute(part, "off", off_perm(d)) for d in (1, 2, 3)]


def on_device(
    traces,
    shot_id,
    receiver_id,
    cmp_bin,
    offset_class,
    shift_int,
    frac_index,
    damping_table,
    damping_index,
):
    outgoing = pack(traces, shot_id, receiver_id, cmp_bin, offset_class, shift_int, frac_index)
    slots = lax.all_to_all(outgoing, AXES, split_axis=0, concat_axis=0, tiled=True)
    weight = (1.0 / (1.0 + lax.axis_index("off").astype(F32))).reshape(1, 1)
    part, side, rows = stack_first(weight, slots)
    parts = exchange(part)
    shifted, energy, turned = shift_first(rows, side)
    pilot, sums = correlate(True, parts, shifted, energy, side)
    sums = sum_copies(sums)
    part, side, known = stack_next(weight, damping_index, damping_table, rows, side, sums)
    parts = exchange(part)
    shifted, energy = shift_next(turned, side)
    pilot, sums = correlate(False, parts, shifted, energy, side)
    sums = sum_copies(sums)
    rec, shot = finish(damping_index, damping_table, known, sums)
    return (shot.reshape(-1), rec.reshape(-1), pilot)


def solution(mesh):
    mesh = Mesh(mesh.devices.reshape(4, 4, 2, 4), AXES)
    placed = (P(AXES, None),) + (P(AXES),) * 6 + (P(), P())
    return jax.shard_map(
        on_device, mesh=mesh, in_specs=placed, out_specs=(P(), P(), P(AXES[:3], None)), check_vma=False
    )
```

```python
import functools

import jax
import jax.numpy as jnp
from jax import lax
from jax.experimental import pallas as pl
from jax.experimental.pallas import tpu as pltpu
from jax.sharding import Mesh
from jax.sharding import PartitionSpec as P

NS = 2048
LAGS = 101
HALF = LAGS // 2
TAPS = 16
NPHASE = 32
SHIFT_MAX = 8
CLASSES = 4
TRACE_LIMIT = 4
BIN_DEV = 16
TR_DEV = 256
DEVICES = 128
SLOTS = DEVICES * TRACE_LIMIT
LANES = 128
WIDE = NS + LANES
LROWS = 112
LAG_TOP = 106
BINS_STEP = 4
PACK_ROWS = 64
PACK_OUT = 4
PACK_VMEM = 63 * 1024 * 1024
BETA = 24.0
EPS = 1e-06
F32 = jnp.float32
BF16 = jnp.bfloat16
HEAD = 16
AXES = ("y", "x", "core", "off")

NN = (((1,), (0,)), ((), ()))
NT = (((1,), (1,)), ((), ()))
TN = (((0,), (0,)), ((), ()))


def dot(a, b, dims, precision=None):
    return lax.dot_general(a, b, dims, precision=precision, preferred_element_type=F32)


def iota(shape, axis):
    return lax.broadcasted_iota(jnp.int32, shape, axis)


def pack_kernel(*refs):
    meta_in, x_in, out_ref = refs[:6], refs[6], refs[7]
    meta_refs, (x_ref, y_ref, o_ref, meta_sem, x_sem, o_sem) = refs[8:14], refs[14:]
    parts = TR_DEV // PACK_ROWS
    x_copies = [
        pltpu.make_async_copy(
            x_in.at[pl.ds(i * PACK_ROWS, PACK_ROWS), :], x_ref.at[pl.ds(i * PACK_ROWS, PACK_ROWS), :], x_sem.at[i]
        )
        for i in range(parts)
    ]
    meta_copies = [pltpu.make_async_copy(meta_in[i], meta_refs[i], meta_sem.at[i]) for i in range(6)]
    for copy in meta_copies + x_copies:
        copy.start()
    for copy in meta_copies:
        copy.wait()
    shot, rec, bin_, cls, whole, frac = [ref[...] for ref in meta_refs]
    dest = (bin_ // BIN_DEV) * CLASSES + cls
    rows = [
        shot // 128,
        shot % 128,
        rec // 128,
        rec % 128,
        bin_ % BIN_DEV,
        frac,
        jnp.ones_like(shot),
        whole + SHIFT_MAX,
        dest,
    ]
    sub = iota((16, TR_DEV), 0)
    info = jnp.zeros((16, TR_DEV), F32)
    for i, row in enumerate(rows):
        info = jnp.where(sub == i, row.astype(F32), info)
    place = (iota((16, LANES), 1) == iota((16, LANES), 0) + HEAD).astype(F32).astype(BF16)
    cols = dot(info.astype(BF16), place, TN)
    amount = cols[:, HEAD + 7 : HEAD + 8].astype(jnp.int32)
    dest_col = cols[:, HEAD + 8 : HEAD + 9]
    same = (dest_col == dest.astype(F32)) & (iota((TR_DEV, TR_DEV), 0) < iota((TR_DEV, TR_DEV), 1))
    rank = jnp.sum(jnp.where(same, 1.0, 0.0), axis=0, keepdims=True).astype(jnp.int32)
    slot = dest * TRACE_LIMIT + rank
    onehot = (iota((SLOTS, TR_DEV), 0) == slot).astype(F32).astype(BF16)
    amount = amount - SHIFT_MAX
    tail = cols.astype(BF16)
    step = 32
    lane = iota((step, LANES), 1)
    blocks = WIDE // LANES
    for r in range(0, TR_DEV, step):
        if r % PACK_ROWS == 0:
            x_copies[r // PACK_ROWS].wait()
        source = lane + amount[r : r + step, :]
        index = source & (LANES - 1)
        turned = [
            jnp.take_along_axis(
                x_ref[r : r + step, c * LANES : (c + 1) * LANES].astype(F32), index, axis=1, mode="promise_in_bounds"
            )
            for c in range(blocks - 1)
        ] + [jnp.zeros((step, LANES), F32)]
        for c in range(blocks):
            before, after = turned[c - 1], turned[(c + 1) % blocks]
            y = jnp.where(source < 0, before, jnp.where(source >= LANES, after, turned[c])).astype(BF16)
            if c == blocks - 1:
                y = y + tail[r : r + step, :]
            y_ref[r : r + step, c * LANES : (c + 1) * LANES] = y
    out_copies = []
    group = DEVICES // PACK_OUT
    for i in range(PACK_OUT):
        rows = onehot[i * group * TRACE_LIMIT : (i + 1) * group * TRACE_LIMIT, :]
        placed = dot(rows, y_ref[...], NN).reshape(group, TRACE_LIMIT, WIDE).astype(BF16)
        o_ref[i * group : (i + 1) * group] = placed
        copy = pltpu.make_async_copy(
            o_ref.at[pl.ds(i * group, group)], out_ref.at[pl.ds(i * group, group)], o_sem.at[i]
        )
        copy.start()
        out_copies.append(copy)
    for copy in out_copies:
        copy.wait()


def one_hot_rows(row, count):
    return (iota((count, SLOTS), 0) == row.astype(jnp.int32)).astype(F32)


def one_hot_half(row, count):
    return one_hot_rows(row, count).astype(BF16)


def parts_of(value):
    top = value.astype(BF16)
    rest = value - top.astype(F32)
    middle = rest.astype(BF16)
    return jnp.concatenate([top, middle, (rest - middle.astype(F32)).astype(BF16)], axis=0)


def joined(sums):
    rows = sums.shape[0] // 3
    return (sums[0:rows, :] + sums[rows : 2 * rows, :]) + sums[2 * rows :, :]


def unit(size):
    return (iota((size, size), 0) == iota((size, size), 1)).astype(F32).astype(BF16)


def stack_rows(y_ref, head, frac, side_ref, part_ref, sum_ref):
    live = head[6:7, :]
    u = (iota((TAPS, SLOTS), 0) - (TAPS // 2 - 1)).astype(F32) - frac
    angle = jnp.pi * u
    safe = jnp.where(u == 0.0, 1.0, angle)
    sinc = jnp.where(u == 0.0, 1.0, jnp.sin(safe) / safe)
    taps = sinc * (0.5 + 0.5 * jnp.cos(angle * (1.0 / (TAPS // 2))))
    side_ref[0:16, :] = head
    side_ref[16:32, :] = taps
    owner = head[8:9, :]
    offset = owner - CLASSES * jnp.floor(owner * (1.0 / CLASSES))
    member = one_hot_rows(head[4:5, :], BIN_DEV) * (live / (1.0 + offset))
    rows = [member * taps[k : k + 1, :] for k in range(TAPS)]
    high = [row.astype(BF16) for row in rows]
    low = [(row - top.astype(F32)).astype(BF16) for row, top in zip(rows, high)]
    slots = y_ref[...]
    sum_ref[...] = dot(jnp.concatenate(high, axis=0), slots, NN) + dot(jnp.concatenate(low, axis=0), slots, NN)
    total = jnp.zeros((BIN_DEV, WIDE), F32)
    for k in range(TAPS):
        total = total + pltpu.roll(sum_ref[k * BIN_DEV : (k + 1) * BIN_DEV, :], (TAPS // 2 - 1 - k) % WIDE, 1)
    part_ref[:, :NS] = total[:, :NS].astype(BF16)
    mass = jnp.sum(member, axis=1, keepdims=True)
    m0 = mass.astype(BF16).astype(F32)
    m1 = (mass - m0).astype(BF16).astype(F32)
    m2 = mass - m0 - m1
    lane = iota((BIN_DEV, LANES), 1)
    tail = jnp.where(lane == 0, m0, jnp.where(lane == 1, m1, jnp.where(lane == 2, m2, 0.0)))
    part_ref[:, NS:] = tail.astype(BF16)


def first_kernel(slots_ref, part_ref, side_ref, y_ref, sum_ref):
    y_ref[...] = slots_ref[...].reshape(SLOTS, WIDE)
    head = dot(unit(LANES), y_ref[:, NS:], NT)[HEAD : HEAD + 16, :]
    stack_rows(y_ref, head, head[5:6, :] * (1.0 / NPHASE), side_ref, part_ref, sum_ref)


def next_kernel(damp_ref, y_ref, head_ref, sums_ref, part_ref, side_ref, known_ref, sum_ref):
    damp = damp_ref[0:1, :]
    sums = gathered(sums_ref)
    count = sums[10:20, :]
    known_ref[...] = jnp.zeros_like(known_ref)
    known_ref[0:10, :] = sums[0:10, :] / ((1.0 + damp) * count + damp)
    known_ref[16:26, :] = count
    head = head_ref[0:16, :]
    frac = head[5:6, :] * (1.0 / NPHASE)
    for base, at in ((8, 0), (0, 2)):
        low = one_hot_half(head[at + 1 : at + 2, :], 128)
        high = one_hot_rows(head[at : at + 1, :], 8)
        found = joined(dot(parts_of(known_ref[base : base + 8, :]), low, NN))
        frac = frac + jnp.sum(found * high, axis=0, keepdims=True)
    stack_rows(y_ref, head, frac, side_ref, part_ref, sum_ref)


def last_kernel(damp_ref, known_ref, sums_ref, rec_ref, shot_ref):
    damp = damp_ref[8:9, :]
    step = gathered(sums_ref) / ((1.0 + damp) * known_ref[16:32, :] + damp)
    total = known_ref[0:16, :] + step
    rec_ref[...] = total[0:8, :]
    shot_ref[...] = total[8:10, :]


def turn_kernel(y_ref, side_ref, st_ref, energy_ref, xt_ref):
    eye = unit(LANES)
    groups = SLOTS // LANES
    for c in range(NS // LANES):
        block = dot(eye, y_ref[:, c * LANES : (c + 1) * LANES], NT)
        for q in range(groups):
            xt_ref[q, 8 + c * LANES : 8 + (c + 1) * LANES, :] = block[:, q * LANES : (q + 1) * LANES]
    block = dot(eye, y_ref[:, NS:], NT)
    for q in range(groups):
        part = block[:, q * LANES : (q + 1) * LANES]
        xt_ref[q, 0:8, :] = part[120:128, :]
        xt_ref[q, 8 + NS : 16 + NS, :] = part[0:8, :]
    shift_kernel(xt_ref, side_ref, st_ref, energy_ref)


def shift_kernel(xt_ref, side_ref, st_ref, energy_ref):
    groups = SLOTS // LANES
    chunk = 32
    energies = []
    for q in range(groups):
        tap = [
            jnp.broadcast_to(side_ref[16 + k : 17 + k, q * LANES : (q + 1) * LANES], (8, LANES)) for k in range(TAPS)
        ]

        def body(i, energy):
            base = pl.multiple_of(i * chunk, chunk)
            totals = [None] * (chunk // 8)
            for p in range(chunk + TAPS - 8):
                window = xt_ref[q, pl.ds(base + 1 + p, 8), :]
                for h in range(chunk // 8):
                    k = p - 8 * h
                    if 0 <= k < TAPS:
                        term = tap[k] * window
                        totals[h] = term if totals[h] is None else totals[h] + term
            for h in range(0, chunk // 8, 2):
                rounded = jnp.concatenate(totals[h : h + 2], axis=0).astype(BF16)
                st_ref[pl.ds(base + 8 * h, 16), q * LANES : (q + 1) * LANES] = rounded
                energy = energy + (totals[h] * totals[h] + totals[h + 1] * totals[h + 1])
            return energy

        energy = lax.fori_loop(0, NS // chunk, body, jnp.zeros((8, LANES), F32), unroll=4)
        energies.append(jnp.sum(energy, axis=0, keepdims=True))
    energy_ref[...] = jnp.broadcast_to(jnp.concatenate(energies, axis=1), (8, SLOTS))


def corr_kernel(first, p0_ref, p1_ref, p2_ref, p3_ref, st_ref, energy_ref, side_ref, pilot_ref, grad_ref, lag_ref, wide_ref):
    total = (p0_ref[...].astype(F32) + p2_ref[...].astype(F32)) + (
        p1_ref[...].astype(F32) + p3_ref[...].astype(F32)
    )
    mass = (total[:, NS : NS + 1] + total[:, NS + 1 : NS + 2]) + total[:, NS + 2 : NS + 3]
    pilot = (total[:, :NS] * lax.rsqrt(mass + 1.0)).astype(BF16)
    pilot_ref[...] = pilot
    wide = pilot.astype(F32)
    wide_ref[:, :NS] = wide
    wide_ref[:, NS:] = jnp.zeros((BIN_DEV, LANES), F32)
    pilot_scale = lax.rsqrt(jnp.sum(wide * wide, axis=1, keepdims=True) + EPS)
    head = side_ref[0:16, :]
    live = head[6:7, :]
    member = one_hot_rows(head[4:5, :], BIN_DEV) * live
    corr = jnp.zeros((LROWS, SLOTS), F32)
    for b0 in range(0, BIN_DEV, BINS_STEP):
        for bb in range(BINS_STEP):
            row = jnp.broadcast_to(wide_ref[b0 + bb : b0 + bb + 1, :], (8, WIDE))
            for g in range(0, LROWS, 16):
                two = [
                    pltpu.roll(row, (WIDE - (LAG_TOP - HALF) + g + h) % WIDE, 1, stride=1, stride_axis=0)[:, :NS]
                    for h in (0, 8)
                ]
                at = (b0 + bb) * LROWS + g
                lag_ref[at : at + 16, :] = jnp.concatenate(two, axis=0).astype(BF16)
        every = dot(lag_ref[b0 * LROWS : (b0 + BINS_STEP) * LROWS, :], st_ref[...], NN)
        for bb in range(BINS_STEP):
            corr = corr + member[b0 + bb : b0 + bb + 1, :] * every[bb * LROWS : (bb + 1) * LROWS, :]
    scale = lax.rsqrt(energy_ref[0:1, :] + EPS) * jnp.sum(member * pilot_scale, axis=0, keepdims=True)
    lag = LAG_TOP - iota((LROWS, SLOTS), 0)
    exponent = jnp.where((lag >= 0) & (lag < LAGS), jnp.exp(BETA * (corr * scale)), 0.0)
    delay = jnp.sum(exponent * (lag - HALF).astype(F32), axis=0, keepdims=True) / jnp.sum(
        exponent, axis=0, keepdims=True
    )
    misfit = -delay * live
    grad_ref[...] = jnp.zeros_like(grad_ref)
    for at, out, rows in ((2, 0, 8), (0, 8, 2)):
        low = one_hot_half(head[at + 1 : at + 2, :], 128)
        high = one_hot_rows(head[at : at + 1, :], 8)
        values = high * misfit
        if first:
            values = jnp.concatenate([values, high * live], axis=0)
        sums = joined(dot(parts_of(values), low, NT))
        grad_ref[out : out + rows, :] = sums[0:rows, :]
        if first:
            grad_ref[16 + out : 16 + out + rows, :] = sums[8 : 8 + rows, :]


def spread_kernel(own_ref, other_ref, out_ref, rows_ref):
    total = own_ref[...] + other_ref[...]
    rows_ref[...] = jnp.zeros_like(rows_ref)
    rows_ref[0:10, :] = total[0:10, :]
    if total.shape[0] > 16:
        rows_ref[10:20, :] = total[16:26, :]
    out_ref[...] = jnp.broadcast_to(rows_ref[...].astype(BF16)[None], out_ref.shape)


def gathered(ref):
    return jnp.sum(ref[...].astype(F32), axis=0)


VMEM = pl.BlockSpec(memory_space=pltpu.VMEM)
HBM = pl.BlockSpec(memory_space=pl.ANY)
SMEM = pl.BlockSpec(memory_space=pltpu.SMEM)
PARAMS = pltpu.CompilerParams(vmem_limit_bytes=40 * 1024 * 1024)


def shape(dims, dtype):
    return jax.ShapeDtypeStruct(dims, dtype)


def call(kernel, out, memory, scratch, name, flops, moved, *args):
    return pl.pallas_call(
        kernel,
        out_shape=out,
        in_specs=[SMEM if space else VMEM for space in memory],
        out_specs=jax.tree.map(lambda _: VMEM, out),
        scratch_shapes=scratch,
        compiler_params=PARAMS,
        cost_estimate=pl.CostEstimate(flops=flops, bytes_accessed=moved, transcendentals=0),
        name=name,
    )(*args)


def pack(traces, *meta):
    scratch = [pltpu.VMEM((1, TR_DEV), jnp.int32)] * 6 + [
        pltpu.VMEM((TR_DEV, NS), BF16),
        pltpu.VMEM((TR_DEV, WIDE), BF16),
        pltpu.VMEM((DEVICES, TRACE_LIMIT, WIDE), BF16),
        pltpu.SemaphoreType.DMA((6,)),
        pltpu.SemaphoreType.DMA((TR_DEV // PACK_ROWS,)),
        pltpu.SemaphoreType.DMA((PACK_OUT,)),
    ]
    return pl.pallas_call(
        pack_kernel,
        out_shape=shape((DEVICES, TRACE_LIMIT, WIDE), BF16),
        in_specs=[HBM] * 7,
        out_specs=HBM,
        scratch_shapes=scratch,
        compiler_params=pltpu.CompilerParams(vmem_limit_bytes=PACK_VMEM),
        name="pack",
    )(*[row.reshape(1, TR_DEV) for row in meta], traces)


PART = shape((BIN_DEV, WIDE), BF16)
SIDE = shape((32, SLOTS), F32)
ROWS = pltpu.VMEM((TAPS * BIN_DEV, WIDE), F32)


def stack_first(slots):
    out = (PART, SIDE, shape((SLOTS, WIDE), BF16))
    return call(first_kernel, out, (0,), [ROWS], "stack_first", 3 * 10**9, 10**7, slots)


KNOWN = shape((32, LANES), F32)


def stack_next(damps, rows, side, sums):
    out = (PART, SIDE, KNOWN)
    return call(next_kernel, out, (0,) * 4, [ROWS], "stack_next", 3 * 10**9, 10**7, damps, rows, side, sums)


def finish(damps, known, sums):
    out = (shape((8, LANES), F32), shape((2, LANES), F32))
    return call(last_kernel, out, (0,) * 3, [], "finish", 10**4, 10**5, damps, known, sums)


SHIFTED = (shape((NS, SLOTS), BF16), shape((8, SLOTS), F32))
TURNED = shape((SLOTS // LANES, NS + 16, LANES), F32)


def shift_first(rows, side):
    return call(turn_kernel, (*SHIFTED, TURNED), (0, 0), [], "shift_first", 6 * 10**9, 2 * 10**7, rows, side)


def shift_next(turned, side):
    return call(shift_kernel, SHIFTED, (0, 0), [], "shift_next", 6 * 10**9, 2 * 10**7, turned, side)


def correlate(first, parts, shifted, energy, side):
    out = (shape((BIN_DEV, NS), BF16), shape((32 if first else 16, LANES), F32))
    scratch = [pltpu.VMEM((BIN_DEV * LROWS, NS), BF16), pltpu.VMEM((BIN_DEV, WIDE), F32)]
    kernel = functools.partial(corr_kernel, first)
    return call(kernel, out, (0,) * 7, scratch, "correlate", 4 * 10**9, 10**7, *parts, shifted, energy, side)


def off_perm(d):
    return [(i, (i + d) % 4) for i in range(4)]


def sum_copies(value):
    other = lax.ppermute(value, "core", [(0, 1), (1, 0)])
    rows = 16 if value.shape[0] == 16 else 24
    out = shape((DEVICES // 2, rows, LANES), BF16)
    scratch = [pltpu.VMEM((rows, LANES), F32)]
    copies = call(spread_kernel, out, (0, 0), scratch, "spread", 10**5, 10**6, value, other)
    return lax.all_to_all(copies, ("y", "x", "off"), split_axis=0, concat_axis=0, tiled=True)


def exchange(part):
    return part, *[lax.ppermute(part, "off", off_perm(d)) for d in (1, 2, 3)]


def on_device(
    traces,
    shot_id,
    receiver_id,
    cmp_bin,
    offset_class,
    shift_int,
    frac_index,
    damping_table,
    damping_index,
):
    outgoing = pack(traces, shot_id, receiver_id, cmp_bin, offset_class, shift_int, frac_index)
    slots = lax.all_to_all(outgoing, AXES, split_axis=0, concat_axis=0, tiled=True)
    entries = jnp.arange(damping_table.shape[0], dtype=jnp.int32)
    chosen = jnp.sum(jnp.where(entries == damping_index[:, None], damping_table, 0.0), axis=1)
    damps = jnp.broadcast_to(chosen[:, None, None], (2, 8, LANES)).reshape(16, LANES)
    part, side, rows = stack_first(slots)
    parts = exchange(part)
    shifted, energy, turned = shift_first(rows, side)
    pilot, sums = correlate(True, parts, shifted, energy, side)
    sums = sum_copies(sums)
    part, side, known = stack_next(damps, rows, side, sums)
    parts = exchange(part)
    shifted, energy = shift_next(turned, side)
    pilot, sums = correlate(False, parts, shifted, energy, side)
    sums = sum_copies(sums)
    rec, shot = finish(damps, known, sums)
    return (shot.reshape(-1), rec.reshape(-1), pilot)


def solution(mesh):
    mesh = Mesh(mesh.devices.reshape(4, 4, 2, 4), AXES)
    placed = (P(AXES, None),) + (P(AXES),) * 6 + (P(), P())
    return jax.shard_map(
        on_device, mesh=mesh, in_specs=placed, out_specs=(P(), P(), P(AXES[:3], None)), check_vma=False
    )
```

```python
import functools

import jax
import jax.numpy as jnp
from jax import lax
from jax.experimental import pallas as pl
from jax.experimental.pallas import tpu as pltpu
from jax.sharding import Mesh
from jax.sharding import PartitionSpec as P

NS = 2048
LAGS = 101
HALF = LAGS // 2
TAPS = 16
NPHASE = 32
SHIFT_MAX = 8
CLASSES = 4
TRACE_LIMIT = 4
BIN_DEV = 16
TR_DEV = 256
DEVICES = 128
SLOTS = DEVICES * TRACE_LIMIT
LANES = 128
WIDE = NS + LANES
LROWS = 104
LAG_TOP = 102
LAG_PAD = 4
BINS_STEP = 4
PACK_ROWS = 64
PACK_OUT = 4
PACK_VMEM = 63 * 1024 * 1024
BETA = 24.0
EPS = 1e-06
F32 = jnp.float32
BF16 = jnp.bfloat16
HEAD = 16
AXES = ("y", "x", "core", "off")

NN = (((1,), (0,)), ((), ()))
NT = (((1,), (1,)), ((), ()))
TN = (((0,), (0,)), ((), ()))


def dot(a, b, dims, precision=None):
    return lax.dot_general(a, b, dims, precision=precision, preferred_element_type=F32)


def iota(shape, axis):
    return lax.broadcasted_iota(jnp.int32, shape, axis)


def pack_kernel(*refs):
    meta_in, x_in, out_ref = refs[:6], refs[6], refs[7]
    meta_refs, (x_ref, y_ref, o_ref, meta_sem, x_sem, o_sem) = refs[8:14], refs[14:]
    parts = TR_DEV // PACK_ROWS
    x_copies = [
        pltpu.make_async_copy(
            x_in.at[pl.ds(i * PACK_ROWS, PACK_ROWS), :], x_ref.at[pl.ds(i * PACK_ROWS, PACK_ROWS), :], x_sem.at[i]
        )
        for i in range(parts)
    ]
    meta_copies = [pltpu.make_async_copy(meta_in[i], meta_refs[i], meta_sem.at[i]) for i in range(6)]
    for copy in meta_copies + x_copies:
        copy.start()
    for copy in meta_copies:
        copy.wait()
    shot, rec, bin_, cls, whole, frac = [ref[...] for ref in meta_refs]
    dest = (bin_ // BIN_DEV) * CLASSES + cls
    rows = [
        shot // 128,
        shot % 128,
        rec // 128,
        rec % 128,
        bin_ % BIN_DEV,
        frac,
        jnp.ones_like(shot),
        whole + SHIFT_MAX,
        dest,
    ]
    sub = iota((16, TR_DEV), 0)
    info = jnp.zeros((16, TR_DEV), F32)
    for i, row in enumerate(rows):
        info = jnp.where(sub == i, row.astype(F32), info)
    place = (iota((16, LANES), 1) == iota((16, LANES), 0) + HEAD).astype(F32).astype(BF16)
    cols = dot(info.astype(BF16), place, TN)
    amount = cols[:, HEAD + 7 : HEAD + 8].astype(jnp.int32)
    dest_col = cols[:, HEAD + 8 : HEAD + 9]
    same = (dest_col == dest.astype(F32)) & (iota((TR_DEV, TR_DEV), 0) < iota((TR_DEV, TR_DEV), 1))
    rank = jnp.sum(jnp.where(same, 1.0, 0.0), axis=0, keepdims=True).astype(jnp.int32)
    slot = dest * TRACE_LIMIT + rank
    onehot = (iota((SLOTS, TR_DEV), 0) == slot).astype(F32).astype(BF16)
    amount = amount - SHIFT_MAX
    tail = cols.astype(BF16)
    step = 32
    lane = iota((step, LANES), 1)
    blocks = WIDE // LANES
    for r in range(0, TR_DEV, step):
        if r % PACK_ROWS == 0:
            x_copies[r // PACK_ROWS].wait()
        source = lane + amount[r : r + step, :]
        index = source & (LANES - 1)
        turned = [
            jnp.take_along_axis(
                x_ref[r : r + step, c * LANES : (c + 1) * LANES].astype(F32), index, axis=1, mode="promise_in_bounds"
            )
            for c in range(blocks - 1)
        ] + [jnp.zeros((step, LANES), F32)]
        for c in range(blocks):
            before, after = turned[c - 1], turned[(c + 1) % blocks]
            y = jnp.where(source < 0, before, jnp.where(source >= LANES, after, turned[c])).astype(BF16)
            if c == blocks - 1:
                y = y + tail[r : r + step, :]
            y_ref[r : r + step, c * LANES : (c + 1) * LANES] = y
    out_copies = []
    group = DEVICES // PACK_OUT
    for i in range(PACK_OUT):
        rows = onehot[i * group * TRACE_LIMIT : (i + 1) * group * TRACE_LIMIT, :]
        placed = dot(rows, y_ref[...], NN).reshape(group, TRACE_LIMIT, WIDE).astype(BF16)
        o_ref[i * group : (i + 1) * group] = placed
        copy = pltpu.make_async_copy(
            o_ref.at[pl.ds(i * group, group)], out_ref.at[pl.ds(i * group, group)], o_sem.at[i]
        )
        copy.start()
        out_copies.append(copy)
    for copy in out_copies:
        copy.wait()


def one_hot_rows(row, count):
    return (iota((count, SLOTS), 0) == row.astype(jnp.int32)).astype(F32)


def one_hot_half(row, count):
    return one_hot_rows(row, count).astype(BF16)


def parts_of(value):
    top = value.astype(BF16)
    rest = value - top.astype(F32)
    middle = rest.astype(BF16)
    return jnp.concatenate([top, middle, (rest - middle.astype(F32)).astype(BF16)], axis=0)


def joined(sums):
    rows = sums.shape[0] // 3
    return (sums[0:rows, :] + sums[rows : 2 * rows, :]) + sums[2 * rows :, :]


def unit(size):
    return (iota((size, size), 0) == iota((size, size), 1)).astype(F32).astype(BF16)


def stack_rows(y_ref, head, frac, side_ref, part_ref, sum_ref):
    live = head[6:7, :]
    u = (iota((TAPS, SLOTS), 0) - (TAPS // 2 - 1)).astype(F32) - frac
    angle = jnp.pi * u
    safe = jnp.where(u == 0.0, 1.0, angle)
    sinc = jnp.where(u == 0.0, 1.0, jnp.sin(safe) / safe)
    taps = sinc * (0.5 + 0.5 * jnp.cos(angle * (1.0 / (TAPS // 2))))
    side_ref[0:16, :] = head
    side_ref[16:32, :] = taps
    owner = head[8:9, :]
    offset = owner - CLASSES * jnp.floor(owner * (1.0 / CLASSES))
    member = one_hot_rows(head[4:5, :], BIN_DEV) * (live / (1.0 + offset))
    rows = [member * taps[k : k + 1, :] for k in range(TAPS)]
    high = [row.astype(BF16) for row in rows]
    low = [(row - top.astype(F32)).astype(BF16) for row, top in zip(rows, high)]
    slots = y_ref[...]
    sum_ref[...] = dot(jnp.concatenate(high, axis=0), slots, NN) + dot(jnp.concatenate(low, axis=0), slots, NN)
    total = jnp.zeros((BIN_DEV, WIDE), F32)
    for k in range(TAPS):
        total = total + pltpu.roll(sum_ref[k * BIN_DEV : (k + 1) * BIN_DEV, :], (TAPS // 2 - 1 - k) % WIDE, 1)
    part_ref[:, :NS] = total[:, :NS].astype(BF16)
    mass = jnp.sum(member, axis=1, keepdims=True)
    m0 = mass.astype(BF16).astype(F32)
    m1 = (mass - m0).astype(BF16).astype(F32)
    m2 = mass - m0 - m1
    lane = iota((BIN_DEV, LANES), 1)
    tail = jnp.where(lane == 0, m0, jnp.where(lane == 1, m1, jnp.where(lane == 2, m2, 0.0)))
    part_ref[:, NS:] = tail.astype(BF16)


def first_kernel(slots_ref, part_ref, side_ref, y_ref, sum_ref):
    y_ref[...] = slots_ref[...].reshape(SLOTS, WIDE)
    head = dot(unit(LANES), y_ref[:, NS:], NT)[HEAD : HEAD + 16, :]
    stack_rows(y_ref, head, head[5:6, :] * (1.0 / NPHASE), side_ref, part_ref, sum_ref)


def next_kernel(damp_ref, y_ref, head_ref, sums_ref, part_ref, side_ref, known_ref, sum_ref):
    damp = damp_ref[0:1, :]
    sums = gathered(sums_ref)
    count = sums[10:20, :]
    known_ref[...] = jnp.zeros_like(known_ref)
    known_ref[0:10, :] = sums[0:10, :] / ((1.0 + damp) * count + damp)
    known_ref[16:26, :] = count
    head = head_ref[0:16, :]
    frac = head[5:6, :] * (1.0 / NPHASE)
    for base, at in ((8, 0), (0, 2)):
        low = one_hot_half(head[at + 1 : at + 2, :], 128)
        high = one_hot_rows(head[at : at + 1, :], 8)
        found = joined(dot(parts_of(known_ref[base : base + 8, :]), low, NN))
        frac = frac + jnp.sum(found * high, axis=0, keepdims=True)
    stack_rows(y_ref, head, frac, side_ref, part_ref, sum_ref)


def last_kernel(damp_ref, known_ref, sums_ref, rec_ref, shot_ref):
    damp = damp_ref[8:9, :]
    step = gathered(sums_ref) / ((1.0 + damp) * known_ref[16:32, :] + damp)
    total = known_ref[0:16, :] + step
    rec_ref[...] = total[0:8, :]
    shot_ref[...] = total[8:10, :]


def turn_kernel(y_ref, side_ref, st_ref, energy_ref, xt_ref):
    eye = unit(LANES)
    groups = SLOTS // LANES
    for c in range(NS // LANES):
        block = dot(eye, y_ref[:, c * LANES : (c + 1) * LANES], NT)
        for q in range(groups):
            xt_ref[q, 8 + c * LANES : 8 + (c + 1) * LANES, :] = block[:, q * LANES : (q + 1) * LANES]
    block = dot(eye, y_ref[:, NS:], NT)
    for q in range(groups):
        part = block[:, q * LANES : (q + 1) * LANES]
        xt_ref[q, 0:8, :] = part[120:128, :]
        xt_ref[q, 8 + NS : 16 + NS, :] = part[0:8, :]
    shift_kernel(xt_ref, side_ref, st_ref, energy_ref)


def shift_kernel(xt_ref, side_ref, st_ref, energy_ref):
    groups = SLOTS // LANES
    chunk = 32
    energies = []
    for q in range(groups):
        tap = [
            jnp.broadcast_to(side_ref[16 + k : 17 + k, q * LANES : (q + 1) * LANES], (8, LANES)) for k in range(TAPS)
        ]

        def body(i, energy):
            base = pl.multiple_of(i * chunk, chunk)
            totals = [None] * (chunk // 8)
            for p in range(chunk + TAPS - 8):
                window = xt_ref[q, pl.ds(base + 1 + p, 8), :]
                for h in range(chunk // 8):
                    k = p - 8 * h
                    if 0 <= k < TAPS:
                        term = tap[k] * window
                        totals[h] = term if totals[h] is None else totals[h] + term
            for h in range(0, chunk // 8, 2):
                rounded = jnp.concatenate(totals[h : h + 2], axis=0).astype(BF16)
                st_ref[pl.ds(base + 8 * h, 16), q * LANES : (q + 1) * LANES] = rounded
                energy = energy + (totals[h] * totals[h] + totals[h + 1] * totals[h + 1])
            return energy

        energy = lax.fori_loop(0, NS // chunk, body, jnp.zeros((8, LANES), F32), unroll=4)
        energies.append(jnp.sum(energy, axis=0, keepdims=True))
    energy_ref[...] = jnp.broadcast_to(jnp.concatenate(energies, axis=1), (8, SLOTS))


def corr_kernel(first, p0_ref, p1_ref, p2_ref, p3_ref, st_ref, energy_ref, side_ref, pilot_ref, grad_ref, lag_ref, wide_ref):
    total = (p0_ref[...].astype(F32) + p2_ref[...].astype(F32)) + (
        p1_ref[...].astype(F32) + p3_ref[...].astype(F32)
    )
    mass = (total[:, NS : NS + 1] + total[:, NS + 1 : NS + 2]) + total[:, NS + 2 : NS + 3]
    pilot = (total[:, :NS] * lax.rsqrt(mass + 1.0)).astype(BF16)
    pilot_ref[...] = pilot
    wide = pilot.astype(F32)
    wide_ref[...] = pltpu.roll(jnp.concatenate([wide, jnp.zeros((BIN_DEV, LANES), F32)], axis=1), LAG_PAD, 1)
    pilot_scale = lax.rsqrt(jnp.sum(wide * wide, axis=1, keepdims=True) + EPS)
    head = side_ref[0:16, :]
    live = head[6:7, :]
    member = one_hot_rows(head[4:5, :], BIN_DEV) * live
    corr = jnp.zeros((LROWS, SLOTS), F32)
    for b0 in range(0, BIN_DEV, BINS_STEP):
        for bb in range(0, BINS_STEP, 2):
            eights = []
            for b in (b0 + bb, b0 + bb + 1):
                row = jnp.broadcast_to(wide_ref[b : b + 1, :], (8, WIDE))
                for g in range(0, LROWS, 8):
                    amount = (WIDE - (LAG_TOP - HALF) - LAG_PAD + g) % WIDE
                    eights.append(pltpu.roll(row, amount, 1, stride=1, stride_axis=0)[:, :NS])
                    if len(eights) % 2 == 0:
                        at = (b0 + bb) * LROWS + 8 * (len(eights) - 2)
                        lag_ref[at : at + 16, :] = jnp.concatenate(eights[-2:], axis=0).astype(BF16)
        every = dot(lag_ref[b0 * LROWS : (b0 + BINS_STEP) * LROWS, :], st_ref[...], NN)
        for bb in range(BINS_STEP):
            corr = corr + member[b0 + bb : b0 + bb + 1, :] * every[bb * LROWS : (bb + 1) * LROWS, :]
    scale = lax.rsqrt(energy_ref[0:1, :] + EPS) * jnp.sum(member * pilot_scale, axis=0, keepdims=True)
    lag = LAG_TOP - iota((LROWS, SLOTS), 0)
    exponent = jnp.where((lag >= 0) & (lag < LAGS), jnp.exp(BETA * (corr * scale)), 0.0)
    delay = jnp.sum(exponent * (lag - HALF).astype(F32), axis=0, keepdims=True) / jnp.sum(
        exponent, axis=0, keepdims=True
    )
    misfit = -delay * live
    grad_ref[...] = jnp.zeros_like(grad_ref)
    for at, out, rows in ((2, 0, 8), (0, 8, 2)):
        low = one_hot_half(head[at + 1 : at + 2, :], 128)
        high = one_hot_rows(head[at : at + 1, :], 8)
        values = high * misfit
        if first:
            values = jnp.concatenate([values, high * live], axis=0)
        sums = joined(dot(parts_of(values), low, NT))
        grad_ref[out : out + rows, :] = sums[0:rows, :]
        if first:
            grad_ref[16 + out : 16 + out + rows, :] = sums[8 : 8 + rows, :]


def spread_kernel(own_ref, other_ref, out_ref, rows_ref):
    total = own_ref[...] + other_ref[...]
    rows_ref[...] = jnp.zeros_like(rows_ref)
    rows_ref[0:10, :] = total[0:10, :]
    if total.shape[0] > 16:
        rows_ref[10:20, :] = total[16:26, :]
    out_ref[...] = jnp.broadcast_to(rows_ref[...].astype(BF16)[None], out_ref.shape)


def gathered(ref):
    return jnp.sum(ref[...].astype(F32), axis=0)


VMEM = pl.BlockSpec(memory_space=pltpu.VMEM)
HBM = pl.BlockSpec(memory_space=pl.ANY)
SMEM = pl.BlockSpec(memory_space=pltpu.SMEM)
PARAMS = pltpu.CompilerParams(vmem_limit_bytes=24 * 1024 * 1024)


def shape(dims, dtype):
    return jax.ShapeDtypeStruct(dims, dtype)


def call(kernel, out, memory, scratch, name, flops, moved, *args):
    return pl.pallas_call(
        kernel,
        out_shape=out,
        in_specs=[SMEM if space else VMEM for space in memory],
        out_specs=jax.tree.map(lambda _: VMEM, out),
        scratch_shapes=scratch,
        compiler_params=PARAMS,
        cost_estimate=pl.CostEstimate(flops=flops, bytes_accessed=moved, transcendentals=0),
        name=name,
    )(*args)


def pack(traces, *meta):
    scratch = [pltpu.VMEM((1, TR_DEV), jnp.int32)] * 6 + [
        pltpu.VMEM((TR_DEV, NS), BF16),
        pltpu.VMEM((TR_DEV, WIDE), BF16),
        pltpu.VMEM((DEVICES, TRACE_LIMIT, WIDE), BF16),
        pltpu.SemaphoreType.DMA((6,)),
        pltpu.SemaphoreType.DMA((TR_DEV // PACK_ROWS,)),
        pltpu.SemaphoreType.DMA((PACK_OUT,)),
    ]
    return pl.pallas_call(
        pack_kernel,
        out_shape=shape((DEVICES, TRACE_LIMIT, WIDE), BF16),
        in_specs=[HBM] * 7,
        out_specs=HBM,
        scratch_shapes=scratch,
        compiler_params=pltpu.CompilerParams(vmem_limit_bytes=PACK_VMEM),
        name="pack",
    )(*[row.reshape(1, TR_DEV) for row in meta], traces)


PART = shape((BIN_DEV, WIDE), BF16)
SIDE = shape((32, SLOTS), F32)
ROWS = pltpu.VMEM((TAPS * BIN_DEV, WIDE), F32)


def stack_first(slots):
    out = (PART, SIDE, shape((SLOTS, WIDE), BF16))
    return call(first_kernel, out, (0,), [ROWS], "stack_first", 3 * 10**9, 10**7, slots)


KNOWN = shape((32, LANES), F32)


def stack_next(damps, rows, side, sums):
    out = (PART, SIDE, KNOWN)
    return call(next_kernel, out, (0,) * 4, [ROWS], "stack_next", 3 * 10**9, 10**7, damps, rows, side, sums)


def finish(damps, known, sums):
    out = (shape((8, LANES), F32), shape((2, LANES), F32))
    return call(last_kernel, out, (0,) * 3, [], "finish", 10**4, 10**5, damps, known, sums)


SHIFTED = (shape((NS, SLOTS), BF16), shape((8, SLOTS), F32))
TURNED = shape((SLOTS // LANES, NS + 16, LANES), F32)


def shift_first(rows, side):
    return call(turn_kernel, (*SHIFTED, TURNED), (0, 0), [], "shift_first", 6 * 10**9, 2 * 10**7, rows, side)


def shift_next(turned, side):
    return call(shift_kernel, SHIFTED, (0, 0), [], "shift_next", 6 * 10**9, 2 * 10**7, turned, side)


def correlate(first, parts, shifted, energy, side):
    out = (shape((BIN_DEV, NS), BF16), shape((32 if first else 16, LANES), F32))
    scratch = [pltpu.VMEM((BIN_DEV * LROWS, NS), BF16), pltpu.VMEM((BIN_DEV, WIDE), F32)]
    kernel = functools.partial(corr_kernel, first)
    return call(kernel, out, (0,) * 7, scratch, "correlate", 4 * 10**9, 10**7, *parts, shifted, energy, side)


def off_perm(d):
    return [(i, (i + d) % 4) for i in range(4)]


def sum_copies(value):
    other = lax.ppermute(value, "core", [(0, 1), (1, 0)])
    rows = 16 if value.shape[0] == 16 else 24
    out = shape((DEVICES // 2, rows, LANES), BF16)
    scratch = [pltpu.VMEM((rows, LANES), F32)]
    copies = call(spread_kernel, out, (0, 0), scratch, "spread", 10**5, 10**6, value, other)
    return lax.all_to_all(copies, ("y", "x", "off"), split_axis=0, concat_axis=0, tiled=True)


def exchange(part):
    return part, *[lax.ppermute(part, "off", off_perm(d)) for d in (1, 2, 3)]


def on_device(
    traces,
    shot_id,
    receiver_id,
    cmp_bin,
    offset_class,
    shift_int,
    frac_index,
    damping_table,
    damping_index,
):
    outgoing = pack(traces, shot_id, receiver_id, cmp_bin, offset_class, shift_int, frac_index)
    slots = lax.all_to_all(outgoing, AXES, split_axis=0, concat_axis=0, tiled=True)
    entries = jnp.arange(damping_table.shape[0], dtype=jnp.int32)
    chosen = jnp.sum(jnp.where(entries == damping_index[:, None], damping_table, 0.0), axis=1)
    damps = jnp.broadcast_to(chosen[:, None, None], (2, 8, LANES)).reshape(16, LANES)
    part, side, rows = stack_first(slots)
    parts = exchange(part)
    shifted, energy, turned = shift_first(rows, side)
    pilot, sums = correlate(True, parts, shifted, energy, side)
    sums = sum_copies(sums)
    part, side, known = stack_next(damps, rows, side, sums)
    parts = exchange(part)
    shifted, energy = shift_next(turned, side)
    pilot, sums = correlate(False, parts, shifted, energy, side)
    sums = sum_copies(sums)
    rec, shot = finish(damps, known, sums)
    return (shot.reshape(-1), rec.reshape(-1), pilot)


def solution(mesh):
    mesh = Mesh(mesh.devices.reshape(4, 4, 2, 4), AXES)
    placed = (P(AXES, None),) + (P(AXES),) * 6 + (P(), P())
    return jax.shard_map(
        on_device, mesh=mesh, in_specs=placed, out_specs=(P(), P(), P(AXES[:3], None)), check_vma=False
    )
```

```python
import functools

import jax
import jax.numpy as jnp
from jax import lax
from jax.experimental import pallas as pl
from jax.experimental.pallas import tpu as pltpu
from jax.sharding import Mesh
from jax.sharding import PartitionSpec as P

NS = 2048
LAGS = 101
HALF = LAGS // 2
TAPS = 16
NPHASE = 32
SHIFT_MAX = 8
CLASSES = 4
TRACE_LIMIT = 4
BIN_DEV = 16
TR_DEV = 256
DEVICES = 128
SLOTS = DEVICES * TRACE_LIMIT
LANES = 128
WIDE = NS + LANES
LROWS = 104
LAG_TOP = 102
LAG_PAD = 4
BINS_STEP = 4
PACK_ROWS = 64
PACK_OUT = 4
PACK_VMEM = 63 * 1024 * 1024
BETA = 24.0
EPS = 1e-06
F32 = jnp.float32
BF16 = jnp.bfloat16
HEAD = 16
AXES = ("y", "x", "core", "off")

NN = (((1,), (0,)), ((), ()))
NT = (((1,), (1,)), ((), ()))
TN = (((0,), (0,)), ((), ()))


def dot(a, b, dims, precision=None):
    return lax.dot_general(a, b, dims, precision=precision, preferred_element_type=F32)


def iota(shape, axis):
    return lax.broadcasted_iota(jnp.int32, shape, axis)


def pack_kernel(*refs):
    meta_in, x_in, out_ref = refs[:6], refs[6], refs[7]
    meta_refs, (x_ref, y_ref, o_ref, meta_sem, x_sem, o_sem) = refs[8:14], refs[14:]
    parts = TR_DEV // PACK_ROWS
    x_copies = [
        pltpu.make_async_copy(
            x_in.at[pl.ds(i * PACK_ROWS, PACK_ROWS), :], x_ref.at[pl.ds(i * PACK_ROWS, PACK_ROWS), :], x_sem.at[i]
        )
        for i in range(parts)
    ]
    meta_copies = [pltpu.make_async_copy(meta_in[i], meta_refs[i], meta_sem.at[i]) for i in range(6)]
    for copy in meta_copies + x_copies:
        copy.start()
    for copy in meta_copies:
        copy.wait()
    shot, rec, bin_, cls, whole, frac = [ref[...] for ref in meta_refs]
    dest = (bin_ // BIN_DEV) * CLASSES + cls
    rows = [
        shot // 128,
        shot % 128,
        rec // 128,
        rec % 128,
        bin_ % BIN_DEV,
        frac,
        jnp.ones_like(shot),
        whole + SHIFT_MAX,
        dest,
    ]
    sub = iota((16, TR_DEV), 0)
    info = jnp.zeros((16, TR_DEV), F32)
    for i, row in enumerate(rows):
        info = jnp.where(sub == i, row.astype(F32), info)
    place = (iota((16, LANES), 1) == iota((16, LANES), 0) + HEAD).astype(F32).astype(BF16)
    cols = dot(info.astype(BF16), place, TN)
    amount = cols[:, HEAD + 7 : HEAD + 8].astype(jnp.int32)
    dest_col = cols[:, HEAD + 8 : HEAD + 9]
    same = (dest_col == dest.astype(F32)) & (iota((TR_DEV, TR_DEV), 0) < iota((TR_DEV, TR_DEV), 1))
    rank = jnp.sum(jnp.where(same, 1.0, 0.0), axis=0, keepdims=True).astype(jnp.int32)
    slot = dest * TRACE_LIMIT + rank
    onehot = (iota((SLOTS, TR_DEV), 0) == slot).astype(F32).astype(BF16)
    amount = amount - SHIFT_MAX
    tail = cols.astype(BF16)
    step = 32
    lane = iota((step, LANES), 1)
    blocks = WIDE // LANES
    for r in range(0, TR_DEV, step):
        if r % PACK_ROWS == 0:
            x_copies[r // PACK_ROWS].wait()
        source = lane + amount[r : r + step, :]
        index = source & (LANES - 1)
        turned = [
            jnp.take_along_axis(
                x_ref[r : r + step, c * LANES : (c + 1) * LANES].astype(F32), index, axis=1, mode="promise_in_bounds"
            )
            for c in range(blocks - 1)
        ] + [jnp.zeros((step, LANES), F32)]
        for c in range(blocks):
            before, after = turned[c - 1], turned[(c + 1) % blocks]
            y = jnp.where(source < 0, before, jnp.where(source >= LANES, after, turned[c])).astype(BF16)
            if c == blocks - 1:
                y = y + tail[r : r + step, :]
            y_ref[r : r + step, c * LANES : (c + 1) * LANES] = y
    out_copies = []
    group = DEVICES // PACK_OUT
    for i in range(PACK_OUT):
        rows = onehot[i * group * TRACE_LIMIT : (i + 1) * group * TRACE_LIMIT, :]
        placed = dot(rows, y_ref[...], NN).reshape(group, TRACE_LIMIT, WIDE).astype(BF16)
        o_ref[i * group : (i + 1) * group] = placed
        copy = pltpu.make_async_copy(
            o_ref.at[pl.ds(i * group, group)], out_ref.at[pl.ds(i * group, group)], o_sem.at[i]
        )
        copy.start()
        out_copies.append(copy)
    for copy in out_copies:
        copy.wait()


def one_hot_rows(row, count):
    return (iota((count, SLOTS), 0) == row.astype(jnp.int32)).astype(F32)


def one_hot_half(row, count):
    return one_hot_rows(row, count).astype(BF16)


def parts_of(value):
    top = value.astype(BF16)
    rest = value - top.astype(F32)
    middle = rest.astype(BF16)
    return jnp.concatenate([top, middle, (rest - middle.astype(F32)).astype(BF16)], axis=0)


def joined(sums):
    rows = sums.shape[0] // 3
    return (sums[0:rows, :] + sums[rows : 2 * rows, :]) + sums[2 * rows :, :]


def unit(size):
    return (iota((size, size), 0) == iota((size, size), 1)).astype(F32).astype(BF16)


def stack_rows(y_ref, head, frac, side_ref, part_ref, sum_ref):
    live = head[6:7, :]
    u = (iota((TAPS, SLOTS), 0) - (TAPS // 2 - 1)).astype(F32) - frac
    angle = jnp.pi * u
    safe = jnp.where(u == 0.0, 1.0, angle)
    sinc = jnp.where(u == 0.0, 1.0, jnp.sin(safe) / safe)
    taps = sinc * (0.5 + 0.5 * jnp.cos(angle * (1.0 / (TAPS // 2))))
    side_ref[0:16, :] = head
    side_ref[16:32, :] = taps
    owner = head[8:9, :]
    offset = owner - CLASSES * jnp.floor(owner * (1.0 / CLASSES))
    member = one_hot_rows(head[4:5, :], BIN_DEV) * (live / (1.0 + offset))
    rows = [member * taps[k : k + 1, :] for k in range(TAPS)]
    high = [row.astype(BF16) for row in rows]
    low = [(row - top.astype(F32)).astype(BF16) for row, top in zip(rows, high)]
    slots = y_ref[...]
    sum_ref[...] = dot(jnp.concatenate(high, axis=0), slots, NN) + dot(jnp.concatenate(low, axis=0), slots, NN)
    total = jnp.zeros((BIN_DEV, WIDE), F32)
    for k in range(TAPS):
        total = total + pltpu.roll(sum_ref[k * BIN_DEV : (k + 1) * BIN_DEV, :], (TAPS // 2 - 1 - k) % WIDE, 1)
    part_ref[:, :NS] = total[:, :NS].astype(BF16)
    mass = jnp.sum(member, axis=1, keepdims=True)
    m0 = mass.astype(BF16).astype(F32)
    m1 = (mass - m0).astype(BF16).astype(F32)
    m2 = mass - m0 - m1
    lane = iota((BIN_DEV, LANES), 1)
    tail = jnp.where(lane == 0, m0, jnp.where(lane == 1, m1, jnp.where(lane == 2, m2, 0.0)))
    part_ref[:, NS:] = tail.astype(BF16)


def first_kernel(damp_ref, slots_ref, part_ref, side_ref, y_ref, kept_ref, sum_ref):
    kept_ref[...] = damp_ref[...]
    y_ref[...] = slots_ref[...].reshape(SLOTS, WIDE)
    head = dot(unit(LANES), y_ref[:, NS:], NT)[HEAD : HEAD + 16, :]
    stack_rows(y_ref, head, head[5:6, :] * (1.0 / NPHASE), side_ref, part_ref, sum_ref)


def next_kernel(damp_ref, y_ref, head_ref, sums_ref, part_ref, side_ref, known_ref, sum_ref):
    damp = damp_ref[0:1, :]
    sums = gathered(sums_ref)
    count = sums[10:20, :]
    known_ref[...] = jnp.zeros_like(known_ref)
    known_ref[0:10, :] = sums[0:10, :] / ((1.0 + damp) * count + damp)
    known_ref[16:26, :] = count
    head = head_ref[0:16, :]
    frac = head[5:6, :] * (1.0 / NPHASE)
    for base, at in ((8, 0), (0, 2)):
        low = one_hot_half(head[at + 1 : at + 2, :], 128)
        high = one_hot_rows(head[at : at + 1, :], 8)
        found = joined(dot(parts_of(known_ref[base : base + 8, :]), low, NN))
        frac = frac + jnp.sum(found * high, axis=0, keepdims=True)
    stack_rows(y_ref, head, frac, side_ref, part_ref, sum_ref)


def last_kernel(damp_ref, known_ref, sums_ref, rec_ref, shot_ref):
    damp = damp_ref[8:9, :]
    step = gathered(sums_ref) / ((1.0 + damp) * known_ref[16:32, :] + damp)
    total = known_ref[0:16, :] + step
    rec_ref[...] = total[0:8, :]
    shot_ref[...] = total[8:10, :]


def turn_kernel(y_ref, side_ref, st_ref, energy_ref, xt_ref):
    eye = unit(LANES)
    groups = SLOTS // LANES
    for c in range(NS // LANES):
        block = dot(eye, y_ref[:, c * LANES : (c + 1) * LANES], NT)
        for q in range(groups):
            xt_ref[q, 8 + c * LANES : 8 + (c + 1) * LANES, :] = block[:, q * LANES : (q + 1) * LANES]
    block = dot(eye, y_ref[:, NS:], NT)
    for q in range(groups):
        part = block[:, q * LANES : (q + 1) * LANES]
        xt_ref[q, 0:8, :] = part[120:128, :]
        xt_ref[q, 8 + NS : 16 + NS, :] = part[0:8, :]
    shift_kernel(xt_ref, side_ref, st_ref, energy_ref)


def shift_kernel(xt_ref, side_ref, st_ref, energy_ref):
    groups = SLOTS // LANES
    chunk = 32
    energies = []
    for q in range(groups):
        tap = [
            jnp.broadcast_to(side_ref[16 + k : 17 + k, q * LANES : (q + 1) * LANES], (8, LANES)) for k in range(TAPS)
        ]

        def body(i, energy):
            base = pl.multiple_of(i * chunk, chunk)
            totals = [None] * (chunk // 8)
            for p in range(chunk + TAPS - 8):
                window = xt_ref[q, pl.ds(base + 1 + p, 8), :]
                for h in range(chunk // 8):
                    k = p - 8 * h
                    if 0 <= k < TAPS:
                        term = tap[k] * window
                        totals[h] = term if totals[h] is None else totals[h] + term
            for h in range(0, chunk // 8, 2):
                rounded = jnp.concatenate(totals[h : h + 2], axis=0).astype(BF16)
                st_ref[pl.ds(base + 8 * h, 16), q * LANES : (q + 1) * LANES] = rounded
                energy = energy + (totals[h] * totals[h] + totals[h + 1] * totals[h + 1])
            return energy

        energy = lax.fori_loop(0, NS // chunk, body, jnp.zeros((8, LANES), F32), unroll=4)
        energies.append(jnp.sum(energy, axis=0, keepdims=True))
    energy_ref[...] = jnp.broadcast_to(jnp.concatenate(energies, axis=1), (8, SLOTS))


def corr_kernel(first, p0_ref, p1_ref, p2_ref, p3_ref, st_ref, energy_ref, side_ref, pilot_ref, grad_ref, lag_ref, wide_ref):
    total = (p0_ref[...].astype(F32) + p2_ref[...].astype(F32)) + (
        p1_ref[...].astype(F32) + p3_ref[...].astype(F32)
    )
    mass = (total[:, NS : NS + 1] + total[:, NS + 1 : NS + 2]) + total[:, NS + 2 : NS + 3]
    pilot = (total[:, :NS] * lax.rsqrt(mass + 1.0)).astype(BF16)
    pilot_ref[...] = pilot
    wide = pilot.astype(F32)
    wide_ref[...] = pltpu.roll(jnp.concatenate([wide, jnp.zeros((BIN_DEV, LANES), F32)], axis=1), LAG_PAD, 1)
    pilot_scale = lax.rsqrt(jnp.sum(wide * wide, axis=1, keepdims=True) + EPS)
    head = side_ref[0:16, :]
    live = head[6:7, :]
    member = one_hot_rows(head[4:5, :], BIN_DEV) * live
    corr = jnp.zeros((LROWS, SLOTS), F32)
    for b0 in range(0, BIN_DEV, BINS_STEP):
        for bb in range(0, BINS_STEP, 2):
            eights = []
            for b in (b0 + bb, b0 + bb + 1):
                row = jnp.broadcast_to(wide_ref[b : b + 1, :], (8, WIDE))
                for g in range(0, LROWS, 8):
                    amount = (WIDE - (LAG_TOP - HALF) - LAG_PAD + g) % WIDE
                    eights.append(pltpu.roll(row, amount, 1, stride=1, stride_axis=0)[:, :NS])
                    if len(eights) % 2 == 0:
                        at = (b0 + bb) * LROWS + 8 * (len(eights) - 2)
                        lag_ref[at : at + 16, :] = jnp.concatenate(eights[-2:], axis=0).astype(BF16)
        every = dot(lag_ref[b0 * LROWS : (b0 + BINS_STEP) * LROWS, :], st_ref[...], NN)
        for bb in range(BINS_STEP):
            corr = corr + member[b0 + bb : b0 + bb + 1, :] * every[bb * LROWS : (bb + 1) * LROWS, :]
    scale = lax.rsqrt(energy_ref[0:1, :] + EPS) * jnp.sum(member * pilot_scale, axis=0, keepdims=True)
    lag = LAG_TOP - iota((LROWS, SLOTS), 0)
    exponent = jnp.where((lag >= 0) & (lag < LAGS), jnp.exp(BETA * (corr * scale)), 0.0)
    delay = jnp.sum(exponent * (lag - HALF).astype(F32), axis=0, keepdims=True) / jnp.sum(
        exponent, axis=0, keepdims=True
    )
    misfit = -delay * live
    grad_ref[...] = jnp.zeros_like(grad_ref)
    for at, out, rows in ((2, 0, 8), (0, 8, 2)):
        low = one_hot_half(head[at + 1 : at + 2, :], 128)
        high = one_hot_rows(head[at : at + 1, :], 8)
        values = high * misfit
        if first:
            values = jnp.concatenate([values, high * live], axis=0)
        sums = joined(dot(parts_of(values), low, NT))
        grad_ref[out : out + rows, :] = sums[0:rows, :]
        if first:
            grad_ref[16 + out : 16 + out + rows, :] = sums[8 : 8 + rows, :]


def spread_kernel(own_ref, other_ref, out_ref, rows_ref):
    total = own_ref[...] + other_ref[...]
    rows_ref[...] = jnp.zeros_like(rows_ref)
    rows_ref[0:10, :] = total[0:10, :]
    if total.shape[0] > 16:
        rows_ref[10:20, :] = total[16:26, :]
    out_ref[...] = jnp.broadcast_to(rows_ref[...].astype(BF16)[None], out_ref.shape)


def gathered(ref):
    return jnp.sum(ref[...].astype(F32), axis=0)


VMEM = pl.BlockSpec(memory_space=pltpu.VMEM)
HBM = pl.BlockSpec(memory_space=pl.ANY)
SMEM = pl.BlockSpec(memory_space=pltpu.SMEM)
PARAMS = pltpu.CompilerParams(vmem_limit_bytes=24 * 1024 * 1024)


def shape(dims, dtype):
    return jax.ShapeDtypeStruct(dims, dtype)


def call(kernel, out, memory, scratch, name, flops, moved, *args):
    return pl.pallas_call(
        kernel,
        out_shape=out,
        in_specs=[SMEM if space else VMEM for space in memory],
        out_specs=jax.tree.map(lambda _: VMEM, out),
        scratch_shapes=scratch,
        compiler_params=PARAMS,
        cost_estimate=pl.CostEstimate(flops=flops, bytes_accessed=moved, transcendentals=0),
        name=name,
    )(*args)


def pack(traces, *meta):
    scratch = [pltpu.VMEM((1, TR_DEV), jnp.int32)] * 6 + [
        pltpu.VMEM((TR_DEV, NS), BF16),
        pltpu.VMEM((TR_DEV, WIDE), BF16),
        pltpu.VMEM((DEVICES, TRACE_LIMIT, WIDE), BF16),
        pltpu.SemaphoreType.DMA((6,)),
        pltpu.SemaphoreType.DMA((TR_DEV // PACK_ROWS,)),
        pltpu.SemaphoreType.DMA((PACK_OUT,)),
    ]
    return pl.pallas_call(
        pack_kernel,
        out_shape=shape((DEVICES, TRACE_LIMIT, WIDE), BF16),
        in_specs=[HBM] * 7,
        out_specs=HBM,
        scratch_shapes=scratch,
        compiler_params=pltpu.CompilerParams(vmem_limit_bytes=PACK_VMEM),
        name="pack",
    )(*[row.reshape(1, TR_DEV) for row in meta], traces)


PART = shape((BIN_DEV, WIDE), BF16)
SIDE = shape((32, SLOTS), F32)
ROWS = pltpu.VMEM((TAPS * BIN_DEV, WIDE), F32)


def stack_first(damps, slots):
    out = (PART, SIDE, shape((SLOTS, WIDE), BF16), shape((16, LANES), F32))
    return call(first_kernel, out, (0, 0), [ROWS], "stack_first", 3 * 10**9, 10**7, damps, slots)


KNOWN = shape((32, LANES), F32)


def stack_next(damps, rows, side, sums):
    out = (PART, SIDE, KNOWN)
    return call(next_kernel, out, (0,) * 4, [ROWS], "stack_next", 3 * 10**9, 10**7, damps, rows, side, sums)


def finish(damps, known, sums):
    out = (shape((8, LANES), F32), shape((2, LANES), F32))
    return call(last_kernel, out, (0,) * 3, [], "finish", 10**4, 10**5, damps, known, sums)


SHIFTED = (shape((NS, SLOTS), BF16), shape((8, SLOTS), F32))
TURNED = shape((SLOTS // LANES, NS + 16, LANES), F32)


def shift_first(rows, side):
    return call(turn_kernel, (*SHIFTED, TURNED), (0, 0), [], "shift_first", 6 * 10**9, 2 * 10**7, rows, side)


def shift_next(turned, side):
    return call(shift_kernel, SHIFTED, (0, 0), [], "shift_next", 6 * 10**9, 2 * 10**7, turned, side)


def correlate(first, parts, shifted, energy, side):
    out = (shape((BIN_DEV, NS), BF16), shape((32 if first else 16, LANES), F32))
    scratch = [pltpu.VMEM((BIN_DEV * LROWS, NS), BF16), pltpu.VMEM((BIN_DEV, WIDE), F32)]
    kernel = functools.partial(corr_kernel, first)
    return call(kernel, out, (0,) * 7, scratch, "correlate", 4 * 10**9, 10**7, *parts, shifted, energy, side)


def off_perm(d):
    return [(i, (i + d) % 4) for i in range(4)]


def sum_copies(value):
    other = lax.ppermute(value, "core", [(0, 1), (1, 0)])
    rows = 16 if value.shape[0] == 16 else 24
    out = shape((DEVICES // 2, rows, LANES), BF16)
    scratch = [pltpu.VMEM((rows, LANES), F32)]
    copies = call(spread_kernel, out, (0, 0), scratch, "spread", 10**5, 10**6, value, other)
    return lax.all_to_all(copies, ("y", "x", "off"), split_axis=0, concat_axis=0, tiled=True)


def exchange(part):
    return part, *[lax.ppermute(part, "off", off_perm(d)) for d in (1, 2, 3)]


def on_device(
    traces,
    shot_id,
    receiver_id,
    cmp_bin,
    offset_class,
    shift_int,
    frac_index,
    damping_table,
    damping_index,
):
    outgoing = pack(traces, shot_id, receiver_id, cmp_bin, offset_class, shift_int, frac_index)
    slots = lax.all_to_all(outgoing, AXES, split_axis=0, concat_axis=0, tiled=True)
    entries = jnp.arange(damping_table.shape[0], dtype=jnp.int32)
    chosen = jnp.sum(jnp.where(entries == damping_index[:, None], damping_table, 0.0), axis=1)
    damps = jnp.broadcast_to(chosen[:, None, None], (2, 8, LANES)).reshape(16, LANES)
    part, side, rows, damps = stack_first(damps, slots)
    parts = exchange(part)
    shifted, energy, turned = shift_first(rows, side)
    pilot, sums = correlate(True, parts, shifted, energy, side)
    sums = sum_copies(sums)
    part, side, known = stack_next(damps, rows, side, sums)
    parts = exchange(part)
    shifted, energy = shift_next(turned, side)
    pilot, sums = correlate(False, parts, shifted, energy, side)
    sums = sum_copies(sums)
    rec, shot = finish(damps, known, sums)
    return (shot.reshape(-1), rec.reshape(-1), pilot)


def solution(mesh):
    mesh = Mesh(mesh.devices.reshape(4, 4, 2, 4), AXES)
    placed = (P(AXES, None),) + (P(AXES),) * 6 + (P(), P())
    return jax.shard_map(
        on_device, mesh=mesh, in_specs=placed, out_specs=(P(), P(), P(AXES[:3], None)), check_vma=False
    )
```

```python
import functools

import jax
import jax.numpy as jnp
from jax import lax
from jax.experimental import pallas as pl
from jax.experimental.pallas import tpu as pltpu
from jax.sharding import Mesh
from jax.sharding import PartitionSpec as P

NS = 2048
LAGS = 101
HALF = LAGS // 2
TAPS = 16
NPHASE = 32
SHIFT_MAX = 8
CLASSES = 4
TRACE_LIMIT = 4
BIN_DEV = 16
TR_DEV = 256
DEVICES = 128
SLOTS = DEVICES * TRACE_LIMIT
LANES = 128
WIDE = NS + LANES
LROWS = 104
LAG_TOP = 102
LAG_PAD = 4
BINS_STEP = 4
PACK_ROWS = 256
PACK_OUT = 4
PACK_VMEM = 63 * 1024 * 1024
BETA = 24.0
EPS = 1e-06
F32 = jnp.float32
BF16 = jnp.bfloat16
HEAD = 16
AXES = ("y", "x", "core", "off")

NN = (((1,), (0,)), ((), ()))
NT = (((1,), (1,)), ((), ()))
TN = (((0,), (0,)), ((), ()))


def dot(a, b, dims, precision=None):
    return lax.dot_general(a, b, dims, precision=precision, preferred_element_type=F32)


def iota(shape, axis):
    return lax.broadcasted_iota(jnp.int32, shape, axis)


def pack_kernel(*refs):
    meta_in, x_in, out_ref = refs[:6], refs[6], refs[7]
    meta_refs, (x_ref, y_ref, o_ref, meta_sem, x_sem, o_sem) = refs[8:14], refs[14:]
    parts = TR_DEV // PACK_ROWS
    x_copies = [
        pltpu.make_async_copy(
            x_in.at[pl.ds(i * PACK_ROWS, PACK_ROWS), :], x_ref.at[pl.ds(i * PACK_ROWS, PACK_ROWS), :], x_sem.at[i]
        )
        for i in range(parts)
    ]
    meta_copies = [pltpu.make_async_copy(meta_in[i], meta_refs[i], meta_sem.at[i]) for i in range(6)]
    for copy in meta_copies + x_copies:
        copy.start()
    for copy in meta_copies:
        copy.wait()
    shot, rec, bin_, cls, whole, frac = [ref[...] for ref in meta_refs]
    dest = (bin_ // BIN_DEV) * CLASSES + cls
    rows = [
        shot // 128,
        shot % 128,
        rec // 128,
        rec % 128,
        bin_ % BIN_DEV,
        frac,
        jnp.ones_like(shot),
        whole + SHIFT_MAX,
        dest,
    ]
    sub = iota((16, TR_DEV), 0)
    info = jnp.zeros((16, TR_DEV), F32)
    for i, row in enumerate(rows):
        info = jnp.where(sub == i, row.astype(F32), info)
    place = (iota((16, LANES), 1) == iota((16, LANES), 0) + HEAD).astype(F32).astype(BF16)
    cols = dot(info.astype(BF16), place, TN)
    amount = cols[:, HEAD + 7 : HEAD + 8].astype(jnp.int32)
    dest_col = cols[:, HEAD + 8 : HEAD + 9]
    same = (dest_col == dest.astype(F32)) & (iota((TR_DEV, TR_DEV), 0) < iota((TR_DEV, TR_DEV), 1))
    rank = jnp.sum(jnp.where(same, 1.0, 0.0), axis=0, keepdims=True).astype(jnp.int32)
    slot = dest * TRACE_LIMIT + rank
    onehot = (iota((SLOTS, TR_DEV), 0) == slot).astype(F32).astype(BF16)
    amount = amount - SHIFT_MAX
    tail = cols.astype(BF16)
    step = 32
    lane = iota((step, LANES), 1)
    blocks = WIDE // LANES
    for r in range(0, TR_DEV, step):
        if r % PACK_ROWS == 0:
            x_copies[r // PACK_ROWS].wait()
        source = lane + amount[r : r + step, :]
        index = source & (LANES - 1)
        turned = [
            jnp.take_along_axis(
                x_ref[r : r + step, c * LANES : (c + 1) * LANES].astype(F32), index, axis=1, mode="promise_in_bounds"
            )
            for c in range(blocks - 1)
        ] + [jnp.zeros((step, LANES), F32)]
        for c in range(blocks):
            before, after = turned[c - 1], turned[(c + 1) % blocks]
            y = jnp.where(source < 0, before, jnp.where(source >= LANES, after, turned[c])).astype(BF16)
            if c == blocks - 1:
                y = y + tail[r : r + step, :]
            y_ref[r : r + step, c * LANES : (c + 1) * LANES] = y
    out_copies = []
    group = DEVICES // PACK_OUT
    for i in range(PACK_OUT):
        rows = onehot[i * group * TRACE_LIMIT : (i + 1) * group * TRACE_LIMIT, :]
        placed = dot(rows, y_ref[...], NN).reshape(group, TRACE_LIMIT, WIDE).astype(BF16)
        o_ref[i * group : (i + 1) * group] = placed
        copy = pltpu.make_async_copy(
            o_ref.at[pl.ds(i * group, group)], out_ref.at[pl.ds(i * group, group)], o_sem.at[i]
        )
        copy.start()
        out_copies.append(copy)
    for copy in out_copies:
        copy.wait()


def one_hot_rows(row, count):
    return (iota((count, SLOTS), 0) == row.astype(jnp.int32)).astype(F32)


def one_hot_half(row, count):
    return one_hot_rows(row, count).astype(BF16)


def parts_of(value):
    top = value.astype(BF16)
    rest = value - top.astype(F32)
    middle = rest.astype(BF16)
    return jnp.concatenate([top, middle, (rest - middle.astype(F32)).astype(BF16)], axis=0)


def joined(sums):
    rows = sums.shape[0] // 3
    return (sums[0:rows, :] + sums[rows : 2 * rows, :]) + sums[2 * rows :, :]


def unit(size):
    return (iota((size, size), 0) == iota((size, size), 1)).astype(F32).astype(BF16)


def stack_rows(y_ref, head, frac, side_ref, part_ref, sum_ref):
    live = head[6:7, :]
    u = (iota((TAPS, SLOTS), 0) - (TAPS // 2 - 1)).astype(F32) - frac
    angle = jnp.pi * u
    safe = jnp.where(u == 0.0, 1.0, angle)
    sinc = jnp.where(u == 0.0, 1.0, jnp.sin(safe) / safe)
    taps = sinc * (0.5 + 0.5 * jnp.cos(angle * (1.0 / (TAPS // 2))))
    side_ref[0:16, :] = head
    side_ref[16:32, :] = taps
    owner = head[8:9, :]
    offset = owner - CLASSES * jnp.floor(owner * (1.0 / CLASSES))
    member = one_hot_rows(head[4:5, :], BIN_DEV) * (live / (1.0 + offset))
    rows = [member * taps[k : k + 1, :] for k in range(TAPS)]
    rows = jnp.concatenate([row.astype(BF16) for row in rows], axis=0)
    sum_ref[...] = dot(rows, y_ref[...], NN)
    total = jnp.zeros((BIN_DEV, WIDE), F32)
    for k in range(TAPS):
        total = total + pltpu.roll(sum_ref[k * BIN_DEV : (k + 1) * BIN_DEV, :], (TAPS // 2 - 1 - k) % WIDE, 1)
    part_ref[:, :NS] = total[:, :NS].astype(BF16)
    mass = jnp.sum(member, axis=1, keepdims=True)
    m0 = mass.astype(BF16).astype(F32)
    m1 = (mass - m0).astype(BF16).astype(F32)
    m2 = mass - m0 - m1
    lane = iota((BIN_DEV, LANES), 1)
    tail = jnp.where(lane == 0, m0, jnp.where(lane == 1, m1, jnp.where(lane == 2, m2, 0.0)))
    part_ref[:, NS:] = tail.astype(BF16)


def first_kernel(damp_ref, slots_ref, part_ref, side_ref, y_ref, kept_ref, sum_ref):
    kept_ref[...] = damp_ref[...]
    y_ref[...] = slots_ref[...].reshape(SLOTS, WIDE)
    head = dot(unit(LANES), y_ref[:, NS:], NT)[HEAD : HEAD + 16, :]
    stack_rows(y_ref, head, head[5:6, :] * (1.0 / NPHASE), side_ref, part_ref, sum_ref)


def next_kernel(damp_ref, y_ref, head_ref, sums_ref, part_ref, side_ref, known_ref, sum_ref):
    damp = damp_ref[0:1, :]
    sums = gathered(sums_ref)
    count = sums[10:20, :]
    known_ref[...] = jnp.zeros_like(known_ref)
    known_ref[0:10, :] = sums[0:10, :] / ((1.0 + damp) * count + damp)
    known_ref[16:26, :] = count
    head = head_ref[0:16, :]
    frac = head[5:6, :] * (1.0 / NPHASE)
    for base, at in ((8, 0), (0, 2)):
        low = one_hot_half(head[at + 1 : at + 2, :], 128)
        high = one_hot_rows(head[at : at + 1, :], 8)
        found = joined(dot(parts_of(known_ref[base : base + 8, :]), low, NN))
        frac = frac + jnp.sum(found * high, axis=0, keepdims=True)
    stack_rows(y_ref, head, frac, side_ref, part_ref, sum_ref)


def last_kernel(damp_ref, known_ref, sums_ref, rec_ref, shot_ref):
    damp = damp_ref[8:9, :]
    step = gathered(sums_ref) / ((1.0 + damp) * known_ref[16:32, :] + damp)
    total = known_ref[0:16, :] + step
    rec_ref[...] = total[0:8, :]
    shot_ref[...] = total[8:10, :]


def turn_kernel(y_ref, side_ref, st_ref, energy_ref, xt_ref):
    eye = unit(LANES)
    groups = SLOTS // LANES
    for c in range(NS // LANES):
        block = dot(eye, y_ref[:, c * LANES : (c + 1) * LANES], NT)
        for q in range(groups):
            xt_ref[q, 8 + c * LANES : 8 + (c + 1) * LANES, :] = block[:, q * LANES : (q + 1) * LANES]
    block = dot(eye, y_ref[:, NS:], NT)
    for q in range(groups):
        part = block[:, q * LANES : (q + 1) * LANES]
        xt_ref[q, 0:8, :] = part[120:128, :]
        xt_ref[q, 8 + NS : 16 + NS, :] = part[0:8, :]
    shift_kernel(xt_ref, side_ref, st_ref, energy_ref)


def shift_kernel(xt_ref, side_ref, st_ref, energy_ref):
    groups = SLOTS // LANES
    chunk = 32
    energies = []
    for q in range(groups):
        tap = [
            jnp.broadcast_to(side_ref[16 + k : 17 + k, q * LANES : (q + 1) * LANES], (8, LANES)) for k in range(TAPS)
        ]

        def body(i, energy):
            base = pl.multiple_of(i * chunk, chunk)
            totals = [None] * (chunk // 8)
            for p in range(chunk + TAPS - 8):
                window = xt_ref[q, pl.ds(base + 1 + p, 8), :]
                for h in range(chunk // 8):
                    k = p - 8 * h
                    if 0 <= k < TAPS:
                        term = tap[k] * window
                        totals[h] = term if totals[h] is None else totals[h] + term
            for h in range(0, chunk // 8, 2):
                rounded = jnp.concatenate(totals[h : h + 2], axis=0).astype(BF16)
                st_ref[pl.ds(base + 8 * h, 16), q * LANES : (q + 1) * LANES] = rounded
                energy = energy + (totals[h] * totals[h] + totals[h + 1] * totals[h + 1])
            return energy

        energy = lax.fori_loop(0, NS // chunk, body, jnp.zeros((8, LANES), F32), unroll=4)
        energies.append(jnp.sum(energy, axis=0, keepdims=True))
    energy_ref[...] = jnp.broadcast_to(jnp.concatenate(energies, axis=1), (8, SLOTS))


def corr_kernel(first, p0_ref, p1_ref, p2_ref, p3_ref, st_ref, energy_ref, side_ref, *refs):
    grad_ref, lag_ref, wide_ref = refs[-3:]
    total = (p0_ref[...].astype(F32) + p2_ref[...].astype(F32)) + (
        p1_ref[...].astype(F32) + p3_ref[...].astype(F32)
    )
    mass = (total[:, NS : NS + 1] + total[:, NS + 1 : NS + 2]) + total[:, NS + 2 : NS + 3]
    pilot = (total[:, :NS] * lax.rsqrt(mass + 1.0)).astype(BF16)
    if not first:
        refs[0][...] = pilot
    wide = pilot.astype(F32)
    wide_ref[...] = pltpu.roll(jnp.concatenate([wide, jnp.zeros((BIN_DEV, LANES), F32)], axis=1), LAG_PAD, 1)
    pilot_scale = lax.rsqrt(jnp.sum(wide * wide, axis=1, keepdims=True) + EPS)
    head = side_ref[0:16, :]
    live = head[6:7, :]
    member = one_hot_rows(head[4:5, :], BIN_DEV) * live
    corr = jnp.zeros((LROWS, SLOTS), F32)
    for b0 in range(0, BIN_DEV, BINS_STEP):
        for bb in range(0, BINS_STEP, 2):
            eights = []
            for b in (b0 + bb, b0 + bb + 1):
                row = jnp.broadcast_to(wide_ref[b : b + 1, :], (8, WIDE))
                for g in range(0, LROWS, 8):
                    amount = (WIDE - (LAG_TOP - HALF) - LAG_PAD + g) % WIDE
                    eights.append(pltpu.roll(row, amount, 1, stride=1, stride_axis=0)[:, :NS])
                    if len(eights) % 2 == 0:
                        at = (b0 + bb) * LROWS + 8 * (len(eights) - 2)
                        lag_ref[at : at + 16, :] = jnp.concatenate(eights[-2:], axis=0).astype(BF16)
        every = dot(lag_ref[b0 * LROWS : (b0 + BINS_STEP) * LROWS, :], st_ref[...], NN)
        for bb in range(BINS_STEP):
            corr = corr + member[b0 + bb : b0 + bb + 1, :] * every[bb * LROWS : (bb + 1) * LROWS, :]
    scale = lax.rsqrt(energy_ref[0:1, :] + EPS) * jnp.sum(member * pilot_scale, axis=0, keepdims=True)
    lag = LAG_TOP - iota((LROWS, SLOTS), 0)
    exponent = jnp.where((lag >= 0) & (lag < LAGS), jnp.exp(BETA * (corr * scale)), 0.0)
    delay = jnp.sum(exponent * (lag - HALF).astype(F32), axis=0, keepdims=True) / jnp.sum(
        exponent, axis=0, keepdims=True
    )
    misfit = -delay * live
    grad_ref[...] = jnp.zeros_like(grad_ref)
    low = jnp.concatenate([one_hot_half(head[at + 1 : at + 2, :], 128) for at in (2, 0)], axis=0)
    high = jnp.concatenate([one_hot_rows(head[at : at + 1, :], 8) for at in (2, 0)], axis=0)
    left = parts_of(high * misfit)
    if first:
        left = jnp.concatenate([left, (high * live).astype(BF16)], axis=0)
    sums = dot(left, low, NT)
    delays = joined(sums[0:48, :])
    grad_ref[0:8, :] = delays[0:8, 0:128]
    grad_ref[8:10, :] = delays[8:10, 128:256]
    if first:
        grad_ref[16:24, :] = sums[48:56, 0:128]
        grad_ref[24:26, :] = sums[56:58, 128:256]


def spread_kernel(own_ref, other_ref, out_ref, rows_ref):
    total = own_ref[...] + other_ref[...]
    rows_ref[...] = jnp.zeros_like(rows_ref)
    rows_ref[0:10, :] = total[0:10, :]
    if total.shape[0] > 16:
        rows_ref[10:20, :] = total[16:26, :]
    out_ref[...] = jnp.broadcast_to(rows_ref[...].astype(BF16)[None], out_ref.shape)


def gathered(ref):
    return jnp.sum(ref[...].astype(F32), axis=0)


VMEM = pl.BlockSpec(memory_space=pltpu.VMEM)
HBM = pl.BlockSpec(memory_space=pl.ANY)
SMEM = pl.BlockSpec(memory_space=pltpu.SMEM)
PARAMS = pltpu.CompilerParams(vmem_limit_bytes=24 * 1024 * 1024)


def shape(dims, dtype):
    return jax.ShapeDtypeStruct(dims, dtype)


def call(kernel, out, memory, scratch, name, flops, moved, *args):
    return pl.pallas_call(
        kernel,
        out_shape=out,
        in_specs=[SMEM if space else VMEM for space in memory],
        out_specs=jax.tree.map(lambda _: VMEM, out),
        scratch_shapes=scratch,
        compiler_params=PARAMS,
        cost_estimate=pl.CostEstimate(flops=flops, bytes_accessed=moved, transcendentals=0),
        name=name,
    )(*args)


def pack(traces, *meta):
    scratch = [pltpu.VMEM((1, TR_DEV), jnp.int32)] * 6 + [
        pltpu.VMEM((TR_DEV, NS), BF16),
        pltpu.VMEM((TR_DEV, WIDE), BF16),
        pltpu.VMEM((DEVICES, TRACE_LIMIT, WIDE), BF16),
        pltpu.SemaphoreType.DMA((6,)),
        pltpu.SemaphoreType.DMA((TR_DEV // PACK_ROWS,)),
        pltpu.SemaphoreType.DMA((PACK_OUT,)),
    ]
    return pl.pallas_call(
        pack_kernel,
        out_shape=shape((DEVICES, TRACE_LIMIT, WIDE), BF16),
        in_specs=[HBM] * 7,
        out_specs=HBM,
        scratch_shapes=scratch,
        compiler_params=pltpu.CompilerParams(vmem_limit_bytes=PACK_VMEM),
        name="pack",
    )(*[row.reshape(1, TR_DEV) for row in meta], traces)


PART = shape((BIN_DEV, WIDE), BF16)
SIDE = shape((32, SLOTS), F32)
ROWS = pltpu.VMEM((TAPS * BIN_DEV, WIDE), F32)


def stack_first(damps, slots):
    out = (PART, SIDE, shape((SLOTS, WIDE), BF16), shape((16, LANES), F32))
    return call(first_kernel, out, (0, 0), [ROWS], "stack_first", 3 * 10**9, 10**7, damps, slots)


KNOWN = shape((32, LANES), F32)


def stack_next(damps, rows, side, sums):
    out = (PART, SIDE, KNOWN)
    return call(next_kernel, out, (0,) * 4, [ROWS], "stack_next", 3 * 10**9, 10**7, damps, rows, side, sums)


def finish(damps, known, sums):
    out = (shape((8, LANES), F32), shape((2, LANES), F32))
    return call(last_kernel, out, (0,) * 3, [], "finish", 10**4, 10**5, damps, known, sums)


SHIFTED = (shape((NS, SLOTS), BF16), shape((8, SLOTS), F32))
TURNED = shape((SLOTS // LANES, NS + 16, LANES), F32)


def shift_first(rows, side):
    return call(turn_kernel, (*SHIFTED, TURNED), (0, 0), [], "shift_first", 6 * 10**9, 2 * 10**7, rows, side)


def shift_next(turned, side):
    return call(shift_kernel, SHIFTED, (0, 0), [], "shift_next", 6 * 10**9, 2 * 10**7, turned, side)


def correlate(first, parts, shifted, energy, side):
    out = (shape((32, LANES), F32),) if first else (shape((BIN_DEV, NS), BF16), shape((16, LANES), F32))
    scratch = [pltpu.VMEM((BIN_DEV * LROWS, NS), BF16), pltpu.VMEM((BIN_DEV, WIDE), F32)]
    kernel = functools.partial(corr_kernel, first)
    return call(kernel, out, (0,) * 7, scratch, "correlate", 4 * 10**9, 10**7, *parts, shifted, energy, side)


def off_perm(d):
    return [(i, (i + d) % 4) for i in range(4)]


def sum_copies(value):
    other = lax.ppermute(value, "core", [(0, 1), (1, 0)])
    rows = 16 if value.shape[0] == 16 else 24
    out = shape((DEVICES // 2, rows, LANES), BF16)
    scratch = [pltpu.VMEM((rows, LANES), F32)]
    copies = call(spread_kernel, out, (0, 0), scratch, "spread", 10**5, 10**6, value, other)
    return lax.all_to_all(copies, ("y", "x", "off"), split_axis=0, concat_axis=0, tiled=True)


def exchange(part):
    return part, *[lax.ppermute(part, "off", off_perm(d)) for d in (1, 2, 3)]


def on_device(
    traces,
    shot_id,
    receiver_id,
    cmp_bin,
    offset_class,
    shift_int,
    frac_index,
    damping_table,
    damping_index,
):
    outgoing = pack(traces, shot_id, receiver_id, cmp_bin, offset_class, shift_int, frac_index)
    slots = lax.all_to_all(outgoing, AXES, split_axis=0, concat_axis=0, tiled=True)
    entries = jnp.arange(damping_table.shape[0], dtype=jnp.int32)
    chosen = jnp.sum(jnp.where(entries == damping_index[:, None], damping_table, 0.0), axis=1)
    damps = jnp.broadcast_to(chosen[:, None, None], (2, 8, LANES)).reshape(16, LANES)
    part, side, rows, damps = stack_first(damps, slots)
    parts = exchange(part)
    shifted, energy, turned = shift_first(rows, side)
    (sums,) = correlate(True, parts, shifted, energy, side)
    sums = sum_copies(sums)
    part, side, known = stack_next(damps, rows, side, sums)
    parts = exchange(part)
    shifted, energy = shift_next(turned, side)
    pilot, sums = correlate(False, parts, shifted, energy, side)
    sums = sum_copies(sums)
    rec, shot = finish(damps, known, sums)
    return (shot.reshape(-1), rec.reshape(-1), pilot)


def solution(mesh):
    mesh = Mesh(mesh.devices.reshape(4, 4, 2, 4), AXES)
    placed = (P(AXES, None),) + (P(AXES),) * 6 + (P(), P())
    return jax.shard_map(
        on_device, mesh=mesh, in_specs=placed, out_specs=(P(), P(), P(AXES[:3], None)), check_vma=False
    )
```

```python
import functools

import jax
import jax.numpy as jnp
from jax import lax
from jax.experimental import pallas as pl
from jax.experimental.pallas import tpu as pltpu
from jax.sharding import Mesh
from jax.sharding import PartitionSpec as P

NS = 2048
LAGS = 101
HALF = LAGS // 2
TAPS = 16
NPHASE = 32
SHIFT_MAX = 8
CLASSES = 4
TRACE_LIMIT = 4
BIN_DEV = 16
TR_DEV = 256
DEVICES = 128
SLOTS = DEVICES * TRACE_LIMIT
LANES = 128
WIDE = NS + LANES
LROWS = 104
LAG_TOP = 102
LAG_PAD = 4
BINS_STEP = 4
PACK_ROWS = 256
PACK_OUT = 4
PACK_VMEM = 63 * 1024 * 1024
BETA = 24.0
EPS = 1e-06
F32 = jnp.float32
BF16 = jnp.bfloat16
HEAD = 16
AXES = ("y", "x", "core", "off")

NN = (((1,), (0,)), ((), ()))
NT = (((1,), (1,)), ((), ()))
TN = (((0,), (0,)), ((), ()))


def dot(a, b, dims, precision=None):
    return lax.dot_general(a, b, dims, precision=precision, preferred_element_type=F32)


def iota(shape, axis):
    return lax.broadcasted_iota(jnp.int32, shape, axis)


def pack_kernel(*refs):
    meta_in, x_in, out_ref = refs[:6], refs[6], refs[7]
    meta_refs, (x_ref, y_ref, o_ref, meta_sem, x_sem, o_sem) = refs[8:14], refs[14:]
    parts = TR_DEV // PACK_ROWS
    x_copies = [
        pltpu.make_async_copy(
            x_in.at[pl.ds(i * PACK_ROWS, PACK_ROWS), :], x_ref.at[pl.ds(i * PACK_ROWS, PACK_ROWS), :], x_sem.at[i]
        )
        for i in range(parts)
    ]
    meta_copies = [pltpu.make_async_copy(meta_in[i], meta_refs[i], meta_sem.at[i]) for i in range(6)]
    for copy in meta_copies + x_copies:
        copy.start()
    for copy in meta_copies:
        copy.wait()
    shot, rec, bin_, cls, whole, frac = [ref[...] for ref in meta_refs]
    dest = (bin_ // BIN_DEV) * CLASSES + cls
    rows = [
        shot // 128,
        shot % 128,
        rec // 128,
        rec % 128,
        bin_ % BIN_DEV,
        frac,
        jnp.ones_like(shot),
        whole + SHIFT_MAX,
        dest,
    ]
    sub = iota((16, TR_DEV), 0)
    info = jnp.zeros((16, TR_DEV), F32)
    for i, row in enumerate(rows):
        info = jnp.where(sub == i, row.astype(F32), info)
    place = (iota((16, LANES), 1) == iota((16, LANES), 0) + HEAD).astype(F32).astype(BF16)
    cols = dot(info.astype(BF16), place, TN)
    amount = cols[:, HEAD + 7 : HEAD + 8].astype(jnp.int32)
    dest_col = cols[:, HEAD + 8 : HEAD + 9]
    same = (dest_col == dest.astype(F32)) & (iota((TR_DEV, TR_DEV), 0) < iota((TR_DEV, TR_DEV), 1))
    rank = jnp.sum(jnp.where(same, 1.0, 0.0), axis=0, keepdims=True).astype(jnp.int32)
    slot = dest * TRACE_LIMIT + rank
    onehot = (iota((SLOTS, TR_DEV), 0) == slot).astype(F32).astype(BF16)
    amount = amount - SHIFT_MAX
    tail = cols.astype(BF16)
    step = 32
    lane = iota((step, LANES), 1)
    blocks = WIDE // LANES
    for r in range(0, TR_DEV, step):
        if r % PACK_ROWS == 0:
            x_copies[r // PACK_ROWS].wait()
        source = lane + amount[r : r + step, :]
        index = source & (LANES - 1)
        turned = [
            jnp.take_along_axis(
                x_ref[r : r + step, c * LANES : (c + 1) * LANES].astype(F32), index, axis=1, mode="promise_in_bounds"
            )
            for c in range(blocks - 1)
        ] + [jnp.zeros((step, LANES), F32)]
        for c in range(blocks):
            before, after = turned[c - 1], turned[(c + 1) % blocks]
            y = jnp.where(source < 0, before, jnp.where(source >= LANES, after, turned[c])).astype(BF16)
            if c == blocks - 1:
                y = y + tail[r : r + step, :]
            y_ref[r : r + step, c * LANES : (c + 1) * LANES] = y
    out_copies = []
    group = DEVICES // PACK_OUT
    for i in range(PACK_OUT):
        rows = onehot[i * group * TRACE_LIMIT : (i + 1) * group * TRACE_LIMIT, :]
        placed = dot(rows, y_ref[...], NN).reshape(group, TRACE_LIMIT, WIDE).astype(BF16)
        o_ref[i * group : (i + 1) * group] = placed
        copy = pltpu.make_async_copy(
            o_ref.at[pl.ds(i * group, group)], out_ref.at[pl.ds(i * group, group)], o_sem.at[i]
        )
        copy.start()
        out_copies.append(copy)
    for copy in out_copies:
        copy.wait()


def one_hot_rows(row, count):
    return (iota((count, SLOTS), 0) == row.astype(jnp.int32)).astype(F32)


def one_hot_half(row, count):
    return one_hot_rows(row, count).astype(BF16)


def parts_of(value):
    top = value.astype(BF16)
    rest = value - top.astype(F32)
    middle = rest.astype(BF16)
    return jnp.concatenate([top, middle, (rest - middle.astype(F32)).astype(BF16)], axis=0)


def joined(sums):
    rows = sums.shape[0] // 3
    return (sums[0:rows, :] + sums[rows : 2 * rows, :]) + sums[2 * rows :, :]


def unit(size):
    return (iota((size, size), 0) == iota((size, size), 1)).astype(F32).astype(BF16)


def stack_rows(y_ref, head, frac, side_ref, part_ref, sum_ref):
    live = head[6:7, :]
    u = (iota((TAPS, SLOTS), 0) - (TAPS // 2 - 1)).astype(F32) - frac
    angle = jnp.pi * u
    safe = jnp.where(u == 0.0, 1.0, angle)
    sinc = jnp.where(u == 0.0, 1.0, jnp.sin(safe) / safe)
    taps = sinc * (0.5 + 0.5 * jnp.cos(angle * (1.0 / (TAPS // 2))))
    side_ref[0:16, :] = head
    side_ref[16:32, :] = taps
    owner = head[8:9, :]
    offset = owner - CLASSES * jnp.floor(owner * (1.0 / CLASSES))
    member = one_hot_rows(head[4:5, :], BIN_DEV) * (live / (1.0 + offset))
    rows = [member * taps[k : k + 1, :] for k in range(TAPS)]
    rows = jnp.concatenate([row.astype(BF16) for row in rows], axis=0)
    sum_ref[...] = dot(rows, y_ref[...], NN)
    total = jnp.zeros((BIN_DEV, WIDE), F32)
    for k in range(TAPS):
        total = total + pltpu.roll(sum_ref[k * BIN_DEV : (k + 1) * BIN_DEV, :], (TAPS // 2 - 1 - k) % WIDE, 1)
    part_ref[:, :NS] = total[:, :NS].astype(BF16)
    mass = jnp.sum(member, axis=1, keepdims=True)
    m0 = mass.astype(BF16).astype(F32)
    m1 = (mass - m0).astype(BF16).astype(F32)
    m2 = mass - m0 - m1
    lane = iota((BIN_DEV, LANES), 1)
    tail = jnp.where(lane == 0, m0, jnp.where(lane == 1, m1, jnp.where(lane == 2, m2, 0.0)))
    part_ref[:, NS:] = tail.astype(BF16)


def first_kernel(damp_ref, slots_ref, part_ref, side_ref, y_ref, kept_ref, sum_ref):
    kept_ref[...] = damp_ref[...]
    y_ref[...] = slots_ref[...].reshape(SLOTS, WIDE)
    head = dot(unit(LANES), y_ref[:, NS:], NT)[HEAD : HEAD + 16, :]
    stack_rows(y_ref, head, head[5:6, :] * (1.0 / NPHASE), side_ref, part_ref, sum_ref)


def next_kernel(damp_ref, y_ref, head_ref, sums_ref, part_ref, side_ref, known_ref, sum_ref):
    damp = damp_ref[0:1, :]
    sums = gathered(sums_ref)
    count = sums[10:20, :]
    known_ref[...] = jnp.zeros_like(known_ref)
    known_ref[0:10, :] = sums[0:10, :] / ((1.0 + damp) * count + damp)
    known_ref[16:26, :] = count
    head = head_ref[0:16, :]
    frac = head[5:6, :] * (1.0 / NPHASE)
    for base, at in ((8, 0), (0, 2)):
        low = one_hot_half(head[at + 1 : at + 2, :], 128)
        high = one_hot_rows(head[at : at + 1, :], 8)
        found = joined(dot(parts_of(known_ref[base : base + 8, :]), low, NN))
        frac = frac + jnp.sum(found * high, axis=0, keepdims=True)
    stack_rows(y_ref, head, frac, side_ref, part_ref, sum_ref)


def last_kernel(damp_ref, known_ref, sums_ref, rec_ref, shot_ref):
    damp = damp_ref[8:9, :]
    step = gathered(sums_ref) / ((1.0 + damp) * known_ref[16:32, :] + damp)
    total = known_ref[0:16, :] + step
    rec_ref[...] = total[0:8, :]
    shot_ref[...] = total[8:10, :]


def turn_kernel(y_ref, side_ref, st_ref, energy_ref, xt_ref):
    eye = unit(LANES)
    groups = SLOTS // LANES
    for c in range(NS // LANES):
        block = dot(eye, y_ref[:, c * LANES : (c + 1) * LANES], NT)
        for q in range(groups):
            xt_ref[q, 8 + c * LANES : 8 + (c + 1) * LANES, :] = block[:, q * LANES : (q + 1) * LANES]
    block = dot(eye, y_ref[:, NS:], NT)
    for q in range(groups):
        part = block[:, q * LANES : (q + 1) * LANES]
        xt_ref[q, 0:8, :] = part[120:128, :]
        xt_ref[q, 8 + NS : 16 + NS, :] = part[0:8, :]
    shift_kernel(xt_ref, side_ref, st_ref, energy_ref)


def shift_kernel(xt_ref, side_ref, st_ref, energy_ref):
    groups = SLOTS // LANES
    chunk = 32
    energies = []
    for q in range(groups):
        tap = [
            jnp.broadcast_to(side_ref[16 + k : 17 + k, q * LANES : (q + 1) * LANES], (8, LANES)) for k in range(TAPS)
        ]

        def body(i, energy):
            base = pl.multiple_of(i * chunk, chunk)
            totals = [None] * (chunk // 8)
            for p in range(chunk + TAPS - 8):
                window = xt_ref[q, pl.ds(base + 1 + p, 8), :]
                for h in range(chunk // 8):
                    k = p - 8 * h
                    if 0 <= k < TAPS:
                        term = tap[k] * window
                        totals[h] = term if totals[h] is None else totals[h] + term
            for h in range(0, chunk // 8, 2):
                rounded = jnp.concatenate(totals[h : h + 2], axis=0).astype(BF16)
                st_ref[pl.ds(base + 8 * h, 16), q * LANES : (q + 1) * LANES] = rounded
                energy = energy + (totals[h] * totals[h] + totals[h + 1] * totals[h + 1])
            return energy

        energy = lax.fori_loop(0, NS // chunk, body, jnp.zeros((8, LANES), F32), unroll=4)
        energies.append(jnp.sum(energy, axis=0, keepdims=True))
    energy_ref[...] = jnp.broadcast_to(jnp.concatenate(energies, axis=1), (8, SLOTS))


def corr_kernel(first, p0_ref, p1_ref, p2_ref, p3_ref, st_ref, energy_ref, side_ref, *refs):
    grad_ref, lag_ref, wide_ref = refs[:3] if first else refs[1:4]
    total = (p0_ref[...].astype(F32) + p2_ref[...].astype(F32)) + (
        p1_ref[...].astype(F32) + p3_ref[...].astype(F32)
    )
    mass = (total[:, NS : NS + 1] + total[:, NS + 1 : NS + 2]) + total[:, NS + 2 : NS + 3]
    pilot = (total[:, :NS] * lax.rsqrt(mass + 1.0)).astype(BF16)
    if not first:
        pilot_ref, pilot_sem = refs[4:]
        pilot_ref[...] = pilot
        pilot_copy = pltpu.make_async_copy(pilot_ref, refs[0], pilot_sem)
        pilot_copy.start()
    wide = pilot.astype(F32)
    wide_ref[...] = pltpu.roll(jnp.concatenate([wide, jnp.zeros((BIN_DEV, LANES), F32)], axis=1), LAG_PAD, 1)
    pilot_scale = lax.rsqrt(jnp.sum(wide * wide, axis=1, keepdims=True) + EPS)
    head = side_ref[0:16, :]
    live = head[6:7, :]
    member = one_hot_rows(head[4:5, :], BIN_DEV) * live
    corr = jnp.zeros((LROWS, SLOTS), F32)
    for b0 in range(0, BIN_DEV, BINS_STEP):
        for bb in range(0, BINS_STEP, 2):
            eights = []
            for b in (b0 + bb, b0 + bb + 1):
                row = jnp.broadcast_to(wide_ref[b : b + 1, :], (8, WIDE))
                for g in range(0, LROWS, 8):
                    amount = (WIDE - (LAG_TOP - HALF) - LAG_PAD + g) % WIDE
                    eights.append(pltpu.roll(row, amount, 1, stride=1, stride_axis=0)[:, :NS])
                    if len(eights) % 2 == 0:
                        at = (b0 + bb) * LROWS + 8 * (len(eights) - 2)
                        lag_ref[at : at + 16, :] = jnp.concatenate(eights[-2:], axis=0).astype(BF16)
        every = dot(lag_ref[b0 * LROWS : (b0 + BINS_STEP) * LROWS, :], st_ref[...], NN)
        for bb in range(BINS_STEP):
            corr = corr + member[b0 + bb : b0 + bb + 1, :] * every[bb * LROWS : (bb + 1) * LROWS, :]
    scale = lax.rsqrt(energy_ref[0:1, :] + EPS) * jnp.sum(member * pilot_scale, axis=0, keepdims=True)
    lag = LAG_TOP - iota((LROWS, SLOTS), 0)
    exponent = jnp.where((lag >= 0) & (lag < LAGS), jnp.exp(BETA * (corr * scale)), 0.0)
    delay = jnp.sum(exponent * (lag - HALF).astype(F32), axis=0, keepdims=True) / jnp.sum(
        exponent, axis=0, keepdims=True
    )
    misfit = -delay * live
    grad_ref[...] = jnp.zeros_like(grad_ref)
    low = jnp.concatenate([one_hot_half(head[at + 1 : at + 2, :], 128) for at in (2, 0)], axis=0)
    high = jnp.concatenate([one_hot_rows(head[at : at + 1, :], 8) for at in (2, 0)], axis=0)
    left = parts_of(high * misfit)
    if first:
        left = jnp.concatenate([left, (high * live).astype(BF16)], axis=0)
    sums = dot(left, low, NT)
    delays = joined(sums[0:48, :])
    grad_ref[0:8, :] = delays[0:8, 0:128]
    grad_ref[8:10, :] = delays[8:10, 128:256]
    if first:
        grad_ref[16:24, :] = sums[48:56, 0:128]
        grad_ref[24:26, :] = sums[56:58, 128:256]
    else:
        pilot_copy.wait()


def spread_kernel(own_ref, other_ref, out_ref, rows_ref):
    total = own_ref[...] + other_ref[...]
    rows_ref[...] = jnp.zeros_like(rows_ref)
    rows_ref[0:10, :] = total[0:10, :]
    if total.shape[0] > 16:
        rows_ref[10:20, :] = total[16:26, :]
    out_ref[...] = jnp.broadcast_to(rows_ref[...].astype(BF16)[None], out_ref.shape)


def gathered(ref):
    return jnp.sum(ref[...].astype(F32), axis=0)


VMEM = pl.BlockSpec(memory_space=pltpu.VMEM)
HBM = pl.BlockSpec(memory_space=pl.ANY)
SMEM = pl.BlockSpec(memory_space=pltpu.SMEM)
PARAMS = pltpu.CompilerParams(vmem_limit_bytes=24 * 1024 * 1024)


def shape(dims, dtype):
    return jax.ShapeDtypeStruct(dims, dtype)


def call(kernel, out, memory, scratch, name, flops, moved, *args):
    return pl.pallas_call(
        kernel,
        out_shape=out,
        in_specs=[SMEM if space else VMEM for space in memory],
        out_specs=jax.tree.map(lambda _: VMEM, out),
        scratch_shapes=scratch,
        compiler_params=PARAMS,
        cost_estimate=pl.CostEstimate(flops=flops, bytes_accessed=moved, transcendentals=0),
        name=name,
    )(*args)


def pack(traces, *meta):
    scratch = [pltpu.VMEM((1, TR_DEV), jnp.int32)] * 6 + [
        pltpu.VMEM((TR_DEV, NS), BF16),
        pltpu.VMEM((TR_DEV, WIDE), BF16),
        pltpu.VMEM((DEVICES, TRACE_LIMIT, WIDE), BF16),
        pltpu.SemaphoreType.DMA((6,)),
        pltpu.SemaphoreType.DMA((TR_DEV // PACK_ROWS,)),
        pltpu.SemaphoreType.DMA((PACK_OUT,)),
    ]
    return pl.pallas_call(
        pack_kernel,
        out_shape=shape((DEVICES, TRACE_LIMIT, WIDE), BF16),
        in_specs=[HBM] * 7,
        out_specs=HBM,
        scratch_shapes=scratch,
        compiler_params=pltpu.CompilerParams(vmem_limit_bytes=PACK_VMEM),
        name="pack",
    )(*[row.reshape(1, TR_DEV) for row in meta], traces)


PART = shape((BIN_DEV, WIDE), BF16)
SIDE = shape((32, SLOTS), F32)
ROWS = pltpu.VMEM((TAPS * BIN_DEV, WIDE), F32)


def stack_first(damps, slots):
    out = (PART, SIDE, shape((SLOTS, WIDE), BF16), shape((16, LANES), F32))
    return call(first_kernel, out, (0, 0), [ROWS], "stack_first", 3 * 10**9, 10**7, damps, slots)


KNOWN = shape((32, LANES), F32)


def stack_next(damps, rows, side, sums):
    out = (PART, SIDE, KNOWN)
    return call(next_kernel, out, (0,) * 4, [ROWS], "stack_next", 3 * 10**9, 10**7, damps, rows, side, sums)


def finish(damps, known, sums):
    out = (shape((8, LANES), F32), shape((2, LANES), F32))
    return call(last_kernel, out, (0,) * 3, [], "finish", 10**4, 10**5, damps, known, sums)


SHIFTED = (shape((NS, SLOTS), BF16), shape((8, SLOTS), F32))
TURNED = shape((SLOTS // LANES, NS + 16, LANES), F32)


def shift_first(rows, side):
    return call(turn_kernel, (*SHIFTED, TURNED), (0, 0), [], "shift_first", 6 * 10**9, 2 * 10**7, rows, side)


def shift_next(turned, side):
    return call(shift_kernel, SHIFTED, (0, 0), [], "shift_next", 6 * 10**9, 2 * 10**7, turned, side)


def correlate(first, parts, shifted, energy, side):
    sums = shape((32 if first else 16, LANES), F32)
    scratch = [pltpu.VMEM((BIN_DEV * LROWS, NS), BF16), pltpu.VMEM((BIN_DEV, WIDE), F32)]
    if not first:
        scratch += [pltpu.VMEM((BIN_DEV, NS), BF16), pltpu.SemaphoreType.DMA]
    return pl.pallas_call(
        functools.partial(corr_kernel, first),
        out_shape=(sums,) if first else (shape((BIN_DEV, NS), BF16), sums),
        in_specs=[VMEM] * 7,
        out_specs=(VMEM,) if first else (HBM, VMEM),
        scratch_shapes=scratch,
        compiler_params=PARAMS,
        cost_estimate=pl.CostEstimate(flops=4 * 10**9, bytes_accessed=10**7, transcendentals=0),
        name="correlate",
    )(*parts, shifted, energy, side)


def off_perm(d):
    return [(i, (i + d) % 4) for i in range(4)]


def sum_copies(value):
    other = lax.ppermute(value, "core", [(0, 1), (1, 0)])
    rows = 16 if value.shape[0] == 16 else 24
    out = shape((DEVICES // 2, rows, LANES), BF16)
    scratch = [pltpu.VMEM((rows, LANES), F32)]
    copies = call(spread_kernel, out, (0, 0), scratch, "spread", 10**5, 10**6, value, other)
    return lax.all_to_all(copies, ("y", "x", "off"), split_axis=0, concat_axis=0, tiled=True)


def exchange(part):
    return part, *[lax.ppermute(part, "off", off_perm(d)) for d in (1, 2, 3)]


def on_device(
    traces,
    shot_id,
    receiver_id,
    cmp_bin,
    offset_class,
    shift_int,
    frac_index,
    damping_table,
    damping_index,
):
    outgoing = pack(traces, shot_id, receiver_id, cmp_bin, offset_class, shift_int, frac_index)
    slots = lax.all_to_all(outgoing, AXES, split_axis=0, concat_axis=0, tiled=True)
    entries = jnp.arange(damping_table.shape[0], dtype=jnp.int32)
    chosen = jnp.sum(jnp.where(entries == damping_index[:, None], damping_table, 0.0), axis=1)
    damps = jnp.broadcast_to(chosen[:, None, None], (2, 8, LANES)).reshape(16, LANES)
    part, side, rows, damps = stack_first(damps, slots)
    parts = exchange(part)
    shifted, energy, turned = shift_first(rows, side)
    (sums,) = correlate(True, parts, shifted, energy, side)
    sums = sum_copies(sums)
    part, side, known = stack_next(damps, rows, side, sums)
    parts = exchange(part)
    shifted, energy = shift_next(turned, side)
    pilot, sums = correlate(False, parts, shifted, energy, side)
    sums = sum_copies(sums)
    rec, shot = finish(damps, known, sums)
    return (shot.reshape(-1), rec.reshape(-1), pilot)


def solution(mesh):
    mesh = Mesh(mesh.devices.reshape(4, 4, 2, 4), AXES)
    placed = (P(AXES, None),) + (P(AXES),) * 6 + (P(), P())
    return jax.shard_map(
        on_device, mesh=mesh, in_specs=placed, out_specs=(P(), P(), P(AXES[:3], None)), check_vma=False
    )
```

```python
import functools

import jax
import jax.numpy as jnp
from jax import lax
from jax.experimental import pallas as pl
from jax.experimental.pallas import tpu as pltpu
from jax.sharding import Mesh
from jax.sharding import PartitionSpec as P

NS = 2048
LAGS = 101
HALF = LAGS // 2
TAPS = 16
NPHASE = 32
SHIFT_MAX = 8
CLASSES = 4
TRACE_LIMIT = 4
BIN_DEV = 16
TR_DEV = 256
DEVICES = 128
SLOTS = DEVICES * TRACE_LIMIT
LANES = 128
WIDE = NS + LANES
LROWS = 104
LAG_TOP = 102
LAG_PAD = 4
BINS_STEP = 4
PACK_ROWS = 256
PACK_OUT = 4
PACK_VMEM = 63 * 1024 * 1024
BETA = 24.0
EPS = 1e-06
F32 = jnp.float32
BF16 = jnp.bfloat16
HEAD = 16
AXES = ("y", "x", "core", "off")

NN = (((1,), (0,)), ((), ()))
NT = (((1,), (1,)), ((), ()))
TN = (((0,), (0,)), ((), ()))


def dot(a, b, dims, precision=None):
    return lax.dot_general(a, b, dims, precision=precision, preferred_element_type=F32)


def iota(shape, axis):
    return lax.broadcasted_iota(jnp.int32, shape, axis)


def pack_kernel(*refs):
    meta_in, x_in, out_ref = refs[:6], refs[6], refs[7]
    meta_refs, (x_ref, y_ref, o_ref, meta_sem, x_sem, o_sem) = refs[8:14], refs[14:]
    parts = TR_DEV // PACK_ROWS
    x_copies = [
        pltpu.make_async_copy(
            x_in.at[pl.ds(i * PACK_ROWS, PACK_ROWS), :], x_ref.at[pl.ds(i * PACK_ROWS, PACK_ROWS), :], x_sem.at[i]
        )
        for i in range(parts)
    ]
    meta_copies = [pltpu.make_async_copy(meta_in[i], meta_refs[i], meta_sem.at[i]) for i in range(6)]
    for copy in meta_copies + x_copies:
        copy.start()
    for copy in meta_copies:
        copy.wait()
    shot, rec, bin_, cls, whole, frac = [ref[...] for ref in meta_refs]
    dest = (bin_ // BIN_DEV) * CLASSES + cls
    rows = [
        shot // 128,
        shot % 128,
        rec // 128,
        rec % 128,
        bin_ % BIN_DEV,
        frac,
        jnp.ones_like(shot),
        whole + SHIFT_MAX,
        dest,
    ]
    sub = iota((16, TR_DEV), 0)
    info = jnp.zeros((16, TR_DEV), F32)
    for i, row in enumerate(rows):
        info = jnp.where(sub == i, row.astype(F32), info)
    place = (iota((16, LANES), 1) == iota((16, LANES), 0) + HEAD).astype(F32).astype(BF16)
    cols = dot(info.astype(BF16), place, TN)
    amount = cols[:, HEAD + 7 : HEAD + 8].astype(jnp.int32)
    dest_col = cols[:, HEAD + 8 : HEAD + 9]
    same = (dest_col == dest.astype(F32)) & (iota((TR_DEV, TR_DEV), 0) < iota((TR_DEV, TR_DEV), 1))
    rank = jnp.sum(jnp.where(same, 1.0, 0.0), axis=0, keepdims=True).astype(jnp.int32)
    slot = dest * TRACE_LIMIT + rank
    onehot = (iota((SLOTS, TR_DEV), 0) == slot).astype(F32).astype(BF16)
    amount = amount - SHIFT_MAX
    tail = cols.astype(BF16)
    step = 32
    lane = iota((step, LANES), 1)
    blocks = WIDE // LANES
    for r in range(0, TR_DEV, step):
        if r % PACK_ROWS == 0:
            x_copies[r // PACK_ROWS].wait()
        source = lane + amount[r : r + step, :]
        index = source & (LANES - 1)
        turned = [
            jnp.take_along_axis(
                x_ref[r : r + step, c * LANES : (c + 1) * LANES].astype(F32), index, axis=1, mode="promise_in_bounds"
            )
            for c in range(blocks - 1)
        ] + [jnp.zeros((step, LANES), F32)]
        for c in range(blocks):
            before, after = turned[c - 1], turned[(c + 1) % blocks]
            y = jnp.where(source < 0, before, jnp.where(source >= LANES, after, turned[c])).astype(BF16)
            if c == blocks - 1:
                y = y + tail[r : r + step, :]
            y_ref[r : r + step, c * LANES : (c + 1) * LANES] = y
    out_copies = []
    group = DEVICES // PACK_OUT
    for i in range(PACK_OUT):
        rows = onehot[i * group * TRACE_LIMIT : (i + 1) * group * TRACE_LIMIT, :]
        placed = dot(rows, y_ref[...], NN).reshape(group, TRACE_LIMIT, WIDE).astype(BF16)
        o_ref[i * group : (i + 1) * group] = placed
        copy = pltpu.make_async_copy(
            o_ref.at[pl.ds(i * group, group)], out_ref.at[pl.ds(i * group, group)], o_sem.at[i]
        )
        copy.start()
        out_copies.append(copy)
    for copy in out_copies:
        copy.wait()


def one_hot_rows(row, count):
    return (iota((count, SLOTS), 0) == row.astype(jnp.int32)).astype(F32)


def one_hot_half(row, count):
    return one_hot_rows(row, count).astype(BF16)


def parts_of(value):
    top = value.astype(BF16)
    rest = value - top.astype(F32)
    middle = rest.astype(BF16)
    return jnp.concatenate([top, middle, (rest - middle.astype(F32)).astype(BF16)], axis=0)


def joined(sums):
    rows = sums.shape[0] // 3
    return (sums[0:rows, :] + sums[rows : 2 * rows, :]) + sums[2 * rows :, :]


def unit(size):
    return (iota((size, size), 0) == iota((size, size), 1)).astype(F32).astype(BF16)


def stack_rows(y_ref, head, frac, side_ref, part_ref, sum_ref):
    live = head[6:7, :]
    u = (iota((TAPS, SLOTS), 0) - (TAPS // 2 - 1)).astype(F32) - frac
    angle = jnp.pi * u
    safe = jnp.where(u == 0.0, 1.0, angle)
    sinc = jnp.where(u == 0.0, 1.0, jnp.sin(safe) / safe)
    taps = sinc * (0.5 + 0.5 * jnp.cos(angle * (1.0 / (TAPS // 2))))
    side_ref[0:16, :] = head
    side_ref[16:32, :] = taps
    owner = head[8:9, :]
    offset = owner - CLASSES * jnp.floor(owner * (1.0 / CLASSES))
    member = one_hot_rows(head[4:5, :], BIN_DEV) * (live / (1.0 + offset))
    rows = [member * taps[k : k + 1, :] for k in range(TAPS)]
    rows = jnp.concatenate([row.astype(BF16) for row in rows], axis=0)
    sum_ref[...] = dot(rows, y_ref[...], NN)
    total = jnp.zeros((BIN_DEV, WIDE), F32)
    for k in range(TAPS):
        total = total + pltpu.roll(sum_ref[k * BIN_DEV : (k + 1) * BIN_DEV, :], (TAPS // 2 - 1 - k) % WIDE, 1)
    part_ref[:, :NS] = total[:, :NS].astype(BF16)
    mass = jnp.sum(member, axis=1, keepdims=True)
    m0 = mass.astype(BF16).astype(F32)
    m1 = (mass - m0).astype(BF16).astype(F32)
    m2 = mass - m0 - m1
    lane = iota((BIN_DEV, LANES), 1)
    tail = jnp.where(lane == 0, m0, jnp.where(lane == 1, m1, jnp.where(lane == 2, m2, 0.0)))
    part_ref[:, NS:] = tail.astype(BF16)


def first_kernel(damp_ref, slots_ref, part_ref, side_ref, y_ref, kept_ref, sum_ref):
    kept_ref[...] = damp_ref[...]
    y_ref[...] = slots_ref[...].reshape(SLOTS, WIDE)
    head = dot(unit(LANES), y_ref[:, NS:], NT)[HEAD : HEAD + 16, :]
    stack_rows(y_ref, head, head[5:6, :] * (1.0 / NPHASE), side_ref, part_ref, sum_ref)


def next_kernel(damp_ref, y_ref, head_ref, sums_ref, part_ref, side_ref, known_ref, sum_ref):
    damp = damp_ref[0:1, :]
    sums = gathered(sums_ref)
    count = sums[10:20, :]
    known_ref[...] = jnp.zeros_like(known_ref)
    known_ref[0:10, :] = sums[0:10, :] / ((1.0 + damp) * count + damp)
    known_ref[16:26, :] = count
    head = head_ref[0:16, :]
    frac = head[5:6, :] * (1.0 / NPHASE)
    for base, at in ((8, 0), (0, 2)):
        low = one_hot_half(head[at + 1 : at + 2, :], 128)
        high = one_hot_rows(head[at : at + 1, :], 8)
        found = joined(dot(parts_of(known_ref[base : base + 8, :]), low, NN))
        frac = frac + jnp.sum(found * high, axis=0, keepdims=True)
    stack_rows(y_ref, head, frac, side_ref, part_ref, sum_ref)


def last_kernel(damp_ref, known_ref, sums_ref, rec_ref, shot_ref):
    damp = damp_ref[8:9, :]
    step = gathered(sums_ref) / ((1.0 + damp) * known_ref[16:32, :] + damp)
    total = known_ref[0:16, :] + step
    rec_ref[...] = total[0:8, :]
    shot_ref[...] = total[8:10, :]


def turn_kernel(y_ref, side_ref, st_ref, energy_ref, xt_ref):
    eye = unit(LANES)
    groups = SLOTS // LANES
    for c in range(NS // LANES):
        block = dot(eye, y_ref[:, c * LANES : (c + 1) * LANES], NT)
        for q in range(groups):
            xt_ref[q, 8 + c * LANES : 8 + (c + 1) * LANES, :] = block[:, q * LANES : (q + 1) * LANES]
    block = dot(eye, y_ref[:, NS:], NT)
    for q in range(groups):
        part = block[:, q * LANES : (q + 1) * LANES]
        xt_ref[q, 0:8, :] = part[120:128, :]
        xt_ref[q, 8 + NS : 16 + NS, :] = part[0:8, :]
    shift_kernel(xt_ref, side_ref, st_ref, energy_ref)


def shift_kernel(xt_ref, side_ref, st_ref, energy_ref):
    groups = SLOTS // LANES
    chunk = 32
    energies = []
    for q in range(groups):
        tap = [
            jnp.broadcast_to(side_ref[16 + k : 17 + k, q * LANES : (q + 1) * LANES], (8, LANES)) for k in range(TAPS)
        ]

        def body(i, energy):
            base = pl.multiple_of(i * chunk, chunk)
            totals = [None] * (chunk // 8)
            for p in range(chunk + TAPS - 8):
                window = xt_ref[q, pl.ds(base + 1 + p, 8), :]
                for h in range(chunk // 8):
                    k = p - 8 * h
                    if 0 <= k < TAPS:
                        term = tap[k] * window
                        totals[h] = term if totals[h] is None else totals[h] + term
            for h in range(0, chunk // 8, 2):
                rounded = jnp.concatenate(totals[h : h + 2], axis=0).astype(BF16)
                st_ref[pl.ds(base + 8 * h, 16), q * LANES : (q + 1) * LANES] = rounded
                energy = energy + (totals[h] * totals[h] + totals[h + 1] * totals[h + 1])
            return energy

        energy = lax.fori_loop(0, NS // chunk, body, jnp.zeros((8, LANES), F32), unroll=8)
        energies.append(jnp.sum(energy, axis=0, keepdims=True))
    energy_ref[...] = jnp.broadcast_to(jnp.concatenate(energies, axis=1), (8, SLOTS))


def corr_kernel(first, p0_ref, p1_ref, p2_ref, p3_ref, st_ref, energy_ref, side_ref, *refs):
    grad_ref, lag_ref, wide_ref = refs[:3] if first else refs[1:4]
    total = (p0_ref[...].astype(F32) + p2_ref[...].astype(F32)) + (
        p1_ref[...].astype(F32) + p3_ref[...].astype(F32)
    )
    mass = (total[:, NS : NS + 1] + total[:, NS + 1 : NS + 2]) + total[:, NS + 2 : NS + 3]
    pilot = (total[:, :NS] * lax.rsqrt(mass + 1.0)).astype(BF16)
    if not first:
        pilot_ref, pilot_sem = refs[4:]
        pilot_ref[...] = pilot
        pilot_copy = pltpu.make_async_copy(pilot_ref, refs[0], pilot_sem)
        pilot_copy.start()
    wide = pilot.astype(F32)
    wide_ref[...] = pltpu.roll(jnp.concatenate([wide, jnp.zeros((BIN_DEV, LANES), F32)], axis=1), LAG_PAD, 1)
    pilot_scale = lax.rsqrt(jnp.sum(wide * wide, axis=1, keepdims=True) + EPS)
    head = side_ref[0:16, :]
    live = head[6:7, :]
    member = one_hot_rows(head[4:5, :], BIN_DEV) * live
    corr = jnp.zeros((LROWS, SLOTS), F32)
    for b0 in range(0, BIN_DEV, BINS_STEP):
        for bb in range(0, BINS_STEP, 2):
            eights = []
            for b in (b0 + bb, b0 + bb + 1):
                row = jnp.broadcast_to(wide_ref[b : b + 1, :], (8, WIDE))
                for g in range(0, LROWS, 8):
                    amount = (WIDE - (LAG_TOP - HALF) - LAG_PAD + g) % WIDE
                    eights.append(pltpu.roll(row, amount, 1, stride=1, stride_axis=0)[:, :NS])
                    if len(eights) % 2 == 0:
                        at = (b0 + bb) * LROWS + 8 * (len(eights) - 2)
                        lag_ref[at : at + 16, :] = jnp.concatenate(eights[-2:], axis=0).astype(BF16)
        every = dot(lag_ref[b0 * LROWS : (b0 + BINS_STEP) * LROWS, :], st_ref[...], NN)
        for bb in range(BINS_STEP):
            corr = corr + member[b0 + bb : b0 + bb + 1, :] * every[bb * LROWS : (bb + 1) * LROWS, :]
    scale = lax.rsqrt(energy_ref[0:1, :] + EPS) * jnp.sum(member * pilot_scale, axis=0, keepdims=True)
    lag = LAG_TOP - iota((LROWS, SLOTS), 0)
    exponent = jnp.where((lag >= 0) & (lag < LAGS), jnp.exp(BETA * (corr * scale)), 0.0)
    delay = jnp.sum(exponent * (lag - HALF).astype(F32), axis=0, keepdims=True) / jnp.sum(
        exponent, axis=0, keepdims=True
    )
    misfit = -delay * live
    grad_ref[...] = jnp.zeros_like(grad_ref)
    low = jnp.concatenate([one_hot_half(head[at + 1 : at + 2, :], 128) for at in (2, 0)], axis=0)
    high = jnp.concatenate([one_hot_rows(head[at : at + 1, :], 8) for at in (2, 0)], axis=0)
    left = parts_of(high * misfit)
    if first:
        left = jnp.concatenate([left, (high * live).astype(BF16)], axis=0)
    sums = dot(left, low, NT)
    delays = joined(sums[0:48, :])
    grad_ref[0:8, :] = delays[0:8, 0:128]
    grad_ref[8:10, :] = delays[8:10, 128:256]
    if first:
        grad_ref[16:24, :] = sums[48:56, 0:128]
        grad_ref[24:26, :] = sums[56:58, 128:256]
    else:
        pilot_copy.wait()


def spread_kernel(own_ref, other_ref, out_ref, rows_ref):
    total = own_ref[...] + other_ref[...]
    rows_ref[...] = jnp.zeros_like(rows_ref)
    rows_ref[0:10, :] = total[0:10, :]
    if total.shape[0] > 16:
        rows_ref[10:20, :] = total[16:26, :]
    out_ref[...] = jnp.broadcast_to(rows_ref[...].astype(BF16)[None], out_ref.shape)


def gathered(ref):
    return jnp.sum(ref[...].astype(F32), axis=0)


VMEM = pl.BlockSpec(memory_space=pltpu.VMEM)
HBM = pl.BlockSpec(memory_space=pl.ANY)
SMEM = pl.BlockSpec(memory_space=pltpu.SMEM)
PARAMS = pltpu.CompilerParams(vmem_limit_bytes=24 * 1024 * 1024)


def shape(dims, dtype):
    return jax.ShapeDtypeStruct(dims, dtype)


def call(kernel, out, memory, scratch, name, flops, moved, *args):
    return pl.pallas_call(
        kernel,
        out_shape=out,
        in_specs=[SMEM if space else VMEM for space in memory],
        out_specs=jax.tree.map(lambda _: VMEM, out),
        scratch_shapes=scratch,
        compiler_params=PARAMS,
        cost_estimate=pl.CostEstimate(flops=flops, bytes_accessed=moved, transcendentals=0),
        name=name,
    )(*args)


def pack(traces, *meta):
    scratch = [pltpu.VMEM((1, TR_DEV), jnp.int32)] * 6 + [
        pltpu.VMEM((TR_DEV, NS), BF16),
        pltpu.VMEM((TR_DEV, WIDE), BF16),
        pltpu.VMEM((DEVICES, TRACE_LIMIT, WIDE), BF16),
        pltpu.SemaphoreType.DMA((6,)),
        pltpu.SemaphoreType.DMA((TR_DEV // PACK_ROWS,)),
        pltpu.SemaphoreType.DMA((PACK_OUT,)),
    ]
    return pl.pallas_call(
        pack_kernel,
        out_shape=shape((DEVICES, TRACE_LIMIT, WIDE), BF16),
        in_specs=[HBM] * 7,
        out_specs=HBM,
        scratch_shapes=scratch,
        compiler_params=pltpu.CompilerParams(vmem_limit_bytes=PACK_VMEM),
        name="pack",
    )(*[row.reshape(1, TR_DEV) for row in meta], traces)


PART = shape((BIN_DEV, WIDE), BF16)
SIDE = shape((32, SLOTS), F32)
ROWS = pltpu.VMEM((TAPS * BIN_DEV, WIDE), F32)


def stack_first(damps, slots):
    out = (PART, SIDE, shape((SLOTS, WIDE), BF16), shape((16, LANES), F32))
    return call(first_kernel, out, (0, 0), [ROWS], "stack_first", 3 * 10**9, 10**7, damps, slots)


KNOWN = shape((32, LANES), F32)


def stack_next(damps, rows, side, sums):
    out = (PART, SIDE, KNOWN)
    return call(next_kernel, out, (0,) * 4, [ROWS], "stack_next", 3 * 10**9, 10**7, damps, rows, side, sums)


def finish(damps, known, sums):
    out = (shape((8, LANES), F32), shape((2, LANES), F32))
    return call(last_kernel, out, (0,) * 3, [], "finish", 10**4, 10**5, damps, known, sums)


SHIFTED = (shape((NS, SLOTS), BF16), shape((8, SLOTS), F32))
TURNED = shape((SLOTS // LANES, NS + 16, LANES), F32)


def shift_first(rows, side):
    return call(turn_kernel, (*SHIFTED, TURNED), (0, 0), [], "shift_first", 6 * 10**9, 2 * 10**7, rows, side)


def shift_next(turned, side):
    return call(shift_kernel, SHIFTED, (0, 0), [], "shift_next", 6 * 10**9, 2 * 10**7, turned, side)


def correlate(first, parts, shifted, energy, side):
    sums = shape((32 if first else 16, LANES), F32)
    scratch = [pltpu.VMEM((BIN_DEV * LROWS, NS), BF16), pltpu.VMEM((BIN_DEV, WIDE), F32)]
    if not first:
        scratch += [pltpu.VMEM((BIN_DEV, NS), BF16), pltpu.SemaphoreType.DMA]
    return pl.pallas_call(
        functools.partial(corr_kernel, first),
        out_shape=(sums,) if first else (shape((BIN_DEV, NS), BF16), sums),
        in_specs=[VMEM] * 7,
        out_specs=(VMEM,) if first else (HBM, VMEM),
        scratch_shapes=scratch,
        compiler_params=PARAMS,
        cost_estimate=pl.CostEstimate(flops=4 * 10**9, bytes_accessed=10**7, transcendentals=0),
        name="correlate",
    )(*parts, shifted, energy, side)


def off_perm(d):
    return [(i, (i + d) % 4) for i in range(4)]


def sum_copies(value):
    other = lax.ppermute(value, "core", [(0, 1), (1, 0)])
    rows = 16 if value.shape[0] == 16 else 24
    out = shape((DEVICES // 2, rows, LANES), BF16)
    scratch = [pltpu.VMEM((rows, LANES), F32)]
    copies = call(spread_kernel, out, (0, 0), scratch, "spread", 10**5, 10**6, value, other)
    return lax.all_to_all(copies, ("y", "x", "off"), split_axis=0, concat_axis=0, tiled=True)


def exchange(part):
    return part, *[lax.ppermute(part, "off", off_perm(d)) for d in (1, 2, 3)]


def on_device(
    traces,
    shot_id,
    receiver_id,
    cmp_bin,
    offset_class,
    shift_int,
    frac_index,
    damping_table,
    damping_index,
):
    outgoing = pack(traces, shot_id, receiver_id, cmp_bin, offset_class, shift_int, frac_index)
    slots = lax.all_to_all(outgoing, AXES, split_axis=0, concat_axis=0, tiled=True)
    entries = jnp.arange(damping_table.shape[0], dtype=jnp.int32)
    chosen = jnp.sum(jnp.where(entries == damping_index[:, None], damping_table, 0.0), axis=1)
    damps = jnp.broadcast_to(chosen[:, None, None], (2, 8, LANES)).reshape(16, LANES)
    part, side, rows, damps = stack_first(damps, slots)
    parts = exchange(part)
    shifted, energy, turned = shift_first(rows, side)
    (sums,) = correlate(True, parts, shifted, energy, side)
    sums = sum_copies(sums)
    part, side, known = stack_next(damps, rows, side, sums)
    parts = exchange(part)
    shifted, energy = shift_next(turned, side)
    pilot, sums = correlate(False, parts, shifted, energy, side)
    sums = sum_copies(sums)
    rec, shot = finish(damps, known, sums)
    return (shot.reshape(-1), rec.reshape(-1), pilot)


def solution(mesh):
    mesh = Mesh(mesh.devices.reshape(4, 4, 2, 4), AXES)
    placed = (P(AXES, None),) + (P(AXES),) * 6 + (P(), P())
    return jax.shard_map(
        on_device, mesh=mesh, in_specs=placed, out_specs=(P(), P(), P(AXES[:3], None)), check_vma=False
    )
```

```python
import functools

import jax
import jax.numpy as jnp
from jax import lax
from jax.experimental import pallas as pl
from jax.experimental.pallas import tpu as pltpu
from jax.sharding import Mesh
from jax.sharding import PartitionSpec as P

NS = 2048
LAGS = 101
HALF = LAGS // 2
TAPS = 16
NPHASE = 32
SHIFT_MAX = 8
CLASSES = 4
TRACE_LIMIT = 4
BIN_DEV = 16
TR_DEV = 256
DEVICES = 128
SLOTS = DEVICES * TRACE_LIMIT
LANES = 128
WIDE = NS + LANES
LROWS = 104
LAG_TOP = 102
LAG_PAD = 4
BINS_STEP = 4
PACK_ROWS = 256
PACK_OUT = 4
PACK_VMEM = 63 * 1024 * 1024
BETA = 24.0
EPS = 1e-06
F32 = jnp.float32
BF16 = jnp.bfloat16
HEAD = 16
AXES = ("y", "x", "core", "off")

NN = (((1,), (0,)), ((), ()))
NT = (((1,), (1,)), ((), ()))
TN = (((0,), (0,)), ((), ()))


def dot(a, b, dims, precision=None):
    return lax.dot_general(a, b, dims, precision=precision, preferred_element_type=F32)


def iota(shape, axis):
    return lax.broadcasted_iota(jnp.int32, shape, axis)


def pack_kernel(*refs):
    meta_in, x_in, out_ref = refs[:6], refs[6], refs[7]
    meta_refs, (x_ref, y_ref, o_ref, meta_sem, x_sem, o_sem) = refs[8:14], refs[14:]
    parts = TR_DEV // PACK_ROWS
    x_copies = [
        pltpu.make_async_copy(
            x_in.at[pl.ds(i * PACK_ROWS, PACK_ROWS), :], x_ref.at[pl.ds(i * PACK_ROWS, PACK_ROWS), :], x_sem.at[i]
        )
        for i in range(parts)
    ]
    meta_copies = [pltpu.make_async_copy(meta_in[i], meta_refs[i], meta_sem.at[i]) for i in range(6)]
    for copy in meta_copies + x_copies:
        copy.start()
    for copy in meta_copies:
        copy.wait()
    shot, rec, bin_, cls, whole, frac = [ref[...] for ref in meta_refs]
    dest = (bin_ // BIN_DEV) * CLASSES + cls
    rows = [
        shot // 128,
        shot % 128,
        rec // 128,
        rec % 128,
        bin_ % BIN_DEV,
        frac,
        jnp.ones_like(shot),
        whole + SHIFT_MAX,
        dest,
    ]
    sub = iota((16, TR_DEV), 0)
    info = jnp.zeros((16, TR_DEV), F32)
    for i, row in enumerate(rows):
        info = jnp.where(sub == i, row.astype(F32), info)
    place = (iota((16, LANES), 1) == iota((16, LANES), 0) + HEAD).astype(F32).astype(BF16)
    cols = dot(info.astype(BF16), place, TN)
    amount = cols[:, HEAD + 7 : HEAD + 8].astype(jnp.int32)
    dest_col = cols[:, HEAD + 8 : HEAD + 9]
    same = (dest_col == dest.astype(F32)) & (iota((TR_DEV, TR_DEV), 0) < iota((TR_DEV, TR_DEV), 1))
    rank = jnp.sum(jnp.where(same, 1.0, 0.0), axis=0, keepdims=True).astype(jnp.int32)
    slot = dest * TRACE_LIMIT + rank
    onehot = (iota((SLOTS, TR_DEV), 0) == slot).astype(F32).astype(BF16)
    amount = amount - SHIFT_MAX
    tail = cols.astype(BF16)
    step = 32
    lane = iota((step, LANES), 1)
    blocks = WIDE // LANES
    for r in range(0, TR_DEV, step):
        if r % PACK_ROWS == 0:
            x_copies[r // PACK_ROWS].wait()
        source = lane + amount[r : r + step, :]
        index = source & (LANES - 1)
        turned = [
            jnp.take_along_axis(
                x_ref[r : r + step, c * LANES : (c + 1) * LANES].astype(F32), index, axis=1, mode="promise_in_bounds"
            )
            for c in range(blocks - 1)
        ] + [jnp.zeros((step, LANES), F32)]
        for c in range(blocks):
            before, after = turned[c - 1], turned[(c + 1) % blocks]
            y = jnp.where(source < 0, before, jnp.where(source >= LANES, after, turned[c])).astype(BF16)
            if c == blocks - 1:
                y = y + tail[r : r + step, :]
            y_ref[r : r + step, c * LANES : (c + 1) * LANES] = y
    out_copies = []
    group = DEVICES // PACK_OUT
    for i in range(PACK_OUT):
        rows = onehot[i * group * TRACE_LIMIT : (i + 1) * group * TRACE_LIMIT, :]
        placed = dot(rows, y_ref[...], NN).reshape(group, TRACE_LIMIT, WIDE).astype(BF16)
        o_ref[i * group : (i + 1) * group] = placed
        copy = pltpu.make_async_copy(
            o_ref.at[pl.ds(i * group, group)], out_ref.at[pl.ds(i * group, group)], o_sem.at[i]
        )
        copy.start()
        out_copies.append(copy)
    for copy in out_copies:
        copy.wait()


def one_hot_rows(row, count):
    return (iota((count, SLOTS), 0) == row.astype(jnp.int32)).astype(F32)


def one_hot_half(row, count):
    return one_hot_rows(row, count).astype(BF16)


def parts_of(value):
    top = value.astype(BF16)
    rest = value - top.astype(F32)
    middle = rest.astype(BF16)
    return jnp.concatenate([top, middle, (rest - middle.astype(F32)).astype(BF16)], axis=0)


def joined(sums):
    rows = sums.shape[0] // 3
    return (sums[0:rows, :] + sums[rows : 2 * rows, :]) + sums[2 * rows :, :]


def unit(size):
    return (iota((size, size), 0) == iota((size, size), 1)).astype(F32).astype(BF16)


def stack_rows(y_ref, head, frac, side_ref, part_ref, sum_ref):
    live = head[6:7, :]
    u = (iota((TAPS, SLOTS), 0) - (TAPS // 2 - 1)).astype(F32) - frac
    angle = jnp.pi * u
    safe = jnp.where(u == 0.0, 1.0, angle)
    sinc = jnp.where(u == 0.0, 1.0, jnp.sin(safe) / safe)
    taps = sinc * (0.5 + 0.5 * jnp.cos(angle * (1.0 / (TAPS // 2))))
    side_ref[0:16, :] = head
    side_ref[16:32, :] = taps
    owner = head[8:9, :]
    offset = owner - CLASSES * jnp.floor(owner * (1.0 / CLASSES))
    member = one_hot_rows(head[4:5, :], BIN_DEV) * (live / (1.0 + offset))
    rows = [member * taps[k : k + 1, :] for k in range(TAPS)]
    rows = jnp.concatenate([row.astype(BF16) for row in rows], axis=0)
    sum_ref[...] = dot(rows, y_ref[...], NN)
    total = jnp.zeros((BIN_DEV, WIDE), F32)
    for k in range(TAPS):
        total = total + pltpu.roll(sum_ref[k * BIN_DEV : (k + 1) * BIN_DEV, :], (TAPS // 2 - 1 - k) % WIDE, 1)
    part_ref[:, :NS] = total[:, :NS].astype(BF16)
    mass = jnp.sum(member, axis=1, keepdims=True)
    m0 = mass.astype(BF16).astype(F32)
    m1 = (mass - m0).astype(BF16).astype(F32)
    m2 = mass - m0 - m1
    lane = iota((BIN_DEV, LANES), 1)
    tail = jnp.where(lane == 0, m0, jnp.where(lane == 1, m1, jnp.where(lane == 2, m2, 0.0)))
    part_ref[:, NS:] = tail.astype(BF16)


def first_kernel(damp_ref, slots_ref, part_ref, side_ref, y_ref, kept_ref, sum_ref):
    kept_ref[...] = damp_ref[...]
    y_ref[...] = slots_ref[...].reshape(SLOTS, WIDE)
    head = dot(unit(LANES), y_ref[:, NS:], NT)[HEAD : HEAD + 16, :]
    stack_rows(y_ref, head, head[5:6, :] * (1.0 / NPHASE), side_ref, part_ref, sum_ref)


def next_kernel(damp_ref, y_ref, head_ref, sums_ref, part_ref, side_ref, known_ref, sum_ref):
    damp = damp_ref[0:1, :]
    sums = gathered(sums_ref)
    count = sums[10:20, :]
    known_ref[...] = jnp.zeros_like(known_ref)
    known_ref[0:10, :] = sums[0:10, :] / ((1.0 + damp) * count + damp)
    known_ref[16:26, :] = count
    head = head_ref[0:16, :]
    frac = head[5:6, :] * (1.0 / NPHASE)
    for base, at in ((8, 0), (0, 2)):
        low = one_hot_half(head[at + 1 : at + 2, :], 128)
        high = one_hot_rows(head[at : at + 1, :], 8)
        found = joined(dot(parts_of(known_ref[base : base + 8, :]), low, NN))
        frac = frac + jnp.sum(found * high, axis=0, keepdims=True)
    stack_rows(y_ref, head, frac, side_ref, part_ref, sum_ref)


def last_kernel(damp_ref, known_ref, sums_ref, rec_ref, shot_ref):
    damp = damp_ref[8:9, :]
    step = gathered(sums_ref) / ((1.0 + damp) * known_ref[16:32, :] + damp)
    total = known_ref[0:16, :] + step
    rec_ref[...] = total[0:8, :]
    shot_ref[...] = total[8:10, :]


def turn_kernel(y_ref, side_ref, st_ref, energy_ref, xt_ref):
    eye = unit(LANES)
    groups = SLOTS // LANES
    for c in range(NS // LANES):
        block = dot(eye, y_ref[:, c * LANES : (c + 1) * LANES], NT)
        for q in range(groups):
            xt_ref[q, 8 + c * LANES : 8 + (c + 1) * LANES, :] = block[:, q * LANES : (q + 1) * LANES]
    block = dot(eye, y_ref[:, NS:], NT)
    for q in range(groups):
        part = block[:, q * LANES : (q + 1) * LANES]
        xt_ref[q, 0:8, :] = part[120:128, :]
        xt_ref[q, 8 + NS : 16 + NS, :] = part[0:8, :]
    shift_kernel(xt_ref, side_ref, st_ref, energy_ref)


def shift_kernel(xt_ref, side_ref, st_ref, energy_ref):
    groups = SLOTS // LANES
    chunk = 32
    energies = []
    for q in range(groups):
        tap = [
            jnp.broadcast_to(side_ref[16 + k : 17 + k, q * LANES : (q + 1) * LANES], (8, LANES)) for k in range(TAPS)
        ]

        def body(i, energy):
            base = pl.multiple_of(i * chunk, chunk)
            totals = [None] * (chunk // 8)
            for p in range(chunk + TAPS - 8):
                window = xt_ref[q, pl.ds(base + 1 + p, 8), :]
                for h in range(chunk // 8):
                    k = p - 8 * h
                    if 0 <= k < TAPS:
                        term = tap[k] * window
                        totals[h] = term if totals[h] is None else totals[h] + term
            for h in range(0, chunk // 8, 2):
                rounded = jnp.concatenate(totals[h : h + 2], axis=0).astype(BF16)
                st_ref[pl.ds(base + 8 * h, 16), q * LANES : (q + 1) * LANES] = rounded
                energy = energy + (totals[h] * totals[h] + totals[h + 1] * totals[h + 1])
            return energy

        energy = lax.fori_loop(0, NS // chunk, body, jnp.zeros((8, LANES), F32), unroll=16)
        energies.append(jnp.sum(energy, axis=0, keepdims=True))
    energy_ref[...] = jnp.broadcast_to(jnp.concatenate(energies, axis=1), (8, SLOTS))


def corr_kernel(first, p0_ref, p1_ref, p2_ref, p3_ref, st_ref, energy_ref, side_ref, *refs):
    grad_ref, lag_ref, wide_ref = refs[:3] if first else refs[1:4]
    total = (p0_ref[...].astype(F32) + p2_ref[...].astype(F32)) + (
        p1_ref[...].astype(F32) + p3_ref[...].astype(F32)
    )
    mass = (total[:, NS : NS + 1] + total[:, NS + 1 : NS + 2]) + total[:, NS + 2 : NS + 3]
    pilot = (total[:, :NS] * lax.rsqrt(mass + 1.0)).astype(BF16)
    if not first:
        pilot_ref, pilot_sem = refs[4:]
        pilot_ref[...] = pilot
        pilot_copy = pltpu.make_async_copy(pilot_ref, refs[0], pilot_sem)
        pilot_copy.start()
    wide = pilot.astype(F32)
    wide_ref[...] = pltpu.roll(jnp.concatenate([wide, jnp.zeros((BIN_DEV, LANES), F32)], axis=1), LAG_PAD, 1)
    pilot_scale = lax.rsqrt(jnp.sum(wide * wide, axis=1, keepdims=True) + EPS)
    head = side_ref[0:16, :]
    live = head[6:7, :]
    member = one_hot_rows(head[4:5, :], BIN_DEV) * live
    corr = jnp.zeros((LROWS, SLOTS), F32)
    for b0 in range(0, BIN_DEV, BINS_STEP):
        for bb in range(0, BINS_STEP, 2):
            eights = []
            for b in (b0 + bb, b0 + bb + 1):
                row = jnp.broadcast_to(wide_ref[b : b + 1, :], (8, WIDE))
                for g in range(0, LROWS, 8):
                    amount = (WIDE - (LAG_TOP - HALF) - LAG_PAD + g) % WIDE
                    eights.append(pltpu.roll(row, amount, 1, stride=1, stride_axis=0)[:, :NS])
                    if len(eights) % 2 == 0:
                        at = (b0 + bb) * LROWS + 8 * (len(eights) - 2)
                        lag_ref[at : at + 16, :] = jnp.concatenate(eights[-2:], axis=0).astype(BF16)
        every = dot(lag_ref[b0 * LROWS : (b0 + BINS_STEP) * LROWS, :], st_ref[...], NN)
        for bb in range(BINS_STEP):
            corr = corr + member[b0 + bb : b0 + bb + 1, :] * every[bb * LROWS : (bb + 1) * LROWS, :]
    scale = lax.rsqrt(energy_ref[0:1, :] + EPS) * jnp.sum(member * pilot_scale, axis=0, keepdims=True)
    lag = LAG_TOP - iota((LROWS, SLOTS), 0)
    exponent = jnp.where((lag >= 0) & (lag < LAGS), jnp.exp(BETA * (corr * scale)), 0.0)
    delay = jnp.sum(exponent * (lag - HALF).astype(F32), axis=0, keepdims=True) / jnp.sum(
        exponent, axis=0, keepdims=True
    )
    misfit = -delay * live
    grad_ref[...] = jnp.zeros_like(grad_ref)
    low = jnp.concatenate([one_hot_half(head[at + 1 : at + 2, :], 128) for at in (2, 0)], axis=0)
    high = jnp.concatenate([one_hot_rows(head[at : at + 1, :], 8) for at in (2, 0)], axis=0)
    left = parts_of(high * misfit)
    if first:
        left = jnp.concatenate([left, (high * live).astype(BF16)], axis=0)
    sums = dot(left, low, NT)
    delays = joined(sums[0:48, :])
    grad_ref[0:8, :] = delays[0:8, 0:128]
    grad_ref[8:10, :] = delays[8:10, 128:256]
    if first:
        grad_ref[16:24, :] = sums[48:56, 0:128]
        grad_ref[24:26, :] = sums[56:58, 128:256]
    else:
        pilot_copy.wait()


def spread_kernel(own_ref, other_ref, out_ref, rows_ref):
    total = own_ref[...] + other_ref[...]
    rows_ref[...] = jnp.zeros_like(rows_ref)
    rows_ref[0:10, :] = total[0:10, :]
    if total.shape[0] > 16:
        rows_ref[10:20, :] = total[16:26, :]
    out_ref[...] = jnp.broadcast_to(rows_ref[...].astype(BF16)[None], out_ref.shape)


def gathered(ref):
    return jnp.sum(ref[...].astype(F32), axis=0)


VMEM = pl.BlockSpec(memory_space=pltpu.VMEM)
HBM = pl.BlockSpec(memory_space=pl.ANY)
SMEM = pl.BlockSpec(memory_space=pltpu.SMEM)
PARAMS = pltpu.CompilerParams(vmem_limit_bytes=24 * 1024 * 1024)


def shape(dims, dtype):
    return jax.ShapeDtypeStruct(dims, dtype)


def call(kernel, out, memory, scratch, name, flops, moved, *args):
    return pl.pallas_call(
        kernel,
        out_shape=out,
        in_specs=[SMEM if space else VMEM for space in memory],
        out_specs=jax.tree.map(lambda _: VMEM, out),
        scratch_shapes=scratch,
        compiler_params=PARAMS,
        cost_estimate=pl.CostEstimate(flops=flops, bytes_accessed=moved, transcendentals=0),
        name=name,
    )(*args)


def pack(traces, *meta):
    scratch = [pltpu.VMEM((1, TR_DEV), jnp.int32)] * 6 + [
        pltpu.VMEM((TR_DEV, NS), BF16),
        pltpu.VMEM((TR_DEV, WIDE), BF16),
        pltpu.VMEM((DEVICES, TRACE_LIMIT, WIDE), BF16),
        pltpu.SemaphoreType.DMA((6,)),
        pltpu.SemaphoreType.DMA((TR_DEV // PACK_ROWS,)),
        pltpu.SemaphoreType.DMA((PACK_OUT,)),
    ]
    return pl.pallas_call(
        pack_kernel,
        out_shape=shape((DEVICES, TRACE_LIMIT, WIDE), BF16),
        in_specs=[HBM] * 7,
        out_specs=HBM,
        scratch_shapes=scratch,
        compiler_params=pltpu.CompilerParams(vmem_limit_bytes=PACK_VMEM),
        name="pack",
    )(*[row.reshape(1, TR_DEV) for row in meta], traces)


PART = shape((BIN_DEV, WIDE), BF16)
SIDE = shape((32, SLOTS), F32)
ROWS = pltpu.VMEM((TAPS * BIN_DEV, WIDE), F32)


def stack_first(damps, slots):
    out = (PART, SIDE, shape((SLOTS, WIDE), BF16), shape((16, LANES), F32))
    return call(first_kernel, out, (0, 0), [ROWS], "stack_first", 3 * 10**9, 10**7, damps, slots)


KNOWN = shape((32, LANES), F32)


def stack_next(damps, rows, side, sums):
    out = (PART, SIDE, KNOWN)
    return call(next_kernel, out, (0,) * 4, [ROWS], "stack_next", 3 * 10**9, 10**7, damps, rows, side, sums)


def finish(damps, known, sums):
    out = (shape((8, LANES), F32), shape((2, LANES), F32))
    return call(last_kernel, out, (0,) * 3, [], "finish", 10**4, 10**5, damps, known, sums)


SHIFTED = (shape((NS, SLOTS), BF16), shape((8, SLOTS), F32))
TURNED = shape((SLOTS // LANES, NS + 16, LANES), F32)


def shift_first(rows, side):
    return call(turn_kernel, (*SHIFTED, TURNED), (0, 0), [], "shift_first", 6 * 10**9, 2 * 10**7, rows, side)


def shift_next(turned, side):
    return call(shift_kernel, SHIFTED, (0, 0), [], "shift_next", 6 * 10**9, 2 * 10**7, turned, side)


def correlate(first, parts, shifted, energy, side):
    sums = shape((32 if first else 16, LANES), F32)
    scratch = [pltpu.VMEM((BIN_DEV * LROWS, NS), BF16), pltpu.VMEM((BIN_DEV, WIDE), F32)]
    if not first:
        scratch += [pltpu.VMEM((BIN_DEV, NS), BF16), pltpu.SemaphoreType.DMA]
    return pl.pallas_call(
        functools.partial(corr_kernel, first),
        out_shape=(sums,) if first else (shape((BIN_DEV, NS), BF16), sums),
        in_specs=[VMEM] * 7,
        out_specs=(VMEM,) if first else (HBM, VMEM),
        scratch_shapes=scratch,
        compiler_params=PARAMS,
        cost_estimate=pl.CostEstimate(flops=4 * 10**9, bytes_accessed=10**7, transcendentals=0),
        name="correlate",
    )(*parts, shifted, energy, side)


def off_perm(d):
    return [(i, (i + d) % 4) for i in range(4)]


def sum_copies(value):
    other = lax.ppermute(value, "core", [(0, 1), (1, 0)])
    rows = 16 if value.shape[0] == 16 else 24
    out = shape((DEVICES // 2, rows, LANES), BF16)
    scratch = [pltpu.VMEM((rows, LANES), F32)]
    copies = call(spread_kernel, out, (0, 0), scratch, "spread", 10**5, 10**6, value, other)
    return lax.all_to_all(copies, ("y", "x", "off"), split_axis=0, concat_axis=0, tiled=True)


def exchange(part):
    return part, *[lax.ppermute(part, "off", off_perm(d)) for d in (1, 2, 3)]


def on_device(
    traces,
    shot_id,
    receiver_id,
    cmp_bin,
    offset_class,
    shift_int,
    frac_index,
    damping_table,
    damping_index,
):
    outgoing = pack(traces, shot_id, receiver_id, cmp_bin, offset_class, shift_int, frac_index)
    slots = lax.all_to_all(outgoing, AXES, split_axis=0, concat_axis=0, tiled=True)
    entries = jnp.arange(damping_table.shape[0], dtype=jnp.int32)
    chosen = jnp.sum(jnp.where(entries == damping_index[:, None], damping_table, 0.0), axis=1)
    damps = jnp.broadcast_to(chosen[:, None, None], (2, 8, LANES)).reshape(16, LANES)
    part, side, rows, damps = stack_first(damps, slots)
    parts = exchange(part)
    shifted, energy, turned = shift_first(rows, side)
    (sums,) = correlate(True, parts, shifted, energy, side)
    sums = sum_copies(sums)
    part, side, known = stack_next(damps, rows, side, sums)
    parts = exchange(part)
    shifted, energy = shift_next(turned, side)
    pilot, sums = correlate(False, parts, shifted, energy, side)
    sums = sum_copies(sums)
    rec, shot = finish(damps, known, sums)
    return (shot.reshape(-1), rec.reshape(-1), pilot)


def solution(mesh):
    mesh = Mesh(mesh.devices.reshape(4, 4, 2, 4), AXES)
    placed = (P(AXES, None),) + (P(AXES),) * 6 + (P(), P())
    return jax.shard_map(
        on_device, mesh=mesh, in_specs=placed, out_specs=(P(), P(), P(AXES[:3], None)), check_vma=False
    )
```
